32 devices in a mesh: stream: 8 (over y, x, core), span: 4 (over z).
Axes of the slice: x: 2, y: 2, z: 4, core: 2. Of those that a mesh axis runs over, the one named last changes fastest.
Arguments:
- grains: float32 [13, 786432], P(None, ('stream', 'span'))
- send_slots: int32 [32, 2, 2048], P(('stream', 'span')), may hold values from 0 to 24575, as said below
- send_counts: int32 [32, 2], P(('stream', 'span')), may hold values from 0 to 2048, as said below
- cell_index: int32 [917504], P(('stream', 'span')), may hold values from 0 to 65535
- fluid: float32 [3, 256, 32, 256], P(None, 'stream', 'span'), may hold values from -6 to 6
- block_slots: int32 [32, 32, 8], P(('stream', 'span')), may hold values from 0 to 255
- block_counts: int32 [32, 32], P(('stream', 'span')), may hold values from 0 to 8, as said below
Outputs:
- grains_after: float32 [13, 917504], P(None, ('stream', 'span'))
- solid_fields: float32 [4, 256, 32, 256], P(None, 'stream', 'span')
- received: float32 [32, 32, 8, 4, 256], P(('stream', 'span'))
The draws below stay inside these ranges and needn't reach their ends.
Inputs may be any that keep to these rules, and one draw needn't show every extreme that they name: `send_slots`: the entries of one device's two lists are distinct slots of that device. `send_counts`: live entries are the first ones of a list; a list of 2048 live entries exists in both directions. `block_counts`: every device sends 8 columns to some device and receives 8 from some device.
All inputs are finite; a program needn't handle non-finite values.
Results may differ from the reference program's by a relative error of at most 0.00086.
Values sent between devices are 32-bit elements; how exact they have to be, the bound alone decides.
No kernel may reach another device: no remote copies, remote signals or barrier semaphores. Data moves between devices by JAX's collectives and lax.ppermute only.
A program may use at most 64 MiB of HBM per device.

```python
import math
import jax
import jax.numpy as jnp
from jax import lax

CX = 32
CY = 8
CZ = 256
G = 24576
M = 2048
Q = 8
REACH = 3
NX = 256
NY = 32
N_STREAM = 8
N_SPAN = 4
DEVICES = 32


def draw_grains(key, part):
    keys = jax.random.split(key, 4)
    total = DEVICES * G
    place = jax.random.uniform(keys[0], (3, total), jnp.float32)
    moving = jax.random.normal(keys[1], (6, total), jnp.float32)
    size = jax.random.uniform(keys[2], (1, total), jnp.float32, 0.6, 1.2)
    extra = jax.random.uniform(keys[3], (3, total), jnp.float32, 0.0, 1.0)
    return jnp.concatenate([place, moving, size, extra], axis=0)


def draw_send_slots(key, part):
    keys = jax.random.split(key, DEVICES)

    def one_device(inner):
        return jax.random.permutation(inner, G)[:2 * M].reshape(2, M).astype(jnp.int32)
    return jax.vmap(one_device)(keys)


def draw_send_counts(key, part):
    first, second = jax.random.split(key)
    left = jax.random.randint(first, (DEVICES, 2), M // 4, M + 1)
    right = jax.random.randint(second, (DEVICES, 2), M // 4, M + 1)
    counts = left * right // M
    counts = counts.at[0, 0].set(M).at[DEVICES - 1, 1].set(M)
    return counts.astype(jnp.int32)


def draw_block_counts(key, part):
    first, second = jax.random.split(key)
    left = jax.random.randint(first, (DEVICES, DEVICES), 0, Q + 1)
    right = jax.random.randint(second, (DEVICES, DEVICES), 0, Q + 1)
    counts = jnp.maximum(left, right)
    rows = jnp.arange(DEVICES, dtype=jnp.int32)
    counts = counts.at[rows, (rows + 1) % DEVICES].set(Q)
    return counts.astype(jnp.int32)


def touch_ends(entries, stream_key, least, largest):
    dims = entries.shape
    spot = [jax.random.randint(jax.random.fold_in(stream_key, axis), (), 0, dims[axis]) for axis in range(len(dims))]
    entries = entries.at[tuple(spot)].set(least)
    longest = dims.index(max(dims))
    spot[longest] = (spot[longest] + 1) % dims[longest]
    return entries.at[tuple(spot)].set(largest)


def block_levels(stream_key, extent, shards, low, largest):
    loudness = 1.0
    for dim, parts in shards:
        heights = jax.random.uniform(jax.random.fold_in(jax.random.fold_in(stream_key, 6), dim), (parts,), jnp.float32, low / len(shards), largest / len(shards))
        loudness = loudness * jnp.repeat(jnp.exp(heights), extent[dim] // parts).reshape((-1,) + (1,) * (len(extent) - 1 - dim))
    return loudness


def bell_draw(key, extent, width, most, cuts=(), kind=jnp.bfloat16):
    factor_of = block_levels(key, extent, cuts, -0.22, 0.18) if cuts else 1.0
    drawn = jax.random.normal(key, extent, jnp.float32) * width * factor_of
    return jnp.minimum(jnp.maximum(drawn, -most), most).astype(kind)


def setup_inputs(seed: int = 0) -> dict:
    key_of = jax.random.split(jax.random.key(seed), 8)
    grains = draw_grains(jax.random.fold_in(key_of[7], 71), 0)
    send_slots = draw_send_slots(jax.random.fold_in(key_of[7], 71), 0)
    send_counts = draw_send_counts(jax.random.fold_in(key_of[7], 71), 0)
    cell_index = touch_ends(jax.random.randint(key_of[3], (DEVICES * (G + 2 * M),), 0, CX * CY * CZ), jax.random.fold_in(key_of[3], 1), 0, (CX * CY * CZ) - 1).astype(jnp.int32)
    fluid = bell_draw(key_of[4], (3, NX, NY, CZ), 1.0, 6.0, ((1, 8), (2, 4)), jnp.float32)
    block_slots = touch_ends(jax.random.randint(key_of[5], (DEVICES, DEVICES, Q), 0, CX * CY), jax.random.fold_in(key_of[5], 1), 0, (CX * CY) - 1).astype(jnp.int32)
    block_counts = draw_block_counts(jax.random.fold_in(key_of[7], 71), 0)
    return {"grains": grains, "send_slots": send_slots, "send_counts": send_counts, "cell_index": cell_index, "fluid": fluid, "block_slots": block_slots, "block_counts": block_counts}


spread_cells = 1.5
drag_rate = 0.25


def kernel_taps():
    raw = [math.exp(-(k * k) / (2.0 * spread_cells * spread_cells)) for k in range(-REACH, REACH + 1)]
    total = sum(raw)
    return [value / total for value in raw]


def smooth_padded(field, axis, length):
    weights = kernel_taps()
    widths = [(0, 0)] * field.ndim
    widths[axis] = (REACH, REACH)
    padded = jnp.pad(field, widths)
    result = jnp.zeros_like(field)
    for offset in range(2 * REACH + 1):
        result = result + weights[offset] * lax.slice_in_dim(padded, offset, offset + length, axis=axis)
    return result


def reference(grains, send_slots, send_counts, cell_index, fluid, block_slots, block_counts):
    peers = N_STREAM * N_SPAN
    total_grains = G + 2 * M
    records = grains.reshape(13, peers, G)
    slots = send_slots.reshape(peers, 2 * M)
    live = (jnp.arange(M, dtype=jnp.int32)[None, None, :] < send_counts[:, :, None]).astype(jnp.float32)
    live = live.reshape(peers, 2 * M)
    picked = jnp.take_along_axis(records, slots[None], axis=2) * live[None]
    picked = picked.reshape(13, N_STREAM, N_SPAN, 2, M)
    from_below = jnp.roll(picked[:, :, :, 0], 1, axis=1).reshape(13, peers, M)
    from_above = jnp.roll(picked[:, :, :, 1], -1, axis=1).reshape(13, peers, M)
    rows = jnp.arange(peers, dtype=jnp.int32)[:, None]
    removed = jnp.zeros((peers, G), jnp.float32).at[rows, slots].max(live)
    kept = records * (1.0 - removed)[None]
    after = jnp.concatenate([kept, from_below, from_above], axis=2)
    grains_after = after.reshape(13, peers * total_grains)

    volume = 4.18879 * after[9] ** 3
    quant = jnp.stack([volume, volume * after[3], volume * after[4], volume * after[5]]).astype(jnp.bfloat16)
    quant = lax.optimization_barrier(quant).astype(jnp.float32)
    cells = cell_index.reshape(peers, total_grains)

    def deposit_one(pieces):
        values, targets = pieces
        return jax.ops.segment_sum(values.T, targets, num_segments=CX * CY * CZ).T

    field = lax.map(deposit_one, (jnp.moveaxis(quant, 1, 0), cells))
    field = field.reshape(N_STREAM, N_SPAN, 4, CX, CY, CZ).transpose(2, 0, 3, 1, 4, 5).reshape(4, NX, NY, CZ)

    weights = kernel_taps()
    read = jnp.zeros_like(field)
    for offset in range(2 * REACH + 1):
        read = read + weights[offset] * jnp.roll(field, REACH - offset, axis=1)
    spanned = smooth_padded(read, 2, NY)
    solid_fields = smooth_padded(spanned, 3, CZ)

    solid = solid_fields[0]
    moved = fluid + drag_rate * (solid_fields[1:4] - solid[None] * fluid)
    void = 1.0 / (1.0 + solid)
    coupled = jnp.concatenate([moved, void[None]], axis=0)
    columns = coupled.reshape(4, N_STREAM, CX, N_SPAN, CY, CZ).transpose(1, 3, 2, 4, 0, 5)
    columns = columns.reshape(peers, CX * CY, 4, CZ)
    block_live = (jnp.arange(Q, dtype=jnp.int32)[None, None, :] < block_counts[:, :, None]).astype(jnp.float32)
    buffer = jax.vmap(lambda table, picks: table[picks])(columns, block_slots)
    buffer = buffer * block_live[:, :, :, None, None]
    received = jnp.transpose(buffer, (1, 0, 2, 3, 4))
    return grains_after, solid_fields, received
```

```python
import functools
import math

import jax
import jax.numpy as jnp
import numpy as np
from jax import lax
from jax.experimental import pallas as pl
from jax.experimental.pallas import tpu as pltpu
from jax.sharding import PartitionSpec as P

REACH = 3
LANES = 128

spread_cells = 1.5
drag_rate = 0.25

VMEM = pl.BlockSpec(memory_space=pltpu.VMEM)
SMEM = pl.BlockSpec(memory_space=pltpu.SMEM)
NT = (((1,), (1,)), ((), ()))
NN = (((1,), (0,)), ((), ()))


def kernel_taps():
    raw = [
        math.exp(-(k * k) / (2.0 * spread_cells * spread_cells)) for k in range(-REACH, REACH + 1)
    ]
    total = sum(raw)
    return [value / total for value in raw]


def params(mib):
    return pltpu.CompilerParams(vmem_limit_bytes=mib * 2**20)


def two_pieces(matrix):
    high = matrix.astype(jnp.bfloat16)
    low = (matrix - high.astype(np.float32)).astype(jnp.bfloat16)
    return np.stack([high, low])


def band(targets, sources):
    weights = np.array(kernel_taps() + [0.0], np.float32)
    apart = sources[None, :] - targets[:, None]
    return weights[np.where(np.abs(apart) <= REACH, apart + REACH, 2 * REACH + 1)]


def depth_operator(depth):
    cells = np.arange(depth)
    return two_pieces(band(cells, cells))


def stream_operator(rows_x, rows_y):
    ys, xs = np.divmod(np.arange(rows_x * rows_y), rows_x)
    plane, halo_y = np.divmod(np.arange(REACH * rows_y), rows_y)
    source_x = np.concatenate([xs, plane - REACH, plane + rows_x])
    source_y = np.concatenate([ys, halo_y, halo_y])
    return two_pieces(band(xs, source_x) * (ys[:, None] == source_y[None, :]))


def span_operator(rows_x, rows_y):
    xs, ys = np.divmod(np.arange(rows_x * rows_y), rows_y)
    own_y, own_x = np.divmod(np.arange(rows_x * rows_y), rows_x)
    row, halo_x = np.divmod(np.arange(REACH * rows_x), rows_x)
    source_y = np.concatenate([own_y, row - REACH, row + rows_y])
    source_x = np.concatenate([own_x, halo_x, halo_x])
    return two_pieces(band(ys, source_y) * (xs[:, None] == source_x[None, :]))


def halves(values):
    high = values.astype(jnp.bfloat16)
    return high, (values - high.astype(jnp.float32)).astype(jnp.bfloat16)


def dot(left, right, dims=NN):
    return lax.dot_general(left, right, dims, preferred_element_type=jnp.float32)


def leave_kernel(grains_ref, slots_ref, counts_ref, down_ref, up_ref, kept_ref, tail, high_rows, low_rows, gone):
    slot_count = grains_ref.shape[1]
    records = grains_ref.shape[0]
    width = slots_ref.shape[1]
    tiles = slot_count // LANES
    groups = width // LANES
    unroll = 16 if tiles % 16 == 0 else 1
    rest = records - 8

    tail[...] = jnp.zeros_like(tail)

    def fill(i, carry):
        lanes = pl.ds(pl.multiple_of(i * LANES, LANES), LANES)
        tail[0:rest, lanes] = grains_ref[8:records, lanes]
        return carry

    lax.fori_loop(0, tiles, fill, 0)

    lane = lax.broadcasted_iota(jnp.int32, (8, LANES), 1)
    for which, out_ref in ((0, down_ref), (1, up_ref)):
        live_count = counts_ref[0, which]

        def group(g, carry):
            lanes = pl.ds(pl.multiple_of(g * LANES, LANES), LANES)
            slot = jnp.broadcast_to(slots_ref[which:which + 1, lanes], (8, LANES))
            tile_of = lax.shift_right_logical(slot, 7)
            lane_of = lax.bitwise_and(slot, LANES - 1)

            def scan(h, found):
                first, second = found
                for k in range(unroll):
                    tile = h * unroll + k
                    there = pl.ds(pl.multiple_of(tile * LANES, LANES), LANES)
                    hit = tile_of == tile
                    one = jnp.take_along_axis(grains_ref[0:8, there], lane_of, axis=1, mode="promise_in_bounds")
                    two = jnp.take_along_axis(tail[:, there], lane_of, axis=1, mode="promise_in_bounds")
                    first = jnp.where(hit, one, first)
                    second = jnp.where(hit, two, second)
                return first, second

            zero = jnp.zeros((8, LANES), jnp.float32)
            first, second = lax.fori_loop(0, tiles // unroll, scan, (zero, zero))
            live = (lane + g * LANES < live_count).astype(jnp.float32)
            out_ref[0:8, lanes] = first * live
            out_ref[8:records, lanes] = (second * live)[0:rest]
            return carry

        used = lax.div(live_count + (LANES - 1), LANES)
        lax.fori_loop(0, used, group, 0)

        def blank(g, carry):
            lanes = pl.ds(pl.multiple_of(g * LANES, LANES), LANES)
            out_ref[:, lanes] = jnp.zeros((records, LANES), jnp.float32)
            return carry

        lax.fori_loop(used, groups, blank, 0)

    for which in (0, 1):
        slot = slots_ref[which:which + 1, :]
        live = lax.broadcasted_iota(jnp.int32, (1, width), 1) < counts_ref[0, which]
        tile_of = jnp.where(live, lax.shift_right_logical(slot, 7), -1)
        lane_of = lax.bitwise_and(slot, LANES - 1)
        hits = lax.broadcasted_iota(jnp.int32, (tiles, width), 0) == tile_of
        high_rows[...] = jnp.where(hits, 1.0, 0.0).astype(jnp.bfloat16)
        hits = lax.broadcasted_iota(jnp.int32, (LANES, width), 0) == lane_of
        low_rows[...] = jnp.where(hits, 1.0, 0.0).astype(jnp.bfloat16)
        counted = dot(high_rows[...], low_rows[...], NT)
        gone[...] = counted if which == 0 else gone[...] + counted

    def keep(i, carry):
        lanes = pl.ds(pl.multiple_of(i * LANES, LANES), LANES)
        kept_ref[:, lanes] = grains_ref[:, lanes] * (1.0 - gone[pl.ds(i, 1), :])
        return carry

    lax.fori_loop(0, tiles, keep, 0)


def leave(grains, slots, counts):
    records, slot_count = grains.shape
    width = slots.shape[1]
    tiles = slot_count // LANES
    return pl.pallas_call(
        leave_kernel,
        out_shape=(
            jax.ShapeDtypeStruct((records, width), jnp.float32),
            jax.ShapeDtypeStruct((records, width), jnp.float32),
            jax.ShapeDtypeStruct((records, slot_count), jnp.float32),
        ),
        in_specs=[VMEM, VMEM, SMEM],
        out_specs=(VMEM, VMEM, VMEM),
        scratch_shapes=[
            pltpu.VMEM((8, slot_count), jnp.float32),
            pltpu.VMEM((tiles, width), jnp.bfloat16),
            pltpu.VMEM((LANES, width), jnp.bfloat16),
            pltpu.VMEM((tiles, LANES), jnp.float32),
        ],
        compiler_params=params(40),
        name="leave",
    )(grains, slots, counts)


def deposit_kernel(
    channels, rows_x, rows_y, chunk, kept_ref, below_ref, above_ref, cells_ref, depth_ref,
    field_ref, low_ref, high_ref, left, right, total,
):
    columns = rows_x * rows_y
    depth = depth_ref.shape[1]
    plane = rows_y * depth
    count = len(channels)
    row = lax.broadcasted_iota(jnp.int32, (16, LANES), 0).astype(jnp.float32)
    zero = jnp.zeros((16, LANES), jnp.bfloat16)
    one = jnp.ones((16, LANES), jnp.bfloat16)
    total[...] = jnp.zeros_like(total)

    def wide(values):
        return jnp.broadcast_to(values, (16, LANES)).astype(jnp.bfloat16)

    def add(source_ref, start, cell_start):
        for j in range(chunk // LANES):
            lanes = pl.ds(start + j * LANES, LANES)
            here = slice(j * LANES, (j + 1) * LANES)
            cell = cells_ref[:, pl.ds(cell_start + j * LANES, LANES)]
            radius = source_ref[9:10, lanes]
            volume = 4.18879 * (radius * radius * radius)
            parts = [
                wide(volume if c == 0 else volume * source_ref[2 + c:3 + c, lanes]) for c in channels
            ]
            x = lax.div(cell, plane)
            rest = lax.rem(cell, plane)
            y = lax.div(rest, depth)
            column = wide((y * rows_x + x).astype(jnp.float32))
            level = wide(lax.rem(rest, depth).astype(jnp.float32))
            for k in range(columns // 16):
                hit = (row + 16.0 * k).astype(jnp.bfloat16) == column
                for c in range(count):
                    left[c * columns + 16 * k:c * columns + 16 * k + 16, here] = jnp.where(hit, parts[c], zero)
            for k in range(depth // 16):
                hit = (row + 16.0 * k).astype(jnp.bfloat16) == level
                right[16 * k:16 * k + 16, here] = jnp.where(hit, one, zero)
        total[...] += dot(left[...], right[...], NT)

    def over(source_ref, offset):
        def step(i, carry):
            start = pl.multiple_of(i * chunk, chunk)
            add(source_ref, start, pl.multiple_of(start + offset, chunk))
            return carry

        lax.fori_loop(0, source_ref.shape[1] // chunk, step, 0)

    over(kept_ref, 0)
    over(below_ref, kept_ref.shape[1])
    over(above_ref, kept_ref.shape[1] + below_ref.shape[1])

    high, low = halves(total[...])
    field_ref[...] = dot(high, depth_ref[0]) + (dot(high, depth_ref[1]) + dot(low, depth_ref[0]))
    for c in range(count):
        for k in range(REACH):
            for y in range(rows_y):
                to = (c * REACH + k) * rows_y + y
                first = c * columns + y * rows_x + k
                last = first + rows_x - REACH
                low_ref[to:to + 1, :] = field_ref[first:first + 1, :]
                high_ref[to:to + 1, :] = field_ref[last:last + 1, :]


def deposit(channels, rows_x, rows_y, kept, below, above, cells, depth_op, chunk):
    columns = rows_x * rows_y
    depth = depth_op.shape[1]
    count = len(channels)
    halo = count * REACH * rows_y
    return pl.pallas_call(
        functools.partial(deposit_kernel, channels, rows_x, rows_y, chunk),
        out_shape=(
            jax.ShapeDtypeStruct((count * columns, depth), jnp.float32),
            jax.ShapeDtypeStruct((halo, depth), jnp.float32),
            jax.ShapeDtypeStruct((halo, depth), jnp.float32),
        ),
        in_specs=[VMEM] * 5,
        out_specs=(VMEM, VMEM, VMEM),
        scratch_shapes=[
            pltpu.VMEM((count * columns, chunk), jnp.bfloat16),
            pltpu.VMEM((depth, chunk), jnp.bfloat16),
            pltpu.VMEM((count * columns, depth), jnp.float32),
        ],
        compiler_params=params(40),
        name="deposit",
    )(kept, below, above, cells, depth_op)


def mix(operator_ref, pieces):
    total = None
    start = 0
    for piece in pieces:
        size = piece.shape[0]
        take = slice(start, start + size)
        high, low = halves(piece)
        value = dot(operator_ref[0, :, take], high) + (
            dot(operator_ref[1, :, take], high) + dot(operator_ref[0, :, take], low)
        )
        total = value if total is None else total + value
        start += size
    return total


def stream_kernel(count, own_ref, before_ref, after_ref, operator_ref, field_ref, low_ref, high_ref):
    columns = own_ref.shape[0] // count
    halo = before_ref.shape[0] // count
    edge = low_ref.shape[0] // count
    for c in range(count):
        own = slice(c * columns, (c + 1) * columns)
        side = slice(c * halo, (c + 1) * halo)
        value = mix(operator_ref, [own_ref[own, :], jnp.concatenate([before_ref[side, :], after_ref[side, :]], axis=0)])
        field_ref[own, :] = value
        low_ref[c * edge:(c + 1) * edge, :] = value[0:edge]
        high_ref[c * edge:(c + 1) * edge, :] = value[columns - edge:columns]


def stream_pass(count, rows_x, own, before, after, operator):
    edge = count * REACH * rows_x
    depth = own.shape[1]
    return pl.pallas_call(
        functools.partial(stream_kernel, count),
        out_shape=(
            jax.ShapeDtypeStruct(own.shape, jnp.float32),
            jax.ShapeDtypeStruct((edge, depth), jnp.float32),
            jax.ShapeDtypeStruct((edge, depth), jnp.float32),
        ),
        in_specs=[VMEM] * 4,
        out_specs=(VMEM, VMEM, VMEM),
        compiler_params=params(40),
        name="stream_pass",
    )(own, before, after, operator)


def span_kernel(count, rows_q, own_ref, before_ref, after_ref, operator_ref, fluid_ref, picks_ref, solid_ref, out_ref):
    columns = own_ref.shape[0] // count
    edge = before_ref.shape[0] // count
    slots = picks_ref.shape[0]
    choose = picks_ref[...] == lax.broadcasted_iota(jnp.int32, (slots, columns), 1)
    choose = jnp.where(choose, 1.0, 0.0).astype(jnp.bfloat16)
    solids = []
    for c in range(count):
        own = slice(c * columns, (c + 1) * columns)
        side = slice(c * edge, (c + 1) * edge)
        value = mix(operator_ref, [own_ref[own, :], before_ref[side, :], after_ref[side, :]])
        solid_ref[own, :] = value
        solids.append(value)
    for c in range(count):
        if c + 1 < count:
            flow = fluid_ref[c * columns:(c + 1) * columns, :]
            value = flow + drag_rate * (solids[c + 1] - solids[0] * flow)
        else:
            value = 1.0 / (1.0 + solids[0])
        first, rest = halves(value)
        second, third = halves(value - first.astype(jnp.float32))
        sent = dot(choose, first) + (dot(choose, second) + dot(choose, third))
        out_ref[:, c * rows_q:(c + 1) * rows_q, :] = sent.reshape(slots // rows_q, rows_q, -1)


def span_pass(count, own, before, after, operator, fluid, picks, peers, rows_q):
    depth = own.shape[1]
    return pl.pallas_call(
        functools.partial(span_kernel, count, rows_q),
        out_shape=(
            jax.ShapeDtypeStruct(own.shape, jnp.float32),
            jax.ShapeDtypeStruct((peers, count * rows_q, depth), jnp.float32),
        ),
        in_specs=[VMEM] * 6,
        out_specs=(VMEM, VMEM),
        compiler_params=params(40),
        name="span_pass",
    )(own, before, after, operator, fluid, picks)


def shift(value, axis, steps, periodic):
    count = lax.axis_size(axis)
    pairs = [
        (source, (source + steps) % count)
        for source in range(count)
        if periodic or 0 <= source + steps < count
    ]
    return lax.ppermute(value, axis, pairs)


def per_device(grains, send_slots, send_counts, cell_index, fluid, block_slots, block_counts):
    rows_x, rows_y, depth = fluid.shape[1:]
    columns = rows_x * rows_y
    width = send_slots.shape[2]
    peers, rows_q = block_slots.shape[1:]

    down, up, kept = leave(grains, send_slots[0], send_counts)
    below = shift(down, "stream", 1, True)
    above = shift(up, "stream", -1, True)
    grains_after = jnp.concatenate([kept, below, above], axis=1)

    alive = lax.broadcasted_iota(jnp.int32, (peers, rows_q), 1) < block_counts[0][:, None]
    picks = jnp.where(alive, block_slots[0], -1).reshape(peers * rows_q, 1)

    depth_op = jnp.asarray(depth_operator(depth))
    stream_op = jnp.asarray(stream_operator(rows_x, rows_y))
    span_op = jnp.asarray(span_operator(rows_x, rows_y))
    cells = cell_index.reshape(1, -1)
    chunk = math.gcd(grains.shape[1], math.gcd(width, 2048))

    field, low, high = deposit((0, 1, 2, 3), rows_x, rows_y, kept, below, above, cells, depth_op, chunk)
    before = shift(high, "stream", 1, True)
    after = shift(low, "stream", -1, True)
    field, low, high = stream_pass(4, rows_x, field, before, after, stream_op)
    before = shift(high, "span", 1, False)
    after = shift(low, "span", -1, False)
    solid, outgoing = span_pass(
        4, field, before, after, span_op, fluid.reshape(3 * columns, depth), picks, peers, rows_q
    )
    arrived = lax.all_to_all(outgoing, ("stream", "span"), split_axis=0, concat_axis=0, tiled=True)
    received = arrived.reshape(peers, 4, rows_q, depth).transpose(0, 2, 1, 3)
    return grains_after, solid.reshape(4, rows_x, rows_y, depth), received[None]


def solution(mesh):
    return jax.shard_map(
        per_device,
        mesh=mesh,
        in_specs=(
            P(None, ("stream", "span")),
            P(("stream", "span"), None, None),
            P(("stream", "span"), None),
            P(("stream", "span")),
            P(None, "stream", "span", None),
            P(("stream", "span"), None, None),
            P(("stream", "span"), None),
        ),
        out_specs=(
            P(None, ("stream", "span")),
            P(None, "stream", "span", None),
            P(("stream", "span"), None, None, None, None),
        ),
        check_vma=False,
    )
```

```python
import functools
import math

import jax
import jax.numpy as jnp
from jax import lax
from jax.experimental import pallas as pl
from jax.experimental.pallas import tpu as pltpu
from jax.sharding import PartitionSpec as P

REACH = 3
LANES = 128
RECORD = 16

spread_cells = 1.5
drag_rate = 0.25

VMEM = pl.BlockSpec(memory_space=pltpu.VMEM)
ANY = pl.BlockSpec(memory_space=pl.ANY)
HBM = pl.BlockSpec(memory_space=pltpu.HBM)
NT = (((1,), (1,)), ((), ()))
NN = (((1,), (0,)), ((), ()))

QUANT_ROW = (0, 3, 4, 5)
COLUMN_ROW = 6
LEVEL_ROW = 7


def kernel_taps():
    raw = [
        math.exp(-(k * k) / (2.0 * spread_cells * spread_cells)) for k in range(-REACH, REACH + 1)
    ]
    total = sum(raw)
    return [value / total for value in raw]


def params(mib):
    return pltpu.CompilerParams(vmem_limit_bytes=mib * 2**20)


def cost(micros):
    return pl.CostEstimate(flops=0, bytes_accessed=int(micros * 3.0e6), transcendentals=0)


def split(values, size):
    if size & (size - 1):
        return lax.div(values, size), lax.rem(values, size)
    return lax.shift_right_logical(values, size.bit_length() - 1), lax.bitwise_and(values, size - 1)


def halves(values):
    high = values.astype(jnp.bfloat16)
    return high, (values - high.astype(jnp.float32)).astype(jnp.bfloat16)


def dot(left, right, dims=NN):
    return lax.dot_general(left, right, dims, preferred_element_type=jnp.float32)


def wide(values):
    return jnp.broadcast_to(values, (16, LANES)).astype(jnp.bfloat16)


def lane_tile(i):
    return pl.ds(pl.multiple_of(i * LANES, LANES), LANES)


def in_hbm(*values):
    return tuple(pltpu.with_memory_space_constraint(value, pltpu.HBM) for value in values)


def leave_kernel(
    grains_ref, slots_hbm, counts_hbm, down_ref, up_ref, stage, table, picked, slots_v, slots_s, counts_s, sems
):
    records, slot_count = grains_ref.shape
    width = down_ref.shape[1]
    rows = table.shape[0]
    parts = slot_count // rows if slot_count % rows == 0 else slot_count // rows + 1
    copies = [
        pltpu.make_async_copy(slots_hbm, slots_v, sems.at[0]),
        pltpu.make_async_copy(slots_hbm, slots_s, sems.at[1]),
        pltpu.make_async_copy(counts_hbm, counts_s, sems.at[2]),
    ]
    for copy in copies:
        copy.start()

    for part in range(parts):
        size = min(rows, slot_count - part * rows)
        here = slice(part * rows, part * rows + size)
        stage[part * RECORD:part * RECORD + 8, 0:size] = grains_ref[0:8, here]
        stage[part * RECORD + 8:part * RECORD + records, 0:size] = grains_ref[8:records, here]
    for block in range(rows // LANES):
        here = slice(block * LANES, (block + 1) * LANES)
        table[here, :] = jnp.transpose(stage[:, here])
    for copy in copies:
        copy.wait()

    run = picked.shape[0]
    lane = lax.broadcasted_iota(jnp.int32, (8, LANES), 1)
    for which, out_ref in ((0, down_ref), (1, up_ref)):
        live_count = counts_s[0, which]

        def gather(i, carry):
            base = i * run
            for k in range(run):
                row = lax.bitwise_and(slots_s[which, base + k], rows - 1)
                picked[k:k + 1, :] = table[pl.ds(row, 1), :]
            for piece in range(run // LANES):
                lanes = pl.ds(pl.multiple_of(base + piece * LANES, LANES), LANES)
                turned = jnp.transpose(picked[piece * LANES:(piece + 1) * LANES, :])
                slot = jnp.broadcast_to(slots_v[which:which + 1, lanes], (8, LANES))
                part_of = lax.shift_right_logical(slot, rows.bit_length() - 1)
                live = lane + (base + piece * LANES) < live_count
                first = jnp.zeros((8, LANES), jnp.float32)
                second = first
                for part in range(parts):
                    hit = jnp.logical_and(live, part_of == part)
                    first = jnp.where(hit, turned[part * RECORD:part * RECORD + 8], first)
                    second = jnp.where(hit, turned[part * RECORD + 8:part * RECORD + 16], second)
                out_ref[0:8, lanes] = first
                out_ref[8:records, lanes] = second[0:records - 8]
            return carry

        used = lax.div(live_count + (run - 1), run)
        lax.fori_loop(0, used, gather, 0)

        def blank(i, carry):
            lanes = pl.ds(pl.multiple_of(i * run, LANES), run)
            out_ref[:, lanes] = jnp.zeros((records, run), jnp.float32)
            return carry

        lax.fori_loop(used, width // run, blank, 0)


def leave(grains, slots, counts):
    records, slot_count = grains.shape
    width = slots.shape[1]
    rows = max(LANES, 1 << (-(-slot_count // 8) - 1).bit_length())
    run = 2 * LANES if width % (2 * LANES) == 0 else LANES
    out = jax.ShapeDtypeStruct((records, width), jnp.float32)
    return pl.pallas_call(
        leave_kernel,
        out_shape=(out, out),
        in_specs=[VMEM, HBM, HBM],
        out_specs=(VMEM, VMEM),
        scratch_shapes=[
            pltpu.VMEM((LANES, rows), jnp.float32),
            pltpu.VMEM((rows, LANES), jnp.float32),
            pltpu.VMEM((run, LANES), jnp.float32),
            pltpu.VMEM(slots.shape, jnp.int32),
            pltpu.SMEM(slots.shape, jnp.int32),
            pltpu.SMEM(counts.shape, jnp.int32),
            pltpu.SemaphoreType.DMA((3,)),
        ],
        compiler_params=params(16),
        cost_estimate=cost(8),
        name="leave",
    )(grains, *in_hbm(slots, counts))


def weights_at(apart):
    taps = kernel_taps()[REACH:]
    apart = jnp.abs(apart)
    value = jnp.where(apart == 0, taps[0], 0.0)
    for k in range(1, REACH + 1):
        value = jnp.where(apart == k, taps[k], value)
    return value


def put_operator(out_ref, start, value):
    high, low = halves(value)
    stop = start + value.shape[1]
    out_ref[0, :, start:stop] = high
    out_ref[1, :, start:stop] = low


def keep_kernel(
    rows_x, rows_y, depth, grains_ref, slots_hbm, counts_hbm, cells_hbm, picks_hbm, alive_hbm,
    after_ref, quant_ref, depth_ref, stream_ref, span_ref, choose_ref,
    slots_v, counts_s, cells_v, picks_v, alive_v, high_rows, low_rows, gone, sems,
):
    records, slot_count = grains_ref.shape
    total = after_ref.shape[1]
    width = slots_v.shape[1]
    tiles = slot_count // LANES
    columns = rows_x * rows_y
    sources = (slots_hbm, counts_hbm, cells_hbm, picks_hbm, alive_hbm)
    targets = (slots_v, counts_s, cells_v, picks_v, alive_v)
    copies = [
        pltpu.make_async_copy(source, target, sems.at[i])
        for i, (source, target) in enumerate(zip(sources, targets))
    ]
    for copy in copies:
        copy.start()

    target = lax.broadcasted_iota(jnp.int32, (depth, depth), 0)
    source = lax.broadcasted_iota(jnp.int32, (depth, depth), 1)
    put_operator(depth_ref, 0, weights_at(target - source))

    own = (columns, columns)
    target_y, target_x = split(lax.broadcasted_iota(jnp.int32, own, 0), rows_x)
    source_y, source_x = split(lax.broadcasted_iota(jnp.int32, own, 1), rows_x)
    put_operator(stream_ref, 0, jnp.where(target_y == source_y, weights_at(target_x - source_x), 0.0))
    side = (columns, 2 * REACH * rows_y)
    target_y, target_x = split(lax.broadcasted_iota(jnp.int32, side, 0), rows_x)
    plane, source_y = split(lax.broadcasted_iota(jnp.int32, side, 1), rows_y)
    source_x = jnp.where(plane < REACH, plane - REACH, plane - REACH + rows_x)
    put_operator(stream_ref, columns, jnp.where(target_y == source_y, weights_at(target_x - source_x), 0.0))

    target_x, target_y = split(lax.broadcasted_iota(jnp.int32, own, 0), rows_y)
    source_y, source_x = split(lax.broadcasted_iota(jnp.int32, own, 1), rows_x)
    put_operator(span_ref, 0, jnp.where(target_x == source_x, weights_at(target_y - source_y), 0.0))
    side = (columns, 2 * REACH * rows_x)
    target_x, target_y = split(lax.broadcasted_iota(jnp.int32, side, 0), rows_y)
    row, source_x = split(lax.broadcasted_iota(jnp.int32, side, 1), rows_x)
    source_y = jnp.where(row < REACH, row - REACH, row - REACH + rows_y)
    put_operator(span_ref, columns, jnp.where(target_x == source_x, weights_at(target_y - source_y), 0.0))

    for copy in copies:
        copy.wait()

    rows_q, peers = picks_v.shape
    alive = lax.broadcasted_iota(jnp.int32, (rows_q, peers), 0) < alive_v[...]
    picks = jnp.where(alive, picks_v[...], -1)
    place_e, place_q = split(lax.broadcasted_iota(jnp.int32, (peers * rows_q, peers), 0), rows_q)
    here = place_e == lax.broadcasted_iota(jnp.int32, (peers * rows_q, peers), 1)
    column = lax.broadcasted_iota(jnp.int32, (columns, peers), 0)
    chosen = None
    for q in range(rows_q):
        place = jnp.where(jnp.logical_and(here, place_q == q), 1.0, 0.0).astype(jnp.bfloat16)
        named = jnp.where(column == picks[q:q + 1, :], 1.0, 0.0).astype(jnp.bfloat16)
        value = dot(place, named, NT)
        chosen = value if chosen is None else chosen + value
    choose_ref[...] = chosen.astype(jnp.bfloat16)

    row16 = lax.broadcasted_iota(jnp.int32, (16, LANES), 0).astype(jnp.float32)
    lane = lax.broadcasted_iota(jnp.int32, (1, LANES), 1)
    zero = jnp.zeros((16, LANES), jnp.bfloat16)
    one = jnp.ones((16, LANES), jnp.bfloat16)
    for which in (0, 1):

        def mark(i, carry):
            lanes = lane_tile(i)
            to = pl.ds(pl.multiple_of(which * width + i * LANES, LANES), LANES)
            slot = slots_v[which:which + 1, lanes]
            tile_of, lane_of = split(slot, LANES)
            tile_of = jnp.where(lane + i * LANES < counts_s[0, which], tile_of, -1)
            tile_of = wide(tile_of.astype(jnp.float32))
            lane_of = wide(lane_of.astype(jnp.float32))
            for k in range(high_rows.shape[0] // 16):
                hit = (row16 + 16.0 * k).astype(jnp.bfloat16) == tile_of
                high_rows[16 * k:16 * k + 16, to] = jnp.where(hit, one, zero)
            for k in range(LANES // 16):
                hit = (row16 + 16.0 * k).astype(jnp.bfloat16) == lane_of
                low_rows[16 * k:16 * k + 16, to] = jnp.where(hit, one, zero)
            return carry

        lax.fori_loop(0, width // LANES, mark, 0, unroll=4)
    gone[...] = dot(high_rows[...], low_rows[...], NT)

    row8 = lax.broadcasted_iota(jnp.int32, (8, LANES), 0)

    def place(cell):
        x, rest = split(cell, rows_y * depth)
        y, level = split(rest, depth)
        return (y * rows_x + x).astype(jnp.float32), level.astype(jnp.float32)

    def keep(i, carry):
        lanes = lane_tile(i)
        stay = 1.0 - gone[pl.ds(i, 1), :]
        head = grains_ref[0:8, lanes] * stay
        rest = grains_ref[8:records, lanes] * stay
        after_ref[0:8, lanes] = head
        after_ref[8:records, lanes] = rest
        radius = rest[1:2]
        volume = 4.18879 * (radius * radius * radius)
        col, lev = place(cells_v[:, lanes])
        value = jnp.where(row8 == QUANT_ROW[0], volume, volume * head)
        value = jnp.where(row8 == COLUMN_ROW, col, value)
        quant_ref[:, lanes] = jnp.where(row8 == LEVEL_ROW, lev, value)
        return carry

    lax.fori_loop(0, tiles, keep, 0, unroll=8)

    def arrivals(i, carry):
        lanes = lane_tile(i)
        col, lev = place(cells_v[:, lanes])
        quant_ref[:, lanes] = jnp.where(row8 == COLUMN_ROW, col, lev)
        return carry

    lax.fori_loop(tiles, total // LANES, arrivals, 0, unroll=8)


def keep(grains, slots, counts, cells, picks, alive, rows_x, rows_y, depth):
    records, slot_count = grains.shape
    total = cells.shape[1]
    columns = rows_x * rows_y
    marks = -(-(slot_count // LANES) // 16) * 16
    f32, bf16, i32 = jnp.float32, jnp.bfloat16, jnp.int32
    return pl.pallas_call(
        functools.partial(keep_kernel, rows_x, rows_y, depth),
        out_shape=(
            jax.ShapeDtypeStruct((records, total), f32),
            jax.ShapeDtypeStruct((8, total), f32),
            jax.ShapeDtypeStruct((2, depth, depth), bf16),
            jax.ShapeDtypeStruct((2, columns, columns + 2 * REACH * rows_y), bf16),
            jax.ShapeDtypeStruct((2, columns, columns + 2 * REACH * rows_x), bf16),
            jax.ShapeDtypeStruct((picks.size, columns), bf16),
        ),
        in_specs=[VMEM] + [HBM] * 5,
        out_specs=(VMEM,) * 6,
        scratch_shapes=[
            pltpu.VMEM(slots.shape, i32),
            pltpu.SMEM(counts.shape, i32),
            pltpu.VMEM(cells.shape, i32),
            pltpu.VMEM(picks.shape, i32),
            pltpu.VMEM(alive.shape, i32),
            pltpu.VMEM((marks, 2 * slots.shape[1]), bf16),
            pltpu.VMEM((LANES, 2 * slots.shape[1]), bf16),
            pltpu.VMEM((marks, LANES), f32),
            pltpu.SemaphoreType.DMA((5,)),
        ],
        compiler_params=params(20),
        cost_estimate=cost(4),
        name="keep",
    )(grains, *in_hbm(slots, counts, cells, picks, alive))


def join_kernel(after_in, quant_in, below_ref, above_ref, after_ref, quant_ref, sems):
    records, width = below_ref.shape
    start = after_ref.shape[1] - 2 * width
    row8 = lax.broadcasted_iota(jnp.int32, (8, LANES), 0)
    copies = []
    for n, arrived in enumerate((below_ref, above_ref)):
        to = after_ref.at[:, pl.ds(start + n * width, width)]
        copies.append(pltpu.make_async_copy(arrived, to, sems.at[n]))
        copies[n].start()
    for n, arrived in enumerate((below_ref, above_ref)):

        def step(i, carry):
            lanes = lane_tile(i)
            to = pl.ds(pl.multiple_of(start + n * width + i * LANES, LANES), LANES)
            head = arrived[0:8, lanes]
            radius = arrived[9:10, lanes]
            volume = 4.18879 * (radius * radius * radius)
            value = jnp.where(row8 == QUANT_ROW[0], volume, volume * head)
            quant_ref[:, to] = jnp.where(row8 >= COLUMN_ROW, quant_in[:, to], value)
            return carry

        lax.fori_loop(0, width // LANES, step, 0, unroll=8)
    for copy in copies:
        copy.wait()


def join(after, quant, below, above):
    return pl.pallas_call(
        join_kernel,
        out_shape=(
            jax.ShapeDtypeStruct(after.shape, after.dtype),
            jax.ShapeDtypeStruct(quant.shape, quant.dtype),
        ),
        in_specs=[HBM, VMEM, VMEM, VMEM],
        out_specs=(HBM, VMEM),
        scratch_shapes=[pltpu.SemaphoreType.DMA((2,))],
        input_output_aliases={0: 0, 1: 1},
        compiler_params=params(16),
        cost_estimate=cost(1),
        name="join",
    )(after, quant, below, above)


def deposit_kernel(channels, rows_x, rows_y, chunk, span, begins, ends, earlier, *refs):
    refs = list(refs)
    quant_ref = refs.pop(0)
    partial_ref = None if begins else refs.pop(0)
    depth_ref = refs.pop(0) if ends else None
    del refs[:earlier]
    field_ref = refs.pop(0)
    low_ref, high_ref = (refs.pop(0), refs.pop(0)) if ends else (None, None)
    left_a, left_b, right_a, right_b, total = refs
    first, last = span
    columns = rows_x * rows_y
    depth = total.shape[1]
    count = len(channels)
    row16 = lax.broadcasted_iota(jnp.int32, (16, LANES), 0).astype(jnp.float32)
    zero = jnp.zeros((16, LANES), jnp.bfloat16)
    one = jnp.ones((16, LANES), jnp.bfloat16)
    total[...] = jnp.zeros_like(total) if begins else partial_ref[...]

    def build(left, right, step):
        for j in range(chunk // LANES):
            here = slice(j * LANES, (j + 1) * LANES)
            lanes = pl.ds(pl.multiple_of(step * chunk + j * LANES, LANES), LANES)
            parts = [wide(quant_ref[QUANT_ROW[c]:QUANT_ROW[c] + 1, lanes]) for c in channels]
            column = wide(quant_ref[COLUMN_ROW:COLUMN_ROW + 1, lanes])
            level = wide(quant_ref[LEVEL_ROW:LEVEL_ROW + 1, lanes])
            for k in range(columns // 16):
                hit = (row16 + 16.0 * k).astype(jnp.bfloat16) == column
                for c in range(count):
                    left[c * columns + 16 * k:c * columns + 16 * k + 16, here] = jnp.where(hit, parts[c], zero)
            for k in range(depth // 16):
                hit = (row16 + 16.0 * k).astype(jnp.bfloat16) == level
                right[16 * k:16 * k + 16, here] = jnp.where(hit, one, zero)

    build(left_a, right_a, first)

    def two(i, carry):
        now = first + 2 * i
        build(left_b, right_b, now + 1)
        total[...] += dot(left_a[...], right_a[...], NT)
        build(left_a, right_a, jnp.minimum(now + 2, last - 1))
        total[...] += dot(left_b[...], right_b[...], NT)
        return carry

    lax.fori_loop(0, (last - first) // 2, two, 0)
    if (last - first) % 2:
        total[...] += dot(left_a[...], right_a[...], NT)

    if not ends:
        field_ref[...] = total[...]
        return
    high, low = halves(total[...])
    field_ref[...] = dot(high, depth_ref[0]) + (dot(high, depth_ref[1]) + dot(low, depth_ref[0]))
    for c in range(count):
        for k in range(REACH):
            for y in range(rows_y):
                to = (c * REACH + k) * rows_y + y
                low_row = c * columns + y * rows_x + k
                high_row = low_row + rows_x - REACH
                low_ref[to:to + 1, :] = field_ref[low_row:low_row + 1, :]
                high_ref[to:to + 1, :] = field_ref[high_row:high_row + 1, :]


def deposit(channels, rows_x, rows_y, depth, chunk, span, quant, partial, depth_op, earlier):
    columns = rows_x * rows_y
    count = len(channels)
    begins, ends = partial is None, depth_op is not None
    field = jax.ShapeDtypeStruct((count * columns, depth), jnp.float32)
    halo = jax.ShapeDtypeStruct((count * REACH * rows_y, depth), jnp.float32)
    operands = [quant] + ([] if begins else [partial]) + ([depth_op] if ends else [])
    outs = (field, halo, halo) if ends else (field,)
    left = pltpu.VMEM((count * columns, chunk), jnp.bfloat16)
    right = pltpu.VMEM((depth, chunk), jnp.bfloat16)
    return pl.pallas_call(
        functools.partial(deposit_kernel, channels, rows_x, rows_y, chunk, span, begins, ends, len(earlier)),
        out_shape=outs,
        in_specs=[VMEM] * len(operands) + [ANY] * len(earlier),
        out_specs=(VMEM,) * len(outs),
        scratch_shapes=[left, left, right, right, pltpu.VMEM(field.shape, jnp.float32)],
        compiler_params=params(20),
        cost_estimate=cost(0.4 * count * (span[1] - span[0])),
        name="deposit",
    )(*operands, *earlier)


def mix(operator_ref, pieces):
    total = None
    start = 0
    for piece in pieces:
        take = slice(start, start + piece.shape[0])
        high, low = halves(piece)
        value = dot(operator_ref[0, :, take], high) + (
            dot(operator_ref[1, :, take], high) + dot(operator_ref[0, :, take], low)
        )
        total = value if total is None else total + value
        start += piece.shape[0]
    return total


def stream_kernel(count, own_ref, before_ref, after_ref, operator_ref, *refs):
    field_ref, low_ref, high_ref = refs[-3:]
    columns = own_ref.shape[0] // count
    halo = before_ref.shape[0] // count
    edge = low_ref.shape[0] // count
    for c in range(count):
        own = slice(c * columns, (c + 1) * columns)
        side = slice(c * halo, (c + 1) * halo)
        value = mix(operator_ref, [own_ref[own, :], jnp.concatenate([before_ref[side, :], after_ref[side, :]], axis=0)])
        field_ref[own, :] = value
        low_ref[c * edge:(c + 1) * edge, :] = value[0:edge]
        high_ref[c * edge:(c + 1) * edge, :] = value[columns - edge:columns]


def stream_pass(count, rows_x, own, before, after, operator, earlier):
    edge = jax.ShapeDtypeStruct((count * REACH * rows_x, own.shape[1]), jnp.float32)
    return pl.pallas_call(
        functools.partial(stream_kernel, count),
        out_shape=(jax.ShapeDtypeStruct(own.shape, jnp.float32), edge, edge),
        in_specs=[VMEM] * 4 + [ANY] * len(earlier),
        out_specs=(VMEM,) * 3,
        compiler_params=params(12),
        cost_estimate=cost(0.4 * count),
        name="stream_pass",
    )(own, before, after, operator, *earlier)


def span_kernel(channels, rows_q, *refs):
    refs = list(refs)
    own_ref, before_ref, after_ref, operator_ref, choose_ref, fluid_ref = refs[:6]
    base_ref = None if 0 in channels else refs[6]
    solid_ref, out_ref = refs[-2:]
    count = len(channels)
    columns = own_ref.shape[0] // count
    edge = before_ref.shape[0] // count
    choose = choose_ref[...]
    solids = {}
    for n, c in enumerate(channels):
        own = slice(n * columns, (n + 1) * columns)
        side = slice(n * edge, (n + 1) * edge)
        value = mix(operator_ref, [own_ref[own, :], jnp.concatenate([before_ref[side, :], after_ref[side, :]], axis=0)])
        solid_ref[own, :] = value
        solids[c] = value
    base = solids[0] if base_ref is None else base_ref[0:columns, :]
    for n, c in enumerate(channels):
        if c == 0:
            value = 1.0 / (1.0 + base)
        else:
            flow = fluid_ref[(c - 1) * columns:c * columns, :]
            value = flow + drag_rate * (solids[c] - base * flow)
        first, rest = halves(value)
        second, third = halves(value - first.astype(jnp.float32))
        sent = dot(choose, first) + (dot(choose, second) + dot(choose, third))
        out_ref[:, :, count - 1 - n, :] = sent.reshape(sent.shape[0] // rows_q, rows_q, -1)


def span_pass(channels, own, before, after, operator, choose, fluid, base, peers, rows_q, earlier):
    count = len(channels)
    operands = [own, before, after, operator, choose, fluid] + ([] if base is None else [base])
    return pl.pallas_call(
        functools.partial(span_kernel, channels, rows_q),
        out_shape=(
            jax.ShapeDtypeStruct(own.shape, jnp.float32),
            jax.ShapeDtypeStruct((peers, rows_q, count, own.shape[1]), jnp.float32),
        ),
        in_specs=[VMEM] * len(operands) + [ANY] * len(earlier),
        out_specs=(VMEM, VMEM),
        compiler_params=params(16),
        cost_estimate=cost(0.8 * count),
        name="span_pass",
    )(*operands, *earlier)


def shift(value, axis, steps, periodic):
    count = lax.axis_size(axis)
    pairs = [
        (source, (source + steps) % count)
        for source in range(count)
        if periodic or 0 <= source + steps < count
    ]
    return lax.ppermute(value, axis, pairs)


def per_device(grains, send_slots, send_counts, cell_index, fluid, block_slots, block_counts):
    rows_x, rows_y, depth = fluid.shape[1:]
    columns = rows_x * rows_y
    width = send_slots.shape[2]
    peers, rows_q = block_slots.shape[1:]
    total = cell_index.shape[0]
    axes = ("stream", "span")

    down, up = leave(grains, send_slots[0], send_counts)
    below = shift(down, "stream", 1, True)
    above = shift(up, "stream", -1, True)
    after, quant, depth_op, stream_op, span_op, choose = keep(
        grains, send_slots[0], send_counts, cell_index.reshape(1, -1),
        block_slots[0].T, block_counts, rows_x, rows_y, depth,
    )
    grains_after, quant = join(after, quant, below, above)

    chunk = math.gcd(total, 2048)
    steps = total // chunk
    middle = steps // 4 * 2
    flow = fluid.reshape(3 * columns, depth)

    def add(channels, span, partial, last, earlier=()):
        return deposit(
            channels, rows_x, rows_y, depth, chunk, span, quant, partial, depth_op if last else None, earlier
        )

    def stream(field, low, high, earlier):
        before = shift(high, "stream", 1, True)
        after = shift(low, "stream", -1, True)
        return stream_pass(field.shape[0] // columns, rows_x, field, before, after, stream_op, earlier)

    def span(channels, field, low, high, base, earlier):
        before = shift(high, "span", 1, False)
        after = shift(low, "span", -1, False)
        return span_pass(
            channels, field, before, after, span_op, choose, flow, base, peers, rows_q, earlier
        )

    def exchange(outgoing):
        return lax.all_to_all(outgoing, axes, split_axis=0, concat_axis=0, tiled=True)

    outer = add((0, 3), (0, steps), None, True)
    (inner,) = add((2, 1), (0, middle), None, False)
    outer = stream(*outer, (inner,))
    inner = add((2, 1), (middle, steps), inner, True, outer[:1])
    solid_outer, outgoing_outer = span((0, 3), *outer, None, inner[:1])
    arrived_outer = exchange(outgoing_outer)
    inner = stream(*inner, (outgoing_outer,))
    solid_inner, outgoing_inner = span((2, 1), *inner, solid_outer, ())
    arrived_inner = exchange(outgoing_inner)

    solid = jnp.concatenate(
        [solid_outer[:columns], solid_inner[columns:], solid_inner[:columns], solid_outer[columns:]], axis=0
    ).reshape(4, rows_x, rows_y, depth)
    received = jnp.concatenate([arrived_inner, arrived_outer], axis=2)
    return grains_after, solid, received[None]


def solution(mesh):
    return jax.shard_map(
        per_device,
        mesh=mesh,
        in_specs=(
            P(None, ("stream", "span")),
            P(("stream", "span"), None, None),
            P(("stream", "span"), None),
            P(("stream", "span")),
            P(None, "stream", "span", None),
            P(("stream", "span"), None, None),
            P(("stream", "span"), None),
        ),
        out_specs=(
            P(None, ("stream", "span")),
            P(None, "stream", "span", None),
            P(("stream", "span"), None, None, None, None),
        ),
        check_vma=False,
    )
```

```python
import functools
import math

import jax
import jax.numpy as jnp
from jax import lax
from jax.experimental import pallas as pl
from jax.experimental.pallas import tpu as pltpu
from jax.sharding import PartitionSpec as P

REACH = 3
LANES = 128
RECORD = 16

spread_cells = 1.5
drag_rate = 0.25

VMEM = pl.BlockSpec(memory_space=pltpu.VMEM)
ANY = pl.BlockSpec(memory_space=pl.ANY)
HBM = pl.BlockSpec(memory_space=pltpu.HBM)
NT = (((1,), (1,)), ((), ()))
NN = (((1,), (0,)), ((), ()))

QUANT_ROW = (0, 3, 4, 5)
COLUMN_ROW = 6
LEVEL_ROW = 7


def kernel_taps():
    raw = [
        math.exp(-(k * k) / (2.0 * spread_cells * spread_cells)) for k in range(-REACH, REACH + 1)
    ]
    total = sum(raw)
    return [value / total for value in raw]


def params(mib):
    return pltpu.CompilerParams(vmem_limit_bytes=mib * 2**20)


def cost(micros):
    return pl.CostEstimate(flops=0, bytes_accessed=int(micros * 3.0e6), transcendentals=0)


def split(values, size):
    if size & (size - 1):
        return lax.div(values, size), lax.rem(values, size)
    return lax.shift_right_logical(values, size.bit_length() - 1), lax.bitwise_and(values, size - 1)


def halves(values):
    high = values.astype(jnp.bfloat16)
    return high, (values - high.astype(jnp.float32)).astype(jnp.bfloat16)


def dot(left, right, dims=NN):
    return lax.dot_general(left, right, dims, preferred_element_type=jnp.float32)


def wide(values):
    return jnp.broadcast_to(values, (16, LANES)).astype(jnp.bfloat16)


def lane_tile(i):
    return pl.ds(pl.multiple_of(i * LANES, LANES), LANES)


def in_hbm(*values):
    return tuple(pltpu.with_memory_space_constraint(value, pltpu.HBM) for value in values)


def is_odd(axis):
    return lax.rem(lax.axis_index(axis), 2)


def leave_kernel(
    rows_x, rows_y, grains_hbm, slots_hbm, counts_hbm, first_ref, second_ref, depth_ref, stream_ref, span_ref,
    grains_ref, stage, table, picked, slots_v, slots_s, counts_s, sems,
):
    records, slot_count = grains_ref.shape
    width = first_ref.shape[1]
    rows = table.shape[0]
    parts = -(-slot_count // rows)
    sources = (grains_hbm, slots_hbm, slots_hbm, counts_hbm)
    targets = (grains_ref, slots_v, slots_s, counts_s)
    copies = [
        pltpu.make_async_copy(source, target, sems.at[i])
        for i, (source, target) in enumerate(zip(sources, targets))
    ]
    for copy in copies:
        copy.start()
    build_operators(rows_x, rows_y, depth_ref, stream_ref, span_ref)
    copies[0].wait()

    for part in range(parts):
        size = min(rows, slot_count - part * rows)
        here = slice(part * rows, part * rows + size)
        stage[part * RECORD:part * RECORD + 8, 0:size] = grains_ref[0:8, here]
        stage[part * RECORD + 8:part * RECORD + records, 0:size] = grains_ref[8:records, here]
    for block in range(rows // LANES):
        here = slice(block * LANES, (block + 1) * LANES)
        table[here, :] = jnp.transpose(stage[:, here])
    for copy in copies[1:]:
        copy.wait()

    run = picked.shape[0]
    lane = lax.broadcasted_iota(jnp.int32, (8, LANES), 1)
    odd = is_odd("stream")
    for which, out_ref in ((odd, first_ref), (1 - odd, second_ref)):
        live_count = counts_s[0, which]

        def gather(i, carry):
            base = i * run
            for k in range(run):
                row = lax.bitwise_and(slots_s[which, base + k], rows - 1)
                picked[k:k + 1, :] = table[pl.ds(row, 1), :]
            for piece in range(run // LANES):
                lanes = pl.ds(pl.multiple_of(base + piece * LANES, LANES), LANES)
                turned = jnp.transpose(picked[piece * LANES:(piece + 1) * LANES, :])
                slot = jnp.where(which == 0, slots_v[0:1, lanes], slots_v[1:2, lanes])
                slot = jnp.broadcast_to(slot, (8, LANES))
                part_of = lax.shift_right_logical(slot, rows.bit_length() - 1)
                live = lane + (base + piece * LANES) < live_count
                first = jnp.zeros((8, LANES), jnp.float32)
                second = first
                for part in range(parts):
                    hit = jnp.logical_and(live, part_of == part)
                    first = jnp.where(hit, turned[part * RECORD:part * RECORD + 8], first)
                    second = jnp.where(hit, turned[part * RECORD + 8:part * RECORD + 16], second)
                out_ref[0:8, lanes] = first
                out_ref[8:records, lanes] = second[0:records - 8]
            return carry

        used = lax.div(live_count + (run - 1), run)
        lax.fori_loop(0, used, gather, 0)

        def blank(i, carry):
            lanes = pl.ds(pl.multiple_of(i * run, LANES), run)
            out_ref[:, lanes] = jnp.zeros((records, run), jnp.float32)
            return carry

        lax.fori_loop(used, width // run, blank, 0)


def leave(grains, slots, counts, rows_x, rows_y, depth):
    records, slot_count = grains.shape
    width = slots.shape[1]
    columns = rows_x * rows_y
    rows = max(LANES, 1 << (-(-slot_count // 8) - 1).bit_length())
    run = 2 * LANES if width % (2 * LANES) == 0 else LANES
    out = jax.ShapeDtypeStruct((records, width), jnp.float32)
    bf16 = jnp.bfloat16
    return pl.pallas_call(
        functools.partial(leave_kernel, rows_x, rows_y),
        out_shape=(
            out,
            out,
            jax.ShapeDtypeStruct((2, depth, depth), bf16),
            jax.ShapeDtypeStruct((2, columns, columns + 2 * REACH * rows_y), bf16),
            jax.ShapeDtypeStruct((2, columns, columns + 2 * REACH * rows_x), bf16),
        ),
        in_specs=[HBM] * 3,
        out_specs=(VMEM,) * 5,
        scratch_shapes=[
            pltpu.VMEM(grains.shape, jnp.float32),
            pltpu.VMEM((LANES, rows), jnp.float32),
            pltpu.VMEM((rows, LANES), jnp.float32),
            pltpu.VMEM((run, LANES), jnp.float32),
            pltpu.VMEM(slots.shape, jnp.int32),
            pltpu.SMEM(slots.shape, jnp.int32),
            pltpu.SMEM(counts.shape, jnp.int32),
            pltpu.SemaphoreType.DMA((4,)),
        ],
        compiler_params=params(16),
        cost_estimate=cost(8),
        name="leave",
    )(*in_hbm(grains, slots, counts))


def weights_at(apart):
    taps = kernel_taps()[REACH:]
    apart = jnp.abs(apart)
    value = jnp.where(apart == 0, taps[0], 0.0)
    for k in range(1, REACH + 1):
        value = jnp.where(apart == k, taps[k], value)
    return value


def put_operator(out_ref, start, value):
    high, low = halves(value)
    stop = start + value.shape[1]
    out_ref[0, :, start:stop] = high
    out_ref[1, :, start:stop] = low


def build_operators(rows_x, rows_y, depth_ref, stream_ref, span_ref):
    columns = rows_x * rows_y
    depth = depth_ref.shape[1]
    target = lax.broadcasted_iota(jnp.int32, (depth, depth), 0)
    source = lax.broadcasted_iota(jnp.int32, (depth, depth), 1)
    put_operator(depth_ref, 0, weights_at(target - source))

    own = (columns, columns)
    target_y, target_x = split(lax.broadcasted_iota(jnp.int32, own, 0), rows_x)
    source_y, source_x = split(lax.broadcasted_iota(jnp.int32, own, 1), rows_x)
    put_operator(stream_ref, 0, jnp.where(target_y == source_y, weights_at(target_x - source_x), 0.0))
    side = (columns, 2 * REACH * rows_y)
    target_y, target_x = split(lax.broadcasted_iota(jnp.int32, side, 0), rows_x)
    plane, source_y = split(lax.broadcasted_iota(jnp.int32, side, 1), rows_y)
    source_x = jnp.where(plane < REACH, plane - REACH, plane - REACH + rows_x)
    put_operator(stream_ref, columns, jnp.where(target_y == source_y, weights_at(target_x - source_x), 0.0))

    target_x, target_y = split(lax.broadcasted_iota(jnp.int32, own, 0), rows_y)
    source_y, source_x = split(lax.broadcasted_iota(jnp.int32, own, 1), rows_x)
    put_operator(span_ref, 0, jnp.where(target_x == source_x, weights_at(target_y - source_y), 0.0))
    side = (columns, 2 * REACH * rows_x)
    target_x, target_y = split(lax.broadcasted_iota(jnp.int32, side, 0), rows_y)
    row, source_x = split(lax.broadcasted_iota(jnp.int32, side, 1), rows_x)
    source_y = jnp.where(row < REACH, row - REACH, row - REACH + rows_y)
    put_operator(span_ref, columns, jnp.where(target_x == source_x, weights_at(target_y - source_y), 0.0))


def keep_kernel(
    rows_x, rows_y, depth, grains_ref, slots_hbm, counts_hbm, cells_hbm, picks_hbm, alive_hbm,
    after_hbm, quant_ref, choose_ref,
    slots_v, counts_s, cells_v, picks_v, alive_v, high_rows, low_rows, gone, kept, sems,
):
    records, slot_count = grains_ref.shape
    total = quant_ref.shape[1]
    width = slots_v.shape[1]
    tiles = slot_count // LANES
    columns = rows_x * rows_y
    pieces = 4
    sources = (slots_hbm, counts_hbm, cells_hbm, picks_hbm, alive_hbm)
    targets = (slots_v, counts_s, cells_v, picks_v, alive_v)
    copies = [
        pltpu.make_async_copy(source, target, sems.at[i])
        for i, (source, target) in enumerate(zip(sources, targets))
    ]
    for copy in copies:
        copy.start()

    for copy in copies:
        copy.wait()

    rows_q, peers = picks_v.shape
    alive = lax.broadcasted_iota(jnp.int32, (rows_q, peers), 0) < alive_v[...]
    picks = jnp.where(alive, picks_v[...], -1)
    place_e, place_q = split(lax.broadcasted_iota(jnp.int32, (peers * rows_q, peers), 0), rows_q)
    here = place_e == lax.broadcasted_iota(jnp.int32, (peers * rows_q, peers), 1)
    column = lax.broadcasted_iota(jnp.int32, (columns, peers), 0)
    chosen = None
    for q in range(rows_q):
        place = jnp.where(jnp.logical_and(here, place_q == q), 1.0, 0.0).astype(jnp.bfloat16)
        named = jnp.where(column == picks[q:q + 1, :], 1.0, 0.0).astype(jnp.bfloat16)
        value = dot(place, named, NT)
        chosen = value if chosen is None else chosen + value
    choose_ref[...] = chosen.astype(jnp.bfloat16)

    row16 = lax.broadcasted_iota(jnp.int32, (16, LANES), 0).astype(jnp.float32)
    lane = lax.broadcasted_iota(jnp.int32, (1, LANES), 1)
    zero = jnp.zeros((16, LANES), jnp.bfloat16)
    one = jnp.ones((16, LANES), jnp.bfloat16)
    for which in (0, 1):

        def mark(i, carry):
            lanes = lane_tile(i)
            to = pl.ds(pl.multiple_of(which * width + i * LANES, LANES), LANES)
            slot = slots_v[which:which + 1, lanes]
            tile_of, lane_of = split(slot, LANES)
            tile_of = jnp.where(lane + i * LANES < counts_s[0, which], tile_of, -1)
            tile_of = wide(tile_of.astype(jnp.float32))
            lane_of = wide(lane_of.astype(jnp.float32))
            for k in range(high_rows.shape[0] // 16):
                hit = (row16 + 16.0 * k).astype(jnp.bfloat16) == tile_of
                high_rows[16 * k:16 * k + 16, to] = jnp.where(hit, one, zero)
            for k in range(LANES // 16):
                hit = (row16 + 16.0 * k).astype(jnp.bfloat16) == lane_of
                low_rows[16 * k:16 * k + 16, to] = jnp.where(hit, one, zero)
            return carry

        lax.fori_loop(0, width // LANES, mark, 0, unroll=4)
    gone[...] = dot(high_rows[...], low_rows[...], NT)

    row8 = lax.broadcasted_iota(jnp.int32, (8, LANES), 0)

    def place(cell):
        x, rest = split(cell, rows_y * depth)
        y, level = split(rest, depth)
        return (y * rows_x + x).astype(jnp.float32), level.astype(jnp.float32)

    def keep(i, carry):
        lanes = lane_tile(i)
        stay = 1.0 - gone[pl.ds(i, 1), :]
        head = grains_ref[0:8, lanes] * stay
        rest = grains_ref[8:records, lanes] * stay
        kept[0:8, lanes] = head
        kept[8:records, lanes] = rest
        radius = rest[1:2]
        volume = 4.18879 * (radius * radius * radius)
        col, lev = place(cells_v[:, lanes])
        value = jnp.where(row8 == QUANT_ROW[0], volume, volume * head)
        value = jnp.where(row8 == COLUMN_ROW, col, value)
        quant_ref[:, lanes] = jnp.where(row8 == LEVEL_ROW, lev, value)
        return carry

    writes = []
    for n in range(pieces):
        first = tiles * n // pieces
        last = tiles * (n + 1) // pieces
        lax.fori_loop(first, last, keep, 0, unroll=8)
        here = pl.ds(first * LANES, (last - first) * LANES)
        writes.append(pltpu.make_async_copy(kept.at[:, here], after_hbm.at[:, here], sems.at[len(copies) + n]))
        writes[n].start()

    def arrivals(i, carry):
        lanes = lane_tile(i)
        col, lev = place(cells_v[:, lanes])
        quant_ref[:, lanes] = jnp.where(row8 == COLUMN_ROW, col, lev)
        return carry

    lax.fori_loop(tiles, total // LANES, arrivals, 0, unroll=8)
    for write in writes:
        write.wait()


def keep(grains, slots, counts, cells, picks, alive, rows_x, rows_y, depth):
    records, slot_count = grains.shape
    total = cells.shape[1]
    columns = rows_x * rows_y
    marks = -(-(slot_count // LANES) // 16) * 16
    f32, bf16, i32 = jnp.float32, jnp.bfloat16, jnp.int32
    return pl.pallas_call(
        functools.partial(keep_kernel, rows_x, rows_y, depth),
        out_shape=(
            jax.ShapeDtypeStruct((records, total), f32),
            jax.ShapeDtypeStruct((8, total), f32),
            jax.ShapeDtypeStruct((picks.size, columns), bf16),
        ),
        in_specs=[VMEM] + [HBM] * 5,
        out_specs=(HBM, VMEM, VMEM),
        scratch_shapes=[
            pltpu.VMEM(slots.shape, i32),
            pltpu.SMEM(counts.shape, i32),
            pltpu.VMEM(cells.shape, i32),
            pltpu.VMEM(picks.shape, i32),
            pltpu.VMEM(alive.shape, i32),
            pltpu.VMEM((marks, 2 * slots.shape[1]), bf16),
            pltpu.VMEM((LANES, 2 * slots.shape[1]), bf16),
            pltpu.VMEM((marks, LANES), f32),
            pltpu.VMEM(grains.shape, f32),
            pltpu.SemaphoreType.DMA((9,)),
        ],
        compiler_params=params(20),
        cost_estimate=cost(4),
        name="keep",
    )(grains, *in_hbm(slots, counts, cells, picks, alive))


def join_kernel(after_in, quant_in, first_ref, second_ref, after_ref, quant_ref, sems):
    records, width = first_ref.shape
    start = after_ref.shape[1] - 2 * width
    row8 = lax.broadcasted_iota(jnp.int32, (8, LANES), 0)
    odd = is_odd("stream")
    copies = []
    for n, arrived in enumerate((first_ref, second_ref)):
        place = pl.multiple_of(start + (1 - odd if n == 0 else odd) * width, LANES)
        to = after_ref.at[:, pl.ds(place, width)]
        copies.append(pltpu.make_async_copy(arrived, to, sems.at[n]))
        copies[n].start()
    for n, arrived in enumerate((first_ref, second_ref)):

        def step(i, carry):
            lanes = lane_tile(i)
            place = start + (1 - odd if n == 0 else odd) * width
            to = pl.ds(pl.multiple_of(place + i * LANES, LANES), LANES)
            head = arrived[0:8, lanes]
            radius = arrived[9:10, lanes]
            volume = 4.18879 * (radius * radius * radius)
            value = jnp.where(row8 == QUANT_ROW[0], volume, volume * head)
            quant_ref[:, to] = jnp.where(row8 >= COLUMN_ROW, quant_in[:, to], value)
            return carry

        lax.fori_loop(0, width // LANES, step, 0, unroll=8)
    for copy in copies:
        copy.wait()


def join(after, quant, first, second):
    return pl.pallas_call(
        join_kernel,
        out_shape=(
            jax.ShapeDtypeStruct(after.shape, after.dtype),
            jax.ShapeDtypeStruct(quant.shape, quant.dtype),
        ),
        in_specs=[HBM, VMEM, VMEM, VMEM],
        out_specs=(HBM, VMEM),
        scratch_shapes=[pltpu.SemaphoreType.DMA((2,))],
        input_output_aliases={0: 0, 1: 1},
        compiler_params=params(16),
        cost_estimate=cost(1),
        name="join",
    )(*in_hbm(after), quant, first, second)


def deposit_kernel(channels, rows_x, rows_y, chunk, span, begins, ends, earlier, *refs):
    refs = list(refs)
    quant_ref = refs.pop(0)
    partial_ref = None if begins else refs.pop(0)
    depth_ref = refs.pop(0) if ends else None
    del refs[:earlier]
    field_ref = refs.pop(0)
    first_ref, second_ref = (refs.pop(0), refs.pop(0)) if ends else (None, None)
    left_a, left_b, right_a, right_b, total = refs
    begin, end = span
    columns = rows_x * rows_y
    depth = total.shape[1]
    count = len(channels)
    row16 = lax.broadcasted_iota(jnp.int32, (16, LANES), 0).astype(jnp.float32)
    zero = jnp.zeros((16, LANES), jnp.bfloat16)
    one = jnp.ones((16, LANES), jnp.bfloat16)
    total[...] = jnp.zeros_like(total) if begins else partial_ref[...]

    def build(left, right, step):
        for j in range(chunk // LANES):
            here = slice(j * LANES, (j + 1) * LANES)
            lanes = pl.ds(pl.multiple_of(step * chunk + j * LANES, LANES), LANES)
            parts = [wide(quant_ref[QUANT_ROW[c]:QUANT_ROW[c] + 1, lanes]) for c in channels]
            column = wide(quant_ref[COLUMN_ROW:COLUMN_ROW + 1, lanes])
            level = wide(quant_ref[LEVEL_ROW:LEVEL_ROW + 1, lanes])
            for k in range(columns // 16):
                hit = (row16 + 16.0 * k).astype(jnp.bfloat16) == column
                for c in range(count):
                    left[c * columns + 16 * k:c * columns + 16 * k + 16, here] = jnp.where(hit, parts[c], zero)
            for k in range(depth // 16):
                hit = (row16 + 16.0 * k).astype(jnp.bfloat16) == level
                right[16 * k:16 * k + 16, here] = jnp.where(hit, one, zero)

    build(left_a, right_a, begin)

    def two(i, carry):
        now = begin + 2 * i
        build(left_b, right_b, now + 1)
        total[...] += dot(left_a[...], right_a[...], NT)
        build(left_a, right_a, jnp.minimum(now + 2, end - 1))
        total[...] += dot(left_b[...], right_b[...], NT)
        return carry

    lax.fori_loop(0, (end - begin) // 2, two, 0)
    if (end - begin) % 2:
        total[...] += dot(left_a[...], right_a[...], NT)

    if not ends:
        field_ref[...] = total[...]
        return
    high, low = halves(total[...])
    field_ref[...] = dot(high, depth_ref[0]) + (dot(high, depth_ref[1]) + dot(low, depth_ref[0]))
    odd = is_odd("stream")
    first_x = (1 - odd) * (rows_x - REACH)
    second_x = odd * (rows_x - REACH)
    for c in range(count):
        for k in range(REACH):
            for y in range(rows_y):
                to = (c * REACH + k) * rows_y + y
                row = c * columns + y * rows_x + k
                first_ref[to:to + 1, :] = field_ref[pl.ds(row + first_x, 1), :]
                second_ref[to:to + 1, :] = field_ref[pl.ds(row + second_x, 1), :]


def deposit(channels, rows_x, rows_y, depth, chunk, span, quant, partial, depth_op, earlier):
    columns = rows_x * rows_y
    count = len(channels)
    begins, ends = partial is None, depth_op is not None
    field = jax.ShapeDtypeStruct((count * columns, depth), jnp.float32)
    halo = jax.ShapeDtypeStruct((count * REACH * rows_y, depth), jnp.float32)
    operands = [quant] + ([] if begins else [partial]) + ([depth_op] if ends else [])
    outs = (field, halo, halo) if ends else (field,)
    left = pltpu.VMEM((count * columns, chunk), jnp.bfloat16)
    right = pltpu.VMEM((depth, chunk), jnp.bfloat16)
    return pl.pallas_call(
        functools.partial(deposit_kernel, channels, rows_x, rows_y, chunk, span, begins, ends, len(earlier)),
        out_shape=outs,
        in_specs=[VMEM] * len(operands) + [ANY] * len(earlier),
        out_specs=(VMEM,) * len(outs),
        scratch_shapes=[left, left, right, right, pltpu.VMEM(field.shape, jnp.float32)],
        compiler_params=params(20),
        cost_estimate=cost(0.4 * count * (span[1] - span[0])),
        name="deposit",
    )(*operands, *earlier)


def mix(operator_ref, pieces):
    total = None
    start = 0
    for piece in pieces:
        take = slice(start, start + piece.shape[0])
        high, low = halves(piece)
        value = dot(operator_ref[0, :, take], high) + (
            dot(operator_ref[1, :, take], high) + dot(operator_ref[0, :, take], low)
        )
        total = value if total is None else total + value
        start += piece.shape[0]
    return total


def sides(axis, first, second):
    odd = is_odd(axis) == 1
    return jnp.concatenate([jnp.where(odd, first, second), jnp.where(odd, second, first)], axis=0)


def stream_kernel(count, own_ref, first_in, second_in, operator_ref, *refs):
    field_ref, first_ref, second_ref = refs[-3:]
    columns = own_ref.shape[0] // count
    halo = first_in.shape[0] // count
    edge = first_ref.shape[0] // count
    odd = is_odd("span") == 1
    for c in range(count):
        own = slice(c * columns, (c + 1) * columns)
        side = slice(c * halo, (c + 1) * halo)
        value = mix(operator_ref, [own_ref[own, :], sides("stream", first_in[side, :], second_in[side, :])])
        field_ref[own, :] = value
        low, high = value[0:edge], value[columns - edge:columns]
        first_ref[c * edge:(c + 1) * edge, :] = jnp.where(odd, low, high)
        second_ref[c * edge:(c + 1) * edge, :] = jnp.where(odd, high, low)


def stream_pass(count, rows_x, own, first, second, operator, earlier):
    edge = jax.ShapeDtypeStruct((count * REACH * rows_x, own.shape[1]), jnp.float32)
    return pl.pallas_call(
        functools.partial(stream_kernel, count),
        out_shape=(jax.ShapeDtypeStruct(own.shape, jnp.float32), edge, edge),
        in_specs=[VMEM] * 4 + [ANY] * len(earlier),
        out_specs=(VMEM,) * 3,
        compiler_params=params(12),
        cost_estimate=cost(0.4 * count),
        name="stream_pass",
    )(own, first, second, operator, *earlier)


def span_kernel(channels, rows_q, *refs):
    refs = list(refs)
    own_ref, first_in, second_in, operator_ref, choose_ref, fluid_ref = refs[:6]
    base_ref = None if 0 in channels else refs[6]
    solid_ref, out_ref = refs[-2:]
    count = len(channels)
    columns = own_ref.shape[0] // count
    edge = first_in.shape[0] // count
    choose = choose_ref[...]
    solids = {}
    for n, c in enumerate(channels):
        own = slice(n * columns, (n + 1) * columns)
        side = slice(n * edge, (n + 1) * edge)
        value = mix(operator_ref, [own_ref[own, :], sides("span", first_in[side, :], second_in[side, :])])
        solid_ref[own, :] = value
        solids[c] = value
    base = solids[0] if base_ref is None else base_ref[0:columns, :]
    for n, c in enumerate(channels):
        if c == 0:
            value = 1.0 / (1.0 + base)
        else:
            flow = fluid_ref[(c - 1) * columns:c * columns, :]
            value = flow + drag_rate * (solids[c] - base * flow)
        first, rest = halves(value)
        second, third = halves(value - first.astype(jnp.float32))
        sent = dot(choose, first) + (dot(choose, second) + dot(choose, third))
        out_ref[:, :, count - 1 - n, :] = sent.reshape(sent.shape[0] // rows_q, rows_q, -1)


def span_pass(channels, own, first, second, operator, choose, fluid, base, peers, rows_q, earlier):
    count = len(channels)
    operands = [own, first, second, operator, choose, fluid] + ([] if base is None else [base])
    return pl.pallas_call(
        functools.partial(span_kernel, channels, rows_q),
        out_shape=(
            jax.ShapeDtypeStruct(own.shape, jnp.float32),
            jax.ShapeDtypeStruct((peers, rows_q, count, own.shape[1]), jnp.float32),
        ),
        in_specs=[VMEM] * len(operands) + [ANY] * len(earlier),
        out_specs=(VMEM, VMEM),
        compiler_params=params(16),
        cost_estimate=cost(0.8 * count),
        name="span_pass",
    )(*operands, *earlier)


def swap(first, second, axis, periodic):
    count = lax.axis_size(axis)
    assert count % 2 == 0
    pairs = [(source, source ^ 1) for source in range(count)]
    others = [(source, (source + 1 if source % 2 else source - 1) % count) for source in range(count)]
    if not periodic:
        others = [pair for pair in others if abs(pair[0] - pair[1]) == 1]
    return lax.ppermute(first, axis, pairs), lax.ppermute(second, axis, others)


def per_device(grains, send_slots, send_counts, cell_index, fluid, block_slots, block_counts):
    rows_x, rows_y, depth = fluid.shape[1:]
    columns = rows_x * rows_y
    width = send_slots.shape[2]
    peers, rows_q = block_slots.shape[1:]
    total = cell_index.shape[0]
    axes = ("stream", "span")

    *leaving, depth_op, stream_op, span_op = leave(
        grains, send_slots[0], send_counts, rows_x, rows_y, depth
    )
    arrived = swap(*leaving, "stream", True)
    after, quant, choose = keep(
        grains, send_slots[0], send_counts, cell_index.reshape(1, -1),
        block_slots[0].T, block_counts, rows_x, rows_y, depth,
    )
    grains_after, quant = join(after, quant, *arrived)

    chunk = math.gcd(total, 2048)
    steps = total // chunk
    middle = steps // 4
    flow = fluid.reshape(3 * columns, depth)

    def add(channels, span, partial, last, earlier=()):
        return deposit(
            channels, rows_x, rows_y, depth, chunk, span, quant, partial, depth_op if last else None, earlier
        )

    def stream(field, first, second, earlier):
        halos = swap(first, second, "stream", True)
        return stream_pass(field.shape[0] // columns, rows_x, field, *halos, stream_op, earlier)

    def span(channels, field, first, second, base, earlier):
        halos = swap(first, second, "span", False)
        return span_pass(channels, field, *halos, span_op, choose, flow, base, peers, rows_q, earlier)

    def exchange(outgoing):
        return lax.all_to_all(outgoing, axes, split_axis=0, concat_axis=0, tiled=True)

    outer = add((0, 3), (0, steps), None, True)
    (inner,) = add((2, 1), (0, middle), None, False)
    outer = stream(*outer, (inner,))
    inner = add((2, 1), (middle, steps), inner, True, outer[:1])
    solid_outer, outgoing_outer = span((0, 3), *outer, None, inner[:1])
    inner = stream(*inner, (solid_outer,))
    outgoing_outer, inner = lax.optimization_barrier((outgoing_outer, inner))
    arrived_outer = exchange(outgoing_outer)
    solid_inner, outgoing_inner = span((2, 1), *inner, solid_outer, ())
    arrived_inner = exchange(outgoing_inner)

    solid = jnp.concatenate(
        [solid_outer[:columns], solid_inner[columns:], solid_inner[:columns], solid_outer[columns:]], axis=0
    ).reshape(4, rows_x, rows_y, depth)
    received = jnp.concatenate([arrived_inner, arrived_outer], axis=2)
    return grains_after, solid, received[None]


def solution(mesh):
    return jax.shard_map(
        per_device,
        mesh=mesh,
        in_specs=(
            P(None, ("stream", "span")),
            P(("stream", "span"), None, None),
            P(("stream", "span"), None),
            P(("stream", "span")),
            P(None, "stream", "span", None),
            P(("stream", "span"), None, None),
            P(("stream", "span"), None),
        ),
        out_specs=(
            P(None, ("stream", "span")),
            P(None, "stream", "span", None),
            P(("stream", "span"), None, None, None, None),
        ),
        check_vma=False,
    )
```

```python
import functools
import math

import jax
import jax.numpy as jnp
from jax import lax
from jax.experimental import pallas as pl
from jax.experimental.pallas import tpu as pltpu
from jax.sharding import PartitionSpec as P

REACH = 3
LANES = 128
RECORD = 16

spread_cells = 1.5
drag_rate = 0.25

VMEM = pl.BlockSpec(memory_space=pltpu.VMEM)
ANY = pl.BlockSpec(memory_space=pl.ANY)
HBM = pl.BlockSpec(memory_space=pltpu.HBM)
NT = (((1,), (1,)), ((), ()))
NN = (((1,), (0,)), ((), ()))

QUANT_ROW = (0, 3, 4, 5)
COLUMN_ROW = 6
LEVEL_ROW = 7


def kernel_taps():
    raw = [
        math.exp(-(k * k) / (2.0 * spread_cells * spread_cells)) for k in range(-REACH, REACH + 1)
    ]
    total = sum(raw)
    return [value / total for value in raw]


def params(mib):
    return pltpu.CompilerParams(vmem_limit_bytes=mib * 2**20)


def cost(micros):
    return pl.CostEstimate(flops=0, bytes_accessed=int(micros * 3.0e6), transcendentals=0)


def split(values, size):
    if size & (size - 1):
        return lax.div(values, size), lax.rem(values, size)
    return lax.shift_right_logical(values, size.bit_length() - 1), lax.bitwise_and(values, size - 1)


def halves(values):
    high = values.astype(jnp.bfloat16)
    return high, (values - high.astype(jnp.float32)).astype(jnp.bfloat16)


def dot(left, right, dims=NN):
    return lax.dot_general(left, right, dims, preferred_element_type=jnp.float32)


def wide(values):
    return jnp.broadcast_to(values, (16, LANES)).astype(jnp.bfloat16)


def lane_tile(i):
    return pl.ds(pl.multiple_of(i * LANES, LANES), LANES)


def in_hbm(*values):
    return tuple(pltpu.with_memory_space_constraint(value, pltpu.HBM) for value in values)


def is_odd(axis):
    return lax.rem(lax.axis_index(axis), 2)


def leave_kernel(
    rows_x, rows_y, grains_hbm, slots_hbm, counts_hbm, cells_hbm, picks_hbm, alive_hbm,
    first_ref, second_ref, depth_ref, stream_ref, span_ref, choose_ref, marks_ref, cells_ref,
    grains_ref, stage, table, picked, slots_v, slots_s, counts_s, picks_v, alive_v, sems,
):
    records, slot_count = grains_ref.shape
    width = first_ref.shape[1]
    rows = table.shape[0]
    parts = -(-slot_count // rows)
    sources = (grains_hbm, slots_hbm, slots_hbm, counts_hbm, picks_hbm, alive_hbm, cells_hbm)
    targets = (grains_ref, slots_v, slots_s, counts_s, picks_v, alive_v, cells_ref)
    copies = [
        pltpu.make_async_copy(source, target, sems.at[i])
        for i, (source, target) in enumerate(zip(sources, targets))
    ]
    for copy in copies:
        copy.start()
    build_operators(rows_x, rows_y, depth_ref, stream_ref, span_ref)
    copies[0].wait()

    for part in range(parts):
        size = min(rows, slot_count - part * rows)
        here = slice(part * rows, part * rows + size)
        stage[part * RECORD:part * RECORD + 8, 0:size] = grains_ref[0:8, here]
        stage[part * RECORD + 8:part * RECORD + records, 0:size] = grains_ref[8:records, here]
    for block in range(rows // LANES):
        here = slice(block * LANES, (block + 1) * LANES)
        table[here, :] = jnp.transpose(stage[:, here])
    for copy in copies[1:]:
        copy.wait()
    build_choice(picks_v, alive_v, choose_ref)
    for which in (0, 1):
        live = lax.broadcasted_iota(jnp.int32, (1, width), 1) < counts_s[0, which]
        marks_ref[which:which + 1, :] = jnp.where(live, slots_v[which:which + 1, :], -1)

    run = picked.shape[0]
    lane = lax.broadcasted_iota(jnp.int32, (8, LANES), 1)
    odd = is_odd("stream")
    for which, out_ref in ((odd, first_ref), (1 - odd, second_ref)):
        live_count = counts_s[0, which]

        def gather(i, carry):
            base = i * run
            for k in range(run):
                row = lax.bitwise_and(slots_s[which, base + k], rows - 1)
                picked[k:k + 1, :] = table[pl.ds(row, 1), :]
            for piece in range(run // LANES):
                lanes = pl.ds(pl.multiple_of(base + piece * LANES, LANES), LANES)
                turned = jnp.transpose(picked[piece * LANES:(piece + 1) * LANES, :])
                slot = jnp.where(which == 0, slots_v[0:1, lanes], slots_v[1:2, lanes])
                slot = jnp.broadcast_to(slot, (8, LANES))
                part_of = lax.shift_right_logical(slot, rows.bit_length() - 1)
                live = lane + (base + piece * LANES) < live_count
                first = jnp.zeros((8, LANES), jnp.float32)
                second = first
                for part in range(parts):
                    hit = jnp.logical_and(live, part_of == part)
                    first = jnp.where(hit, turned[part * RECORD:part * RECORD + 8], first)
                    second = jnp.where(hit, turned[part * RECORD + 8:part * RECORD + 16], second)
                out_ref[0:8, lanes] = first
                out_ref[8:records, lanes] = second[0:records - 8]
            return carry

        used = lax.div(live_count + (run - 1), run)
        lax.fori_loop(0, used, gather, 0)

        def blank(i, carry):
            lanes = pl.ds(pl.multiple_of(i * run, LANES), run)
            out_ref[:, lanes] = jnp.zeros((records, run), jnp.float32)
            return carry

        lax.fori_loop(used, width // run, blank, 0)


def leave(grains, slots, counts, cells, picks, alive, rows_x, rows_y, depth):
    records, slot_count = grains.shape
    width = slots.shape[1]
    columns = rows_x * rows_y
    rows = max(LANES, 1 << (-(-slot_count // 8) - 1).bit_length())
    run = 2 * LANES if width % (2 * LANES) == 0 else LANES
    out = jax.ShapeDtypeStruct((records, width), jnp.float32)
    bf16 = jnp.bfloat16
    return pl.pallas_call(
        functools.partial(leave_kernel, rows_x, rows_y),
        out_shape=(
            out,
            out,
            jax.ShapeDtypeStruct((2, depth, depth), bf16),
            jax.ShapeDtypeStruct((2, columns, columns + 2 * REACH * rows_y), bf16),
            jax.ShapeDtypeStruct((2, columns, columns + 2 * REACH * rows_x), bf16),
            jax.ShapeDtypeStruct((picks.size, columns), bf16),
            jax.ShapeDtypeStruct(slots.shape, jnp.int32),
            jax.ShapeDtypeStruct(cells.shape, jnp.int32),
        ),
        in_specs=[HBM] * 6,
        out_specs=(VMEM,) * 8,
        scratch_shapes=[
            pltpu.VMEM(grains.shape, jnp.float32),
            pltpu.VMEM((LANES, rows), jnp.float32),
            pltpu.VMEM((rows, LANES), jnp.float32),
            pltpu.VMEM((run, LANES), jnp.float32),
            pltpu.VMEM(slots.shape, jnp.int32),
            pltpu.SMEM(slots.shape, jnp.int32),
            pltpu.SMEM(counts.shape, jnp.int32),
            pltpu.VMEM(picks.shape, jnp.int32),
            pltpu.VMEM(alive.shape, jnp.int32),
            pltpu.SemaphoreType.DMA((7,)),
        ],
        compiler_params=params(16),
        cost_estimate=cost(8),
        name="leave",
    )(*in_hbm(grains, slots, counts, cells, picks, alive))


def weights_at(apart):
    taps = kernel_taps()[REACH:]
    apart = jnp.abs(apart)
    value = jnp.where(apart == 0, taps[0], 0.0)
    for k in range(1, REACH + 1):
        value = jnp.where(apart == k, taps[k], value)
    return value


def put_operator(out_ref, start, value):
    high, low = halves(value)
    stop = start + value.shape[1]
    out_ref[0, :, start:stop] = high
    out_ref[1, :, start:stop] = low


def build_choice(picks_ref, alive_ref, choose_ref):
    rows_q, peers = picks_ref.shape
    slots, columns = choose_ref.shape
    alive = lax.broadcasted_iota(jnp.int32, (rows_q, peers), 0) < alive_ref[...]
    picks = jnp.where(alive, picks_ref[...], -1).astype(jnp.float32).astype(jnp.bfloat16)
    place_e, _ = split(lax.broadcasted_iota(jnp.int32, (slots, peers), 0), rows_q)
    here = place_e == lax.broadcasted_iota(jnp.int32, (slots, peers), 1)
    named = dot(jnp.where(here, 1.0, 0.0).astype(jnp.bfloat16), picks, NT)
    _, place_q = split(lax.broadcasted_iota(jnp.int32, (slots, rows_q), 0), rows_q)
    mine = place_q == lax.broadcasted_iota(jnp.int32, (slots, rows_q), 1)
    named = jnp.sum(jnp.where(mine, named, 0.0), axis=1, keepdims=True)
    hit = named == lax.broadcasted_iota(jnp.int32, (slots, columns), 1).astype(jnp.float32)
    choose_ref[...] = jnp.where(hit, 1.0, 0.0).astype(jnp.bfloat16)


def build_operators(rows_x, rows_y, depth_ref, stream_ref, span_ref):
    columns = rows_x * rows_y
    depth = depth_ref.shape[1]
    target = lax.broadcasted_iota(jnp.int32, (depth, depth), 0)
    source = lax.broadcasted_iota(jnp.int32, (depth, depth), 1)
    put_operator(depth_ref, 0, weights_at(target - source))

    own = (columns, columns)
    target_y, target_x = split(lax.broadcasted_iota(jnp.int32, own, 0), rows_x)
    source_y, source_x = split(lax.broadcasted_iota(jnp.int32, own, 1), rows_x)
    put_operator(stream_ref, 0, jnp.where(target_y == source_y, weights_at(target_x - source_x), 0.0))
    side = (columns, 2 * REACH * rows_y)
    target_y, target_x = split(lax.broadcasted_iota(jnp.int32, side, 0), rows_x)
    plane, source_y = split(lax.broadcasted_iota(jnp.int32, side, 1), rows_y)
    source_x = jnp.where(plane < REACH, plane - REACH, plane - REACH + rows_x)
    put_operator(stream_ref, columns, jnp.where(target_y == source_y, weights_at(target_x - source_x), 0.0))

    target_x, target_y = split(lax.broadcasted_iota(jnp.int32, own, 0), rows_y)
    source_y, source_x = split(lax.broadcasted_iota(jnp.int32, own, 1), rows_x)
    put_operator(span_ref, 0, jnp.where(target_x == source_x, weights_at(target_y - source_y), 0.0))
    side = (columns, 2 * REACH * rows_x)
    target_x, target_y = split(lax.broadcasted_iota(jnp.int32, side, 0), rows_y)
    row, source_x = split(lax.broadcasted_iota(jnp.int32, side, 1), rows_x)
    source_y = jnp.where(row < REACH, row - REACH, row - REACH + rows_y)
    put_operator(span_ref, columns, jnp.where(target_x == source_x, weights_at(target_y - source_y), 0.0))


def keep_kernel(
    rows_x, rows_y, depth, grains_ref, marks_ref, cells_ref, after_hbm, quant_ref,
    high_rows, low_rows, gone, kept, sems,
):
    records, slot_count = grains_ref.shape
    total = quant_ref.shape[1]
    width = marks_ref.shape[1]
    tiles = slot_count // LANES
    pieces = sems.shape[0]

    row16 = lax.broadcasted_iota(jnp.int32, (16, LANES), 0).astype(jnp.float32)
    zero = jnp.zeros((16, LANES), jnp.bfloat16)
    one = jnp.ones((16, LANES), jnp.bfloat16)
    for which in (0, 1):

        def put(i, carry):
            lanes = lane_tile(i)
            to = pl.ds(pl.multiple_of(which * width + i * LANES, LANES), LANES)
            mark = marks_ref[which:which + 1, lanes]
            tile_of, lane_of = split(mark, LANES)
            tile_of = jnp.where(mark < 0, -1, tile_of)
            tile_of = wide(tile_of.astype(jnp.float32))
            lane_of = wide(lane_of.astype(jnp.float32))
            for k in range(high_rows.shape[0] // 16):
                hit = (row16 + 16.0 * k).astype(jnp.bfloat16) == tile_of
                high_rows[16 * k:16 * k + 16, to] = jnp.where(hit, one, zero)
            for k in range(LANES // 16):
                hit = (row16 + 16.0 * k).astype(jnp.bfloat16) == lane_of
                low_rows[16 * k:16 * k + 16, to] = jnp.where(hit, one, zero)
            return carry

        lax.fori_loop(0, width // LANES, put, 0, unroll=8)
    gone[...] = dot(high_rows[...], low_rows[...], NT)

    row8 = lax.broadcasted_iota(jnp.int32, (8, LANES), 0)

    def place(cell):
        x, rest = split(cell, rows_y * depth)
        y, level = split(rest, depth)
        return (y * rows_x + x).astype(jnp.float32), level.astype(jnp.float32)

    def keep(i, carry):
        lanes = lane_tile(i)
        stay = 1.0 - gone[pl.ds(i, 1), :]
        head = grains_ref[0:8, lanes] * stay
        rest = grains_ref[8:records, lanes] * stay
        kept[0:8, lanes] = head
        kept[8:records, lanes] = rest
        radius = rest[1:2]
        volume = 4.18879 * (radius * radius * radius)
        col, lev = place(cells_ref[:, lanes])
        value = jnp.where(row8 == QUANT_ROW[0], volume, volume * head)
        value = jnp.where(row8 == COLUMN_ROW, col, value)
        quant_ref[:, lanes] = jnp.where(row8 == LEVEL_ROW, lev, value)
        return carry

    writes = []
    for n in range(pieces):
        first = tiles * n // pieces
        last = tiles * (n + 1) // pieces
        lax.fori_loop(first, last, keep, 0, unroll=16)
        here = pl.ds(first * LANES, (last - first) * LANES)
        writes.append(pltpu.make_async_copy(kept.at[:, here], after_hbm.at[:, here], sems.at[n]))
        writes[n].start()

    def arrivals(i, carry):
        lanes = lane_tile(i)
        col, lev = place(cells_ref[:, lanes])
        quant_ref[:, lanes] = jnp.where(row8 == COLUMN_ROW, col, lev)
        return carry

    lax.fori_loop(tiles, total // LANES, arrivals, 0, unroll=8)
    for write in writes:
        write.wait()


def keep(grains, marks, cells, rows_x, rows_y, depth):
    records, slot_count = grains.shape
    total = cells.shape[1]
    rows = -(-(slot_count // LANES) // 16) * 16
    f32, bf16 = jnp.float32, jnp.bfloat16
    return pl.pallas_call(
        functools.partial(keep_kernel, rows_x, rows_y, depth),
        out_shape=(jax.ShapeDtypeStruct((records, total), f32), jax.ShapeDtypeStruct((8, total), f32)),
        in_specs=[VMEM] * 3,
        out_specs=(HBM, VMEM),
        scratch_shapes=[
            pltpu.VMEM((rows, 2 * marks.shape[1]), bf16),
            pltpu.VMEM((LANES, 2 * marks.shape[1]), bf16),
            pltpu.VMEM((rows, LANES), f32),
            pltpu.VMEM(grains.shape, f32),
            pltpu.SemaphoreType.DMA((4,)),
        ],
        compiler_params=params(20),
        cost_estimate=cost(4),
        name="keep",
    )(grains, marks, cells)


def join_kernel(after_in, quant_in, first_ref, second_ref, after_ref, quant_ref, sems):
    records, width = first_ref.shape
    start = after_ref.shape[1] - 2 * width
    row8 = lax.broadcasted_iota(jnp.int32, (8, LANES), 0)
    odd = is_odd("stream")
    copies = []
    for n, arrived in enumerate((first_ref, second_ref)):
        place = pl.multiple_of(start + (1 - odd if n == 0 else odd) * width, LANES)
        to = after_ref.at[:, pl.ds(place, width)]
        copies.append(pltpu.make_async_copy(arrived, to, sems.at[n]))
        copies[n].start()
    for n, arrived in enumerate((first_ref, second_ref)):

        def step(i, carry):
            lanes = lane_tile(i)
            place = start + (1 - odd if n == 0 else odd) * width
            to = pl.ds(pl.multiple_of(place + i * LANES, LANES), LANES)
            head = arrived[0:8, lanes]
            radius = arrived[9:10, lanes]
            volume = 4.18879 * (radius * radius * radius)
            value = jnp.where(row8 == QUANT_ROW[0], volume, volume * head)
            quant_ref[:, to] = jnp.where(row8 >= COLUMN_ROW, quant_in[:, to], value)
            return carry

        lax.fori_loop(0, width // LANES, step, 0, unroll=8)
    for copy in copies:
        copy.wait()


def join(after, quant, first, second):
    return pl.pallas_call(
        join_kernel,
        out_shape=(
            jax.ShapeDtypeStruct(after.shape, after.dtype),
            jax.ShapeDtypeStruct(quant.shape, quant.dtype),
        ),
        in_specs=[HBM, VMEM, VMEM, VMEM],
        out_specs=(HBM, VMEM),
        scratch_shapes=[pltpu.SemaphoreType.DMA((2,))],
        input_output_aliases={0: 0, 1: 1},
        compiler_params=params(16),
        cost_estimate=cost(1),
        name="join",
    )(*in_hbm(after), quant, first, second)


def deposit_kernel(channels, rows_x, rows_y, chunk, span, begins, ends, direct, earlier, *refs):
    refs = list(refs)
    quant_ref = refs.pop(0)
    partial_ref = None if begins else refs.pop(0)
    depth_ref = refs.pop(0) if ends else None
    del refs[:earlier]
    field_ref = refs.pop(0)
    first_ref, second_ref = (refs.pop(0), refs.pop(0)) if ends else (None, None)
    total = refs.pop(-1)
    begin, end = span
    columns = rows_x * rows_y
    depth = total.shape[1]
    count = len(channels)
    row16 = lax.broadcasted_iota(jnp.int32, (16, LANES), 0).astype(jnp.float32)
    zero = jnp.zeros((16, LANES), jnp.bfloat16)
    one = jnp.ones((16, LANES), jnp.bfloat16)
    total[...] = jnp.zeros_like(total) if begins else partial_ref[...]

    def build(left, right, step):
        for j in range(chunk // LANES):
            here = slice(j * LANES, (j + 1) * LANES)
            lanes = pl.ds(pl.multiple_of(step * chunk + j * LANES, LANES), LANES)
            parts = [wide(quant_ref[QUANT_ROW[c]:QUANT_ROW[c] + 1, lanes]) for c in channels]
            column = wide(quant_ref[COLUMN_ROW:COLUMN_ROW + 1, lanes])
            level = wide(quant_ref[LEVEL_ROW:LEVEL_ROW + 1, lanes])
            for k in range(columns // 16):
                hit = (row16 + 16.0 * k).astype(jnp.bfloat16) == column
                for c in range(count):
                    left[c * columns + 16 * k:c * columns + 16 * k + 16, here] = jnp.where(hit, parts[c], zero)
            for k in range(depth // 16):
                hit = (row16 + 16.0 * k).astype(jnp.bfloat16) == level
                right[16 * k:16 * k + 16, here] = jnp.where(hit, one, zero)

    def product(start, size):
        lefts = [[] for _ in range(count * columns // 16)]
        rights = [[] for _ in range(depth // 16)]
        for j in range(size // LANES):
            lanes = pl.ds(pl.multiple_of(start + j * LANES, LANES), LANES)
            parts = [wide(quant_ref[QUANT_ROW[c]:QUANT_ROW[c] + 1, lanes]) for c in channels]
            column = wide(quant_ref[COLUMN_ROW:COLUMN_ROW + 1, lanes])
            level = wide(quant_ref[LEVEL_ROW:LEVEL_ROW + 1, lanes])
            for k in range(columns // 16):
                hit = (row16 + 16.0 * k).astype(jnp.bfloat16) == column
                for c in range(count):
                    lefts[c * columns // 16 + k].append(jnp.where(hit, parts[c], zero))
            for k in range(depth // 16):
                hit = (row16 + 16.0 * k).astype(jnp.bfloat16) == level
                rights[k].append(jnp.where(hit, one, zero))
        left = jnp.concatenate([jnp.concatenate(row, axis=1) for row in lefts], axis=0)
        right = jnp.concatenate([jnp.concatenate(row, axis=1) for row in rights], axis=0)
        return dot(left, right, NT)

    if direct:

        def one_step(i, carry):
            total[...] += product(i * direct, direct)
            return carry

        lax.fori_loop(begin * chunk // direct, end * chunk // direct, one_step, 0)
    else:
        left_a, left_b, right_a, right_b = refs
        build(left_a, right_a, begin)

        def two(i, carry):
            now = begin + 2 * i
            build(left_b, right_b, now + 1)
            total[...] += dot(left_a[...], right_a[...], NT)
            build(left_a, right_a, jnp.minimum(now + 2, end - 1))
            total[...] += dot(left_b[...], right_b[...], NT)
            return carry

        lax.fori_loop(0, (end - begin) // 2, two, 0)
        if (end - begin) % 2:
            total[...] += dot(left_a[...], right_a[...], NT)

    if not ends:
        field_ref[...] = total[...]
        return
    high, low = halves(total[...])
    field_ref[...] = dot(high, depth_ref[0]) + (dot(high, depth_ref[1]) + dot(low, depth_ref[0]))
    odd = is_odd("stream")
    first_x = (1 - odd) * (rows_x - REACH)
    second_x = odd * (rows_x - REACH)
    for c in range(count):
        for k in range(REACH):
            for y in range(rows_y):
                to = (c * REACH + k) * rows_y + y
                row = c * columns + y * rows_x + k
                first_ref[to:to + 1, :] = field_ref[pl.ds(row + first_x, 1), :]
                second_ref[to:to + 1, :] = field_ref[pl.ds(row + second_x, 1), :]


def deposit(channels, rows_x, rows_y, depth, chunk, span, direct, quant, partial, depth_op, earlier):
    columns = rows_x * rows_y
    count = len(channels)
    begins, ends = partial is None, depth_op is not None
    field = jax.ShapeDtypeStruct((count * columns, depth), jnp.float32)
    halo = jax.ShapeDtypeStruct((count * REACH * rows_y, depth), jnp.float32)
    operands = [quant] + ([] if begins else [partial]) + ([depth_op] if ends else [])
    outs = (field, halo, halo) if ends else (field,)
    left = pltpu.VMEM((count * columns, chunk), jnp.bfloat16)
    right = pltpu.VMEM((depth, chunk), jnp.bfloat16)
    return pl.pallas_call(
        functools.partial(deposit_kernel, channels, rows_x, rows_y, chunk, span, begins, ends, direct, len(earlier)),
        out_shape=outs,
        in_specs=[VMEM] * len(operands) + [ANY] * len(earlier),
        out_specs=(VMEM,) * len(outs),
        scratch_shapes=([] if direct else [left, left, right, right]) + [pltpu.VMEM(field.shape, jnp.float32)],
        compiler_params=params(20),
        cost_estimate=cost(0.4 * count * (span[1] - span[0])),
        name="deposit",
    )(*operands, *earlier)


def mix(operator_ref, pieces):
    total = None
    start = 0
    for piece in pieces:
        take = slice(start, start + piece.shape[0])
        high, low = halves(piece)
        value = dot(operator_ref[0, :, take], high) + (
            dot(operator_ref[1, :, take], high) + dot(operator_ref[0, :, take], low)
        )
        total = value if total is None else total + value
        start += piece.shape[0]
    return total


def sides(axis, first, second):
    odd = is_odd(axis) == 1
    return jnp.concatenate([jnp.where(odd, first, second), jnp.where(odd, second, first)], axis=0)


def stream_kernel(count, own_ref, first_in, second_in, operator_ref, *refs):
    field_ref, first_ref, second_ref = refs[-3:]
    columns = own_ref.shape[0] // count
    halo = first_in.shape[0] // count
    edge = first_ref.shape[0] // count
    odd = is_odd("span") == 1
    for c in range(count):
        own = slice(c * columns, (c + 1) * columns)
        side = slice(c * halo, (c + 1) * halo)
        value = mix(operator_ref, [own_ref[own, :], sides("stream", first_in[side, :], second_in[side, :])])
        field_ref[own, :] = value
        low, high = value[0:edge], value[columns - edge:columns]
        first_ref[c * edge:(c + 1) * edge, :] = jnp.where(odd, low, high)
        second_ref[c * edge:(c + 1) * edge, :] = jnp.where(odd, high, low)


def stream_pass(count, rows_x, own, first, second, operator, earlier):
    edge = jax.ShapeDtypeStruct((count * REACH * rows_x, own.shape[1]), jnp.float32)
    return pl.pallas_call(
        functools.partial(stream_kernel, count),
        out_shape=(jax.ShapeDtypeStruct(own.shape, jnp.float32), edge, edge),
        in_specs=[VMEM] * 4 + [ANY] * len(earlier),
        out_specs=(VMEM,) * 3,
        compiler_params=params(12),
        cost_estimate=cost(0.4 * count),
        name="stream_pass",
    )(own, first, second, operator, *earlier)


def span_kernel(channels, rows_q, *refs):
    refs = list(refs)
    own_ref, first_in, second_in, operator_ref, choose_ref, fluid_ref = refs[:6]
    base_ref = None if 0 in channels else refs[6]
    solid_ref, out_ref = refs[-2:]
    count = len(channels)
    columns = own_ref.shape[0] // count
    edge = first_in.shape[0] // count
    choose = choose_ref[...]
    solids = {}
    for n, c in enumerate(channels):
        own = slice(n * columns, (n + 1) * columns)
        side = slice(n * edge, (n + 1) * edge)
        value = mix(operator_ref, [own_ref[own, :], sides("span", first_in[side, :], second_in[side, :])])
        solid_ref[own, :] = value
        solids[c] = value
    base = solids[0] if base_ref is None else base_ref[0:columns, :]
    for n, c in enumerate(channels):
        if c == 0:
            value = 1.0 / (1.0 + base)
        else:
            flow = fluid_ref[(c - 1) * columns:c * columns, :]
            value = flow + drag_rate * (solids[c] - base * flow)
        first, rest = halves(value)
        second, third = halves(value - first.astype(jnp.float32))
        sent = dot(choose, first) + (dot(choose, second) + dot(choose, third))
        out_ref[:, :, count - 1 - n, :] = sent.reshape(sent.shape[0] // rows_q, rows_q, -1)


def span_pass(channels, own, first, second, operator, choose, fluid, base, peers, rows_q, earlier):
    count = len(channels)
    operands = [own, first, second, operator, choose, fluid] + ([] if base is None else [base])
    return pl.pallas_call(
        functools.partial(span_kernel, channels, rows_q),
        out_shape=(
            jax.ShapeDtypeStruct(own.shape, jnp.float32),
            jax.ShapeDtypeStruct((peers, rows_q, count, own.shape[1]), jnp.float32),
        ),
        in_specs=[VMEM] * len(operands) + [ANY] * len(earlier),
        out_specs=(VMEM, VMEM),
        compiler_params=params(16),
        cost_estimate=cost(0.8 * count),
        name="span_pass",
    )(*operands, *earlier)


def swap(first, second, axis, periodic):
    count = lax.axis_size(axis)
    assert count % 2 == 0
    pairs = [(source, source ^ 1) for source in range(count)]
    others = [(source, (source + 1 if source % 2 else source - 1) % count) for source in range(count)]
    if not periodic:
        others = [pair for pair in others if abs(pair[0] - pair[1]) == 1]
    return lax.ppermute(first, axis, pairs), lax.ppermute(second, axis, others)


def per_device(grains, send_slots, send_counts, cell_index, fluid, block_slots, block_counts):
    rows_x, rows_y, depth = fluid.shape[1:]
    columns = rows_x * rows_y
    width = send_slots.shape[2]
    peers, rows_q = block_slots.shape[1:]
    total = cell_index.shape[0]
    axes = ("stream", "span")

    first, second, depth_op, stream_op, span_op, choose, marks, cells = leave(
        grains, send_slots[0], send_counts, cell_index.reshape(1, -1), block_slots[0].T, block_counts,
        rows_x, rows_y, depth,
    )
    arrived = swap(first, second, "stream", True)
    after, quant = keep(grains, marks, cells, rows_x, rows_y, depth)
    grains_after, quant = join(after, quant, *arrived)

    chunk = math.gcd(total, 2048)
    steps = total // chunk
    early = steps // 4
    middle = steps * 5 // 7
    flow = fluid.reshape(3 * columns, depth)

    def add(channels, span, direct, partial, last, earlier=()):
        return deposit(
            channels, rows_x, rows_y, depth, chunk, span, direct, quant, partial, depth_op if last else None, earlier
        )

    def stream(field, first, second, earlier):
        halos = swap(first, second, "stream", True)
        return stream_pass(field.shape[0] // columns, rows_x, field, *halos, stream_op, earlier)

    def span(channels, field, first, second, base, earlier):
        halos = swap(first, second, "span", False)
        return span_pass(channels, field, *halos, span_op, choose, flow, base, peers, rows_q, earlier)

    def exchange(outgoing):
        return lax.all_to_all(outgoing, axes, split_axis=0, concat_axis=0, tiled=True)

    direct = chunk // 2
    outer = add((0, 3), (0, steps), 0, None, True)
    (inner,) = add((2, 1), (0, early), direct, None, False)
    outer = stream(*outer, (inner,))
    (inner,) = add((2, 1), (early, middle), direct, inner, False, outer[:1])
    solid_outer, outgoing = span((0, 3), *outer, None, (inner,))
    arrived_outer = exchange(outgoing)
    inner = add((2, 1), (middle, steps), direct, inner, True, (outgoing,))
    inner = stream(*inner, ())
    solid_inner, outgoing = span((2, 1), *inner, solid_outer, ())
    arrived_inner = exchange(outgoing)

    solid = jnp.concatenate(
        [solid_outer[:columns], solid_inner[columns:], solid_inner[:columns], solid_outer[columns:]], axis=0
    ).reshape(4, rows_x, rows_y, depth)
    received = jnp.concatenate([arrived_inner, arrived_outer], axis=2)
    return grains_after, solid, received[None]


def solution(mesh):
    return jax.shard_map(
        per_device,
        mesh=mesh,
        in_specs=(
            P(None, ("stream", "span")),
            P(("stream", "span"), None, None),
            P(("stream", "span"), None),
            P(("stream", "span")),
            P(None, "stream", "span", None),
            P(("stream", "span"), None, None),
            P(("stream", "span"), None),
        ),
        out_specs=(
            P(None, ("stream", "span")),
            P(None, "stream", "span", None),
            P(("stream", "span"), None, None, None, None),
        ),
        check_vma=False,
    )
```

```python
import functools
import math

import jax
import jax.numpy as jnp
from jax import lax
from jax.experimental import pallas as pl
from jax.experimental.pallas import tpu as pltpu
from jax.sharding import PartitionSpec as P

REACH = 3
LANES = 128
RECORD = 16

spread_cells = 1.5
drag_rate = 0.25

VMEM = pl.BlockSpec(memory_space=pltpu.VMEM)
HBM = pl.BlockSpec(memory_space=pltpu.HBM)
NT = (((1,), (1,)), ((), ()))
NN = (((1,), (0,)), ((), ()))

QUANT_ROW = (0, 3, 4, 5)
COLUMN_ROW = 6
LEVEL_ROW = 7


def kernel_taps():
    raw = [
        math.exp(-(k * k) / (2.0 * spread_cells * spread_cells)) for k in range(-REACH, REACH + 1)
    ]
    total = sum(raw)
    return [value / total for value in raw]


def params(mib):
    return pltpu.CompilerParams(vmem_limit_bytes=mib * 2**20)


def cost(micros):
    return pl.CostEstimate(flops=0, bytes_accessed=int(micros * 3.0e6), transcendentals=0)


def split(values, size):
    if size & (size - 1):
        return lax.div(values, size), lax.rem(values, size)
    return lax.shift_right_logical(values, size.bit_length() - 1), lax.bitwise_and(values, size - 1)


def halves(values):
    high = values.astype(jnp.bfloat16)
    return high, (values - high.astype(jnp.float32)).astype(jnp.bfloat16)


def dot(left, right, dims=NN):
    return lax.dot_general(left, right, dims, preferred_element_type=jnp.float32)


def wide(values):
    return jnp.broadcast_to(values, (16, LANES)).astype(jnp.bfloat16)


def lane_tile(i):
    return pl.ds(pl.multiple_of(i * LANES, LANES), LANES)


def in_hbm(*values):
    return tuple(pltpu.with_memory_space_constraint(value, pltpu.HBM) for value in values)


def is_odd(axis):
    return lax.rem(lax.axis_index(axis), 2)


def leave_kernel(
    rows_x, rows_y, grains_hbm, slots_hbm, counts_hbm, cells_hbm, picks_hbm, alive_hbm,
    first_ref, second_ref, depth_ref, stream_ref, span_ref, choose_ref, marks_ref, cells_ref,
    grains_ref, stage, table, picked, slots_v, slots_s, counts_s, picks_v, alive_v, sems,
):
    records, slot_count = grains_ref.shape
    width = first_ref.shape[1]
    rows = table.shape[0]
    parts = -(-slot_count // rows)
    sources = (grains_hbm, slots_hbm, slots_hbm, counts_hbm, picks_hbm, alive_hbm, cells_hbm)
    targets = (grains_ref, slots_v, slots_s, counts_s, picks_v, alive_v, cells_ref)
    copies = [
        pltpu.make_async_copy(source, target, sems.at[i])
        for i, (source, target) in enumerate(zip(sources, targets))
    ]
    for copy in copies:
        copy.start()
    build_operators(rows_x, rows_y, depth_ref, stream_ref, span_ref)
    copies[0].wait()

    for part in range(parts):
        size = min(rows, slot_count - part * rows)
        here = slice(part * rows, part * rows + size)
        stage[part * RECORD:part * RECORD + 8, 0:size] = grains_ref[0:8, here]
        stage[part * RECORD + 8:part * RECORD + records, 0:size] = grains_ref[8:records, here]
    for block in range(rows // LANES):
        here = slice(block * LANES, (block + 1) * LANES)
        table[here, :] = jnp.transpose(stage[:, here])
    for copy in copies[1:]:
        copy.wait()
    build_choice(picks_v, alive_v, choose_ref)
    for which in (0, 1):
        live = lax.broadcasted_iota(jnp.int32, (1, width), 1) < counts_s[0, which]
        marks_ref[which:which + 1, :] = jnp.where(live, slots_v[which:which + 1, :], -1)

    run = picked.shape[0]
    lane = lax.broadcasted_iota(jnp.int32, (8, LANES), 1)
    odd = is_odd("stream")
    for which, out_ref in ((odd, first_ref), (1 - odd, second_ref)):
        live_count = counts_s[0, which]

        def gather(i, carry):
            base = i * run
            for k in range(run):
                row = lax.bitwise_and(slots_s[which, base + k], rows - 1)
                picked[k:k + 1, :] = table[pl.ds(row, 1), :]
            for piece in range(run // LANES):
                lanes = pl.ds(pl.multiple_of(base + piece * LANES, LANES), LANES)
                turned = jnp.transpose(picked[piece * LANES:(piece + 1) * LANES, :])
                slot = jnp.where(which == 0, slots_v[0:1, lanes], slots_v[1:2, lanes])
                slot = jnp.broadcast_to(slot, (8, LANES))
                part_of = lax.shift_right_logical(slot, rows.bit_length() - 1)
                live = lane + (base + piece * LANES) < live_count
                first = jnp.zeros((8, LANES), jnp.float32)
                second = first
                for part in range(parts):
                    hit = jnp.logical_and(live, part_of == part)
                    first = jnp.where(hit, turned[part * RECORD:part * RECORD + 8], first)
                    second = jnp.where(hit, turned[part * RECORD + 8:part * RECORD + 16], second)
                out_ref[0:8, lanes] = first
                out_ref[8:records, lanes] = second[0:records - 8]
            return carry

        used = lax.div(live_count + (run - 1), run)
        lax.fori_loop(0, used, gather, 0)

        def blank(i, carry):
            lanes = pl.ds(pl.multiple_of(i * run, LANES), run)
            out_ref[:, lanes] = jnp.zeros((records, run), jnp.float32)
            return carry

        lax.fori_loop(used, width // run, blank, 0)


def leave(grains, slots, counts, cells, picks, alive, rows_x, rows_y, depth):
    records, slot_count = grains.shape
    width = slots.shape[1]
    columns = rows_x * rows_y
    rows = max(LANES, 1 << (-(-slot_count // 8) - 1).bit_length())
    run = 4 * LANES if width % (4 * LANES) == 0 else LANES
    out = jax.ShapeDtypeStruct((records, width), jnp.float32)
    bf16 = jnp.bfloat16
    return pl.pallas_call(
        functools.partial(leave_kernel, rows_x, rows_y),
        out_shape=(
            out,
            out,
            jax.ShapeDtypeStruct((2, depth, depth), bf16),
            jax.ShapeDtypeStruct((2, columns, columns + 2 * REACH * rows_y), bf16),
            jax.ShapeDtypeStruct((2, columns, columns + 2 * REACH * rows_x), bf16),
            jax.ShapeDtypeStruct((picks.size, columns), bf16),
            jax.ShapeDtypeStruct(slots.shape, jnp.int32),
            jax.ShapeDtypeStruct(cells.shape, jnp.int32),
        ),
        in_specs=[HBM] * 6,
        out_specs=(VMEM,) * 8,
        scratch_shapes=[
            pltpu.VMEM(grains.shape, jnp.float32),
            pltpu.VMEM((LANES, rows), jnp.float32),
            pltpu.VMEM((rows, LANES), jnp.float32),
            pltpu.VMEM((run, LANES), jnp.float32),
            pltpu.VMEM(slots.shape, jnp.int32),
            pltpu.SMEM(slots.shape, jnp.int32),
            pltpu.SMEM(counts.shape, jnp.int32),
            pltpu.VMEM(picks.shape, jnp.int32),
            pltpu.VMEM(alive.shape, jnp.int32),
            pltpu.SemaphoreType.DMA((7,)),
        ],
        compiler_params=params(16),
        cost_estimate=cost(8),
        name="leave",
    )(*in_hbm(grains, slots, counts, cells, picks, alive))


def weights_at(apart):
    taps = kernel_taps()[REACH:]
    apart = jnp.abs(apart)
    value = jnp.where(apart == 0, taps[0], 0.0)
    for k in range(1, REACH + 1):
        value = jnp.where(apart == k, taps[k], value)
    return value


def put_operator(out_ref, start, value):
    high, low = halves(value)
    stop = start + value.shape[1]
    out_ref[0, :, start:stop] = high
    out_ref[1, :, start:stop] = low


def build_choice(picks_ref, alive_ref, choose_ref):
    rows_q, peers = picks_ref.shape
    slots, columns = choose_ref.shape
    alive = lax.broadcasted_iota(jnp.int32, (rows_q, peers), 0) < alive_ref[...]
    picks = jnp.where(alive, picks_ref[...], -1).astype(jnp.float32).astype(jnp.bfloat16)
    place_e, _ = split(lax.broadcasted_iota(jnp.int32, (slots, peers), 0), rows_q)
    here = place_e == lax.broadcasted_iota(jnp.int32, (slots, peers), 1)
    named = dot(jnp.where(here, 1.0, 0.0).astype(jnp.bfloat16), picks, NT)
    _, place_q = split(lax.broadcasted_iota(jnp.int32, (slots, rows_q), 0), rows_q)
    mine = place_q == lax.broadcasted_iota(jnp.int32, (slots, rows_q), 1)
    named = jnp.sum(jnp.where(mine, named, 0.0), axis=1, keepdims=True)
    hit = named == lax.broadcasted_iota(jnp.int32, (slots, columns), 1).astype(jnp.float32)
    choose_ref[...] = jnp.where(hit, 1.0, 0.0).astype(jnp.bfloat16)


def build_operators(rows_x, rows_y, depth_ref, stream_ref, span_ref):
    columns = rows_x * rows_y
    depth = depth_ref.shape[1]
    target = lax.broadcasted_iota(jnp.int32, (depth, depth), 0)
    source = lax.broadcasted_iota(jnp.int32, (depth, depth), 1)
    put_operator(depth_ref, 0, weights_at(target - source))

    own = (columns, columns)
    target_y, target_x = split(lax.broadcasted_iota(jnp.int32, own, 0), rows_x)
    row, source_x = split(lax.broadcasted_iota(jnp.int32, own, 1), rows_x)
    source_y = jnp.where(row < REACH, row, jnp.where(row < 2 * REACH, row + rows_y - 2 * REACH, row - REACH))
    put_operator(span_ref, 0, jnp.where(target_x == source_x, weights_at(target_y - source_y), 0.0))
    side = (columns, 2 * REACH * rows_x)
    target_y, target_x = split(lax.broadcasted_iota(jnp.int32, side, 0), rows_x)
    row, source_x = split(lax.broadcasted_iota(jnp.int32, side, 1), rows_x)
    source_y = jnp.where(row < REACH, row - REACH, row - REACH + rows_y)
    put_operator(span_ref, columns, jnp.where(target_x == source_x, weights_at(target_y - source_y), 0.0))

    target_x, target_y = split(lax.broadcasted_iota(jnp.int32, own, 0), rows_y)
    source_y, source_x = split(lax.broadcasted_iota(jnp.int32, own, 1), rows_x)
    put_operator(stream_ref, 0, jnp.where(target_y == source_y, weights_at(target_x - source_x), 0.0))
    side = (columns, 2 * REACH * rows_y)
    target_x, target_y = split(lax.broadcasted_iota(jnp.int32, side, 0), rows_y)
    plane, source_y = split(lax.broadcasted_iota(jnp.int32, side, 1), rows_y)
    source_x = jnp.where(plane < REACH, plane - REACH, plane - REACH + rows_x)
    put_operator(stream_ref, columns, jnp.where(target_y == source_y, weights_at(target_x - source_x), 0.0))


def row_of(y, rows_y):
    return jnp.where(y < REACH, y, jnp.where(y < rows_y - REACH, y + REACH, y - (rows_y - 2 * REACH)))


def keep_kernel(
    rows_x, rows_y, depth, grains_ref, marks_ref, cells_ref, after_hbm, quant_ref,
    high_rows, low_rows, gone, kept, sems,
):
    records, slot_count = grains_ref.shape
    total = quant_ref.shape[1]
    width = marks_ref.shape[1]
    tiles = slot_count // LANES
    pieces = sems.shape[0]

    row16 = lax.broadcasted_iota(jnp.int32, (16, LANES), 0).astype(jnp.float32)
    zero = jnp.zeros((16, LANES), jnp.bfloat16)
    one = jnp.ones((16, LANES), jnp.bfloat16)
    for which in (0, 1):

        def put(i, carry):
            lanes = lane_tile(i)
            to = pl.ds(pl.multiple_of(which * width + i * LANES, LANES), LANES)
            mark = marks_ref[which:which + 1, lanes]
            tile_of, lane_of = split(mark, LANES)
            tile_of = jnp.where(mark < 0, -1, tile_of)
            tile_of = wide(tile_of.astype(jnp.float32))
            lane_of = wide(lane_of.astype(jnp.float32))
            for k in range(high_rows.shape[0] // 16):
                hit = (row16 + 16.0 * k).astype(jnp.bfloat16) == tile_of
                high_rows[16 * k:16 * k + 16, to] = jnp.where(hit, one, zero)
            for k in range(LANES // 16):
                hit = (row16 + 16.0 * k).astype(jnp.bfloat16) == lane_of
                low_rows[16 * k:16 * k + 16, to] = jnp.where(hit, one, zero)
            return carry

        lax.fori_loop(0, width // LANES, put, 0, unroll=8)
    gone[...] = dot(high_rows[...], low_rows[...], NT)

    row8 = lax.broadcasted_iota(jnp.int32, (8, LANES), 0)

    def place(cell):
        x, rest = split(cell, rows_y * depth)
        y, level = split(rest, depth)
        return (row_of(y, rows_y) * rows_x + x).astype(jnp.float32), level.astype(jnp.float32)

    def keep(i, carry):
        lanes = lane_tile(i)
        stay = 1.0 - gone[pl.ds(i, 1), :]
        head = grains_ref[0:8, lanes] * stay
        rest = grains_ref[8:records, lanes] * stay
        kept[0:8, lanes] = head
        kept[8:records, lanes] = rest
        radius = rest[1:2]
        volume = 4.18879 * (radius * radius * radius)
        col, lev = place(cells_ref[:, lanes])
        value = jnp.where(row8 == QUANT_ROW[0], volume, volume * head)
        value = jnp.where(row8 == COLUMN_ROW, col, value)
        quant_ref[:, lanes] = jnp.where(row8 == LEVEL_ROW, lev, value)
        return carry

    writes = []
    for n in range(pieces):
        first = tiles * n // pieces
        last = tiles * (n + 1) // pieces
        lax.fori_loop(first, last, keep, 0, unroll=16)
        here = pl.ds(first * LANES, (last - first) * LANES)
        writes.append(pltpu.make_async_copy(kept.at[:, here], after_hbm.at[:, here], sems.at[n]))
        writes[n].start()

    def arrivals(i, carry):
        lanes = lane_tile(i)
        col, lev = place(cells_ref[:, lanes])
        quant_ref[:, lanes] = jnp.where(row8 == COLUMN_ROW, col, lev)
        return carry

    lax.fori_loop(tiles, total // LANES, arrivals, 0, unroll=8)
    for write in writes:
        write.wait()


def keep(grains, marks, cells, rows_x, rows_y, depth):
    records, slot_count = grains.shape
    total = cells.shape[1]
    rows = -(-(slot_count // LANES) // 16) * 16
    f32, bf16 = jnp.float32, jnp.bfloat16
    return pl.pallas_call(
        functools.partial(keep_kernel, rows_x, rows_y, depth),
        out_shape=(jax.ShapeDtypeStruct((records, total), f32), jax.ShapeDtypeStruct((8, total), f32)),
        in_specs=[VMEM] * 3,
        out_specs=(HBM, VMEM),
        scratch_shapes=[
            pltpu.VMEM((rows, 2 * marks.shape[1]), bf16),
            pltpu.VMEM((LANES, 2 * marks.shape[1]), bf16),
            pltpu.VMEM((rows, LANES), f32),
            pltpu.VMEM(grains.shape, f32),
            pltpu.SemaphoreType.DMA((4,)),
        ],
        compiler_params=params(20),
        cost_estimate=cost(4),
        name="keep",
    )(grains, marks, cells)


def join_kernel(after_in, quant_in, first_ref, second_ref, after_ref, quant_ref, sems):
    records, width = first_ref.shape
    start = after_ref.shape[1] - 2 * width
    row8 = lax.broadcasted_iota(jnp.int32, (8, LANES), 0)
    odd = is_odd("stream")
    copies = []
    for n, arrived in enumerate((first_ref, second_ref)):
        place = pl.multiple_of(start + (1 - odd if n == 0 else odd) * width, LANES)
        to = after_ref.at[:, pl.ds(place, width)]
        copies.append(pltpu.make_async_copy(arrived, to, sems.at[n]))
        copies[n].start()
    for n, arrived in enumerate((first_ref, second_ref)):

        def step(i, carry):
            lanes = lane_tile(i)
            place = start + (1 - odd if n == 0 else odd) * width
            to = pl.ds(pl.multiple_of(place + i * LANES, LANES), LANES)
            head = arrived[0:8, lanes]
            radius = arrived[9:10, lanes]
            volume = 4.18879 * (radius * radius * radius)
            value = jnp.where(row8 == QUANT_ROW[0], volume, volume * head)
            quant_ref[:, to] = jnp.where(row8 >= COLUMN_ROW, quant_in[:, to], value)
            return carry

        lax.fori_loop(0, width // LANES, step, 0, unroll=8)
    for copy in copies:
        copy.wait()


def join(after, quant, first, second):
    return pl.pallas_call(
        join_kernel,
        out_shape=(
            jax.ShapeDtypeStruct(after.shape, after.dtype),
            jax.ShapeDtypeStruct(quant.shape, quant.dtype),
        ),
        in_specs=[HBM, VMEM, VMEM, VMEM],
        out_specs=(HBM, VMEM),
        scratch_shapes=[pltpu.SemaphoreType.DMA((2,))],
        input_output_aliases={0: 0, 1: 1},
        compiler_params=params(16),
        cost_estimate=cost(1),
        name="join",
    )(*in_hbm(after), quant, first, second)


def deposit_kernel(base, chunk, edges, quant_ref, depth_ref, *refs):
    field_ref = refs[0]
    left_a, left_b, right_a, right_b, total = refs[-5:]
    channels = len(QUANT_ROW)
    columns = field_ref.shape[0] // channels
    depth = depth_ref.shape[1]
    steps = quant_ref.shape[1] // chunk
    row16 = lax.broadcasted_iota(jnp.int32, (16, LANES), 0).astype(jnp.float32)
    zero = jnp.zeros((16, LANES), jnp.bfloat16)
    one = jnp.ones((16, LANES), jnp.bfloat16)
    total[...] = jnp.zeros_like(total)

    def build(left, right, step):
        for j in range(chunk // LANES):
            here = slice(j * LANES, (j + 1) * LANES)
            lanes = pl.ds(pl.multiple_of(step * chunk + j * LANES, LANES), LANES)
            parts = [wide(quant_ref[r:r + 1, lanes]) for r in QUANT_ROW]
            column = wide(quant_ref[COLUMN_ROW:COLUMN_ROW + 1, lanes])
            level = wide(quant_ref[LEVEL_ROW:LEVEL_ROW + 1, lanes])
            for k in range(columns // 16):
                hit = (row16 + (base + 16.0 * k)).astype(jnp.bfloat16) == column
                for c in range(channels):
                    left[c * columns + 16 * k:c * columns + 16 * k + 16, here] = jnp.where(hit, parts[c], zero)
            for k in range(depth // 16):
                hit = (row16 + 16.0 * k).astype(jnp.bfloat16) == level
                right[16 * k:16 * k + 16, here] = jnp.where(hit, one, zero)

    build(left_a, right_a, 0)

    def two(i, carry):
        now = 2 * i
        build(left_b, right_b, now + 1)
        total[...] += dot(left_a[...], right_a[...], NT)
        build(left_a, right_a, jnp.minimum(now + 2, steps - 1))
        total[...] += dot(left_b[...], right_b[...], NT)
        return carry

    lax.fori_loop(0, steps // 2, two, 0)
    if steps % 2:
        total[...] += dot(left_a[...], right_a[...], NT)

    high, low = halves(total[...])
    field_ref[...] = dot(high, depth_ref[0]) + (dot(high, depth_ref[1]) + dot(low, depth_ref[0]))
    if edges:
        first_ref, second_ref = refs[1:3]
        edge = columns // 2
        odd = is_odd("span")
        for c in range(channels):
            to = slice(c * edge, (c + 1) * edge)
            front = c * columns + (1 - odd) * edge
            back = c * columns + odd * edge
            first_ref[to, :] = field_ref[pl.ds(pl.multiple_of(front, 8), edge), :]
            second_ref[to, :] = field_ref[pl.ds(pl.multiple_of(back, 8), edge), :]


def deposit(base, columns, chunk, edges, quant, depth_op):
    depth = depth_op.shape[1]
    channels = len(QUANT_ROW)
    field = jax.ShapeDtypeStruct((channels * columns, depth), jnp.float32)
    edge = jax.ShapeDtypeStruct((channels * columns // 2, depth), jnp.float32)
    outs = (field, edge, edge) if edges else (field,)
    left = pltpu.VMEM((channels * columns, chunk), jnp.bfloat16)
    right = pltpu.VMEM((depth, chunk), jnp.bfloat16)
    return pl.pallas_call(
        functools.partial(deposit_kernel, base, chunk, edges),
        out_shape=outs,
        in_specs=[VMEM, VMEM],
        out_specs=(VMEM,) * len(outs),
        scratch_shapes=[left, left, right, right, pltpu.VMEM(field.shape, jnp.float32)],
        compiler_params=params(20),
        cost_estimate=cost(columns * 0.09),
        name="deposit",
    )(quant, depth_op)


def mix(operator_ref, pieces):
    total = None
    start = 0
    for piece in pieces:
        take = slice(start, start + piece.shape[0])
        high, low = halves(piece)
        value = dot(operator_ref[0, :, take], high) + (
            dot(operator_ref[1, :, take], high) + dot(operator_ref[0, :, take], low)
        )
        total = value if total is None else total + value
        start += piece.shape[0]
    return total


def sides(axis, first, second):
    odd = is_odd(axis) == 1
    return jnp.concatenate([jnp.where(odd, first, second), jnp.where(odd, second, first)], axis=0)


def span_kernel(rows_x, rows_y, edge_ref, inner_ref, first_in, second_in, operator_ref, field_ref, first_ref, second_ref):
    channels = len(QUANT_ROW)
    columns = rows_x * rows_y
    outer = edge_ref.shape[0] // channels
    inner = inner_ref.shape[0] // channels
    halo = first_in.shape[0] // channels
    odd = is_odd("stream")
    first_x = (1 - odd) * (rows_x - REACH)
    second_x = odd * (rows_x - REACH)
    for c in range(channels):
        own = [edge_ref[c * outer:(c + 1) * outer, :], inner_ref[c * inner:(c + 1) * inner, :]]
        side = slice(c * halo, (c + 1) * halo)
        own = jnp.concatenate(own, axis=0)
        value = mix(operator_ref, [own, sides("span", first_in[side, :], second_in[side, :])])
        field_ref[c * columns:(c + 1) * columns, :] = value
    for c in range(channels):
        for k in range(REACH):
            for y in range(rows_y):
                to = (c * REACH + k) * rows_y + y
                row = c * columns + y * rows_x + k
                first_ref[to:to + 1, :] = field_ref[pl.ds(row + first_x, 1), :]
                second_ref[to:to + 1, :] = field_ref[pl.ds(row + second_x, 1), :]


def span_pass(rows_x, rows_y, edge, inner, first, second, operator):
    channels = len(QUANT_ROW)
    depth = edge.shape[1]
    halo = jax.ShapeDtypeStruct((channels * REACH * rows_y, depth), jnp.float32)
    return pl.pallas_call(
        functools.partial(span_kernel, rows_x, rows_y),
        out_shape=(jax.ShapeDtypeStruct((channels * rows_x * rows_y, depth), jnp.float32), halo, halo),
        in_specs=[VMEM] * 5,
        out_specs=(VMEM,) * 3,
        compiler_params=params(12),
        cost_estimate=cost(1.5),
        name="span_pass",
    )(edge, inner, first, second, operator)


def stream_kernel(rows_q, own_ref, first_in, second_in, operator_ref, choose_ref, fluid_ref, solid_ref, out_ref):
    channels = len(QUANT_ROW)
    columns = own_ref.shape[0] // channels
    halo = first_in.shape[0] // channels
    choose = choose_ref[...]
    base = None
    for c in range(channels):
        own = slice(c * columns, (c + 1) * columns)
        side = slice(c * halo, (c + 1) * halo)
        solid = mix(operator_ref, [own_ref[own, :], sides("stream", first_in[side, :], second_in[side, :])])
        solid_ref[own, :] = solid
        if c == 0:
            base = solid
            value = 1.0 / (1.0 + base)
        else:
            flow = fluid_ref[(c - 1) * columns:c * columns, :]
            value = flow + drag_rate * (solid - base * flow)
        first, rest = halves(value)
        second, third = halves(value - first.astype(jnp.float32))
        sent = dot(choose, first) + (dot(choose, second) + dot(choose, third))
        place = (c - 1) % channels
        out_ref[:, :, place, :] = sent.reshape(sent.shape[0] // rows_q, rows_q, -1)


def stream_pass(peers, rows_q, own, first, second, operator, choose, fluid):
    channels = len(QUANT_ROW)
    depth = own.shape[1]
    return pl.pallas_call(
        functools.partial(stream_kernel, rows_q),
        out_shape=(
            jax.ShapeDtypeStruct(own.shape, jnp.float32),
            jax.ShapeDtypeStruct((peers, rows_q, channels, depth), jnp.float32),
        ),
        in_specs=[VMEM] * 6,
        out_specs=(VMEM, VMEM),
        compiler_params=params(16),
        cost_estimate=cost(3.5),
        name="stream_pass",
    )(own, first, second, operator, choose, fluid)


def swap(first, second, axis, periodic):
    count = lax.axis_size(axis)
    assert count % 2 == 0
    pairs = [(source, source ^ 1) for source in range(count)]
    others = [(source, (source + 1 if source % 2 else source - 1) % count) for source in range(count)]
    if not periodic:
        others = [pair for pair in others if abs(pair[0] - pair[1]) == 1]
    second = lax.ppermute(second, axis, others)
    return lax.ppermute(first, axis, pairs), second


def per_device(grains, send_slots, send_counts, cell_index, fluid, block_slots, block_counts):
    rows_x, rows_y, depth = fluid.shape[1:]
    columns = rows_x * rows_y
    width = send_slots.shape[2]
    peers, rows_q = block_slots.shape[1:]
    total = cell_index.shape[0]
    axes = ("stream", "span")

    first, second, depth_op, stream_op, span_op, choose, marks, cells = leave(
        grains, send_slots[0], send_counts, cell_index.reshape(1, -1), block_slots[0].T, block_counts,
        rows_x, rows_y, depth,
    )
    arrived = swap(first, second, "stream", True)
    after, quant = keep(grains, marks, cells, rows_x, rows_y, depth)
    grains_after, quant = join(after, quant, *arrived)

    chunk = math.gcd(total, 2048)
    faces = 2 * REACH * rows_x
    edge, first, second = deposit(0, faces, chunk, True, quant, depth_op)
    first, second = swap(first, second, "span", False)
    (inner,) = deposit(faces, columns - faces, chunk, False, quant, depth_op)
    field, *halos = span_pass(rows_x, rows_y, edge, inner, first, second, span_op)
    halos = swap(*halos, "stream", True)
    solid, outgoing = stream_pass(
        peers, rows_q, field, *halos, stream_op, choose, fluid.reshape(3 * columns, depth)
    )
    arrived = lax.all_to_all(outgoing, axes, split_axis=0, concat_axis=0, tiled=True)
    return grains_after, solid.reshape(4, rows_x, rows_y, depth), arrived[None]


def solution(mesh):
    return jax.shard_map(
        per_device,
        mesh=mesh,
        in_specs=(
            P(None, ("stream", "span")),
            P(("stream", "span"), None, None),
            P(("stream", "span"), None),
            P(("stream", "span")),
            P(None, "stream", "span", None),
            P(("stream", "span"), None, None),
            P(("stream", "span"), None),
        ),
        out_specs=(
            P(None, ("stream", "span")),
            P(None, "stream", "span", None),
            P(("stream", "span"), None, None, None, None),
        ),
        check_vma=False,
    )
```

```python
import functools
import math

import jax
import jax.numpy as jnp
from jax import lax
from jax.experimental import pallas as pl
from jax.experimental.pallas import tpu as pltpu
from jax.sharding import PartitionSpec as P

REACH = 3
LANES = 128
RECORD = 16

spread_cells = 1.5
drag_rate = 0.25

VMEM = pl.BlockSpec(memory_space=pltpu.VMEM)
HBM = pl.BlockSpec(memory_space=pltpu.HBM)
NT = (((1,), (1,)), ((), ()))
NN = (((1,), (0,)), ((), ()))

QUANT_ROW = (0, 3, 4, 5)
COLUMN_ROW = 6
LEVEL_ROW = 7


def kernel_taps():
    raw = [
        math.exp(-(k * k) / (2.0 * spread_cells * spread_cells)) for k in range(-REACH, REACH + 1)
    ]
    total = sum(raw)
    return [value / total for value in raw]


def params(mib):
    return pltpu.CompilerParams(vmem_limit_bytes=mib * 2**20)


def cost(micros):
    return pl.CostEstimate(flops=0, bytes_accessed=int(micros * 3.0e6), transcendentals=0)


def split(values, size):
    if size & (size - 1):
        return lax.div(values, size), lax.rem(values, size)
    return lax.shift_right_logical(values, size.bit_length() - 1), lax.bitwise_and(values, size - 1)


def halves(values):
    high = values.astype(jnp.bfloat16)
    return high, (values - high.astype(jnp.float32)).astype(jnp.bfloat16)


def dot(left, right, dims=NN):
    return lax.dot_general(left, right, dims, preferred_element_type=jnp.float32)


def wide(values):
    return jnp.broadcast_to(values, (16, LANES)).astype(jnp.bfloat16)


def lane_tile(i):
    return pl.ds(pl.multiple_of(i * LANES, LANES), LANES)


def in_hbm(*values):
    return tuple(pltpu.with_memory_space_constraint(value, pltpu.HBM) for value in values)


def is_odd(axis):
    return lax.rem(lax.axis_index(axis), 2)


def leave_kernel(
    rows_x, rows_y, grains_hbm, slots_hbm, counts_hbm, cells_hbm, picks_hbm, alive_hbm,
    first_ref, second_ref, depth_ref, stream_ref, span_ref, choose_ref, marks_ref, cells_ref,
    grains_ref, stage, table, picked, slots_v, slots_s, counts_s, picks_v, alive_v, sems,
):
    records, slot_count = grains_ref.shape
    width = first_ref.shape[1]
    rows = table.shape[0]
    parts = -(-slot_count // rows)
    sources = (grains_hbm, slots_hbm, slots_hbm, counts_hbm, picks_hbm, alive_hbm, cells_hbm)
    targets = (grains_ref, slots_v, slots_s, counts_s, picks_v, alive_v, cells_ref)
    copies = [
        pltpu.make_async_copy(source, target, sems.at[i])
        for i, (source, target) in enumerate(zip(sources, targets))
    ]
    for copy in copies:
        copy.start()
    build_operators(rows_x, rows_y, depth_ref, stream_ref, span_ref)
    copies[0].wait()

    for part in range(parts):
        size = min(rows, slot_count - part * rows)
        here = slice(part * rows, part * rows + size)
        stage[part * RECORD:part * RECORD + 8, 0:size] = grains_ref[0:8, here]
        stage[part * RECORD + 8:part * RECORD + records, 0:size] = grains_ref[8:records, here]
    for block in range(rows // LANES):
        here = slice(block * LANES, (block + 1) * LANES)
        table[here, :] = jnp.transpose(stage[:, here])
    for copy in copies[1:]:
        copy.wait()
    build_choice(picks_v, alive_v, choose_ref)
    for which in (0, 1):
        live = lax.broadcasted_iota(jnp.int32, (1, width), 1) < counts_s[0, which]
        marks_ref[which:which + 1, :] = jnp.where(live, slots_v[which:which + 1, :], -1)

    run = picked.shape[0]
    lane = lax.broadcasted_iota(jnp.int32, (8, LANES), 1)
    odd = is_odd("stream")
    for which in (0, 1):
        live_count = counts_s[0, which]

        def put(lanes, rows_to, value):
            @pl.when(odd == which)
            def _():
                first_ref[rows_to, lanes] = value

            @pl.when(odd != which)
            def _():
                second_ref[rows_to, lanes] = value

        def gather(i, carry):
            base = i * run
            for k in range(run):
                row = lax.bitwise_and(slots_s[which, base + k], rows - 1)
                picked[k:k + 1, :] = table[pl.ds(row, 1), :]
            heads, rests = [], []
            for piece in range(run // LANES):
                lanes = pl.ds(pl.multiple_of(base + piece * LANES, LANES), LANES)
                turned = jnp.transpose(picked[piece * LANES:(piece + 1) * LANES, :])
                slot = jnp.broadcast_to(slots_v[which:which + 1, lanes], (8, LANES))
                part_of = lax.shift_right_logical(slot, rows.bit_length() - 1)
                live = lane + (base + piece * LANES) < live_count
                first = jnp.zeros((8, LANES), jnp.float32)
                second = first
                for part in range(parts):
                    hit = jnp.logical_and(live, part_of == part)
                    first = jnp.where(hit, turned[part * RECORD:part * RECORD + 8], first)
                    second = jnp.where(hit, turned[part * RECORD + 8:part * RECORD + 16], second)
                heads.append(first)
                rests.append(second[0:records - 8])
            lanes = pl.ds(pl.multiple_of(base, LANES), run)
            put(lanes, slice(0, 8), jnp.concatenate(heads, axis=1))
            put(lanes, slice(8, records), jnp.concatenate(rests, axis=1))
            return carry

        used = lax.div(live_count + (run - 1), run)
        lax.fori_loop(0, used, gather, 0)

        def blank(i, carry):
            lanes = pl.ds(pl.multiple_of(i * run, LANES), run)
            put(lanes, slice(0, records), jnp.zeros((records, run), jnp.float32))
            return carry

        lax.fori_loop(used, width // run, blank, 0)


def leave(grains, slots, counts, cells, picks, alive, rows_x, rows_y, depth):
    records, slot_count = grains.shape
    width = slots.shape[1]
    columns = rows_x * rows_y
    rows = max(LANES, 1 << (-(-slot_count // 8) - 1).bit_length())
    run = 2 * LANES if width % (2 * LANES) == 0 else LANES
    out = jax.ShapeDtypeStruct((records, width), jnp.float32)
    bf16 = jnp.bfloat16
    return pl.pallas_call(
        functools.partial(leave_kernel, rows_x, rows_y),
        out_shape=(
            out,
            out,
            jax.ShapeDtypeStruct((2, depth, depth), bf16),
            jax.ShapeDtypeStruct((2, columns, columns + 2 * REACH * rows_y), bf16),
            jax.ShapeDtypeStruct((2, columns, columns + 2 * REACH * rows_x), bf16),
            jax.ShapeDtypeStruct((picks.size, columns), bf16),
            jax.ShapeDtypeStruct(slots.shape, jnp.int32),
            jax.ShapeDtypeStruct(cells.shape, jnp.int32),
        ),
        in_specs=[HBM] * 6,
        out_specs=(VMEM,) * 8,
        scratch_shapes=[
            pltpu.VMEM(grains.shape, jnp.float32),
            pltpu.VMEM((LANES, rows), jnp.float32),
            pltpu.VMEM((rows, LANES), jnp.float32),
            pltpu.VMEM((run, LANES), jnp.float32),
            pltpu.VMEM(slots.shape, jnp.int32),
            pltpu.SMEM(slots.shape, jnp.int32),
            pltpu.SMEM(counts.shape, jnp.int32),
            pltpu.VMEM(picks.shape, jnp.int32),
            pltpu.VMEM(alive.shape, jnp.int32),
            pltpu.SemaphoreType.DMA((7,)),
        ],
        compiler_params=params(16),
        cost_estimate=cost(8),
        name="leave",
    )(*in_hbm(grains, slots, counts, cells, picks, alive))


def weights_at(apart):
    taps = kernel_taps()[REACH:]
    apart = jnp.abs(apart)
    value = jnp.where(apart == 0, taps[0], 0.0)
    for k in range(1, REACH + 1):
        value = jnp.where(apart == k, taps[k], value)
    return value


def put_operator(out_ref, start, value):
    high, low = halves(value)
    stop = start + value.shape[1]
    out_ref[0, :, start:stop] = high
    out_ref[1, :, start:stop] = low


def build_choice(picks_ref, alive_ref, choose_ref):
    rows_q, peers = picks_ref.shape
    slots, columns = choose_ref.shape
    alive = lax.broadcasted_iota(jnp.int32, (rows_q, peers), 0) < alive_ref[...]
    picks = jnp.where(alive, picks_ref[...], -1).astype(jnp.float32).astype(jnp.bfloat16)
    place_e, _ = split(lax.broadcasted_iota(jnp.int32, (slots, peers), 0), rows_q)
    here = place_e == lax.broadcasted_iota(jnp.int32, (slots, peers), 1)
    named = dot(jnp.where(here, 1.0, 0.0).astype(jnp.bfloat16), picks, NT)
    _, place_q = split(lax.broadcasted_iota(jnp.int32, (slots, rows_q), 0), rows_q)
    mine = place_q == lax.broadcasted_iota(jnp.int32, (slots, rows_q), 1)
    named = jnp.sum(jnp.where(mine, named, 0.0), axis=1, keepdims=True)
    hit = named == lax.broadcasted_iota(jnp.int32, (slots, columns), 1).astype(jnp.float32)
    choose_ref[...] = jnp.where(hit, 1.0, 0.0).astype(jnp.bfloat16)


def build_operators(rows_x, rows_y, depth_ref, stream_ref, span_ref):
    columns = rows_x * rows_y
    depth = depth_ref.shape[1]
    target = lax.broadcasted_iota(jnp.int32, (depth, depth), 0)
    source = lax.broadcasted_iota(jnp.int32, (depth, depth), 1)
    put_operator(depth_ref, 0, weights_at(target - source))

    own = (columns, columns)
    target_y, target_x = split(lax.broadcasted_iota(jnp.int32, own, 0), rows_x)
    row, source_x = split(lax.broadcasted_iota(jnp.int32, own, 1), rows_x)
    source_y = jnp.where(row < REACH, row, jnp.where(row < 2 * REACH, row + rows_y - 2 * REACH, row - REACH))
    put_operator(span_ref, 0, jnp.where(target_x == source_x, weights_at(target_y - source_y), 0.0))
    side = (columns, 2 * REACH * rows_x)
    target_y, target_x = split(lax.broadcasted_iota(jnp.int32, side, 0), rows_x)
    row, source_x = split(lax.broadcasted_iota(jnp.int32, side, 1), rows_x)
    source_y = jnp.where(row < REACH, row - REACH, row - REACH + rows_y)
    put_operator(span_ref, columns, jnp.where(target_x == source_x, weights_at(target_y - source_y), 0.0))

    target_x, target_y = split(lax.broadcasted_iota(jnp.int32, own, 0), rows_y)
    source_y, source_x = split(lax.broadcasted_iota(jnp.int32, own, 1), rows_x)
    put_operator(stream_ref, 0, jnp.where(target_y == source_y, weights_at(target_x - source_x), 0.0))
    side = (columns, 2 * REACH * rows_y)
    target_x, target_y = split(lax.broadcasted_iota(jnp.int32, side, 0), rows_y)
    plane, source_y = split(lax.broadcasted_iota(jnp.int32, side, 1), rows_y)
    source_x = jnp.where(plane < REACH, plane - REACH, plane - REACH + rows_x)
    put_operator(stream_ref, columns, jnp.where(target_y == source_y, weights_at(target_x - source_x), 0.0))


def row_of(y, rows_y):
    return jnp.where(y < REACH, y, jnp.where(y < rows_y - REACH, y + REACH, y - (rows_y - 2 * REACH)))


def keep_kernel(
    rows_x, rows_y, depth, grains_ref, marks_ref, cells_ref, after_hbm, quant_ref,
    high_rows, low_rows, gone, kept, sems,
):
    records, slot_count = grains_ref.shape
    total = quant_ref.shape[1]
    width = marks_ref.shape[1]
    tiles = slot_count // LANES
    pieces = sems.shape[0]

    row16 = lax.broadcasted_iota(jnp.int32, (16, LANES), 0).astype(jnp.float32)
    zero = jnp.zeros((16, LANES), jnp.bfloat16)
    one = jnp.ones((16, LANES), jnp.bfloat16)
    for which in (0, 1):

        def put(i, carry):
            lanes = lane_tile(i)
            to = pl.ds(pl.multiple_of(which * width + i * LANES, LANES), LANES)
            mark = marks_ref[which:which + 1, lanes]
            tile_of, lane_of = split(mark, LANES)
            tile_of = jnp.where(mark < 0, -1, tile_of)
            tile_of = wide(tile_of.astype(jnp.float32))
            lane_of = wide(lane_of.astype(jnp.float32))
            for k in range(high_rows.shape[0] // 16):
                hit = (row16 + 16.0 * k).astype(jnp.bfloat16) == tile_of
                high_rows[16 * k:16 * k + 16, to] = jnp.where(hit, one, zero)
            for k in range(LANES // 16):
                hit = (row16 + 16.0 * k).astype(jnp.bfloat16) == lane_of
                low_rows[16 * k:16 * k + 16, to] = jnp.where(hit, one, zero)
            return carry

        lax.fori_loop(0, width // LANES, put, 0, unroll=8)
    gone[...] = dot(high_rows[...], low_rows[...], NT)

    row8 = lax.broadcasted_iota(jnp.int32, (8, LANES), 0)

    def place(cell):
        x, rest = split(cell, rows_y * depth)
        y, level = split(rest, depth)
        return (row_of(y, rows_y) * rows_x + x).astype(jnp.float32), level.astype(jnp.float32)

    def keep(i, carry):
        lanes = lane_tile(i)
        stay = 1.0 - gone[pl.ds(i, 1), :]
        head = grains_ref[0:8, lanes] * stay
        rest = grains_ref[8:records, lanes] * stay
        kept[0:8, lanes] = head
        kept[8:records, lanes] = rest
        radius = rest[1:2]
        volume = 4.18879 * (radius * radius * radius)
        col, lev = place(cells_ref[:, lanes])
        value = jnp.where(row8 == QUANT_ROW[0], volume, volume * head)
        value = jnp.where(row8 == COLUMN_ROW, col, value)
        quant_ref[:, lanes] = jnp.where(row8 == LEVEL_ROW, lev, value)
        return carry

    writes = []
    for n in range(pieces):
        first = tiles * n // pieces
        last = tiles * (n + 1) // pieces
        lax.fori_loop(first, last, keep, 0, unroll=16)
        here = pl.ds(first * LANES, (last - first) * LANES)
        writes.append(pltpu.make_async_copy(kept.at[:, here], after_hbm.at[:, here], sems.at[n]))
        writes[n].start()

    def arrivals(i, carry):
        lanes = lane_tile(i)
        col, lev = place(cells_ref[:, lanes])
        quant_ref[:, lanes] = jnp.where(row8 == COLUMN_ROW, col, lev)
        return carry

    lax.fori_loop(tiles, total // LANES, arrivals, 0, unroll=8)
    for write in writes:
        write.wait()


def keep(grains, marks, cells, rows_x, rows_y, depth):
    records, slot_count = grains.shape
    total = cells.shape[1]
    rows = -(-(slot_count // LANES) // 16) * 16
    f32, bf16 = jnp.float32, jnp.bfloat16
    return pl.pallas_call(
        functools.partial(keep_kernel, rows_x, rows_y, depth),
        out_shape=(jax.ShapeDtypeStruct((records, total), f32), jax.ShapeDtypeStruct((8, total), f32)),
        in_specs=[VMEM] * 3,
        out_specs=(HBM, VMEM),
        scratch_shapes=[
            pltpu.VMEM((rows, 2 * marks.shape[1]), bf16),
            pltpu.VMEM((LANES, 2 * marks.shape[1]), bf16),
            pltpu.VMEM((rows, LANES), f32),
            pltpu.VMEM(grains.shape, f32),
            pltpu.SemaphoreType.DMA((4,)),
        ],
        compiler_params=params(20),
        cost_estimate=cost(4),
        name="keep",
    )(grains, marks, cells)


def join_kernel(after_in, quant_in, first_ref, second_ref, after_ref, quant_ref, sems):
    records, width = first_ref.shape
    start = after_ref.shape[1] - 2 * width
    row8 = lax.broadcasted_iota(jnp.int32, (8, LANES), 0)
    odd = is_odd("stream")
    copies = []
    for n, arrived in enumerate((first_ref, second_ref)):
        place = pl.multiple_of(start + (1 - odd if n == 0 else odd) * width, LANES)
        to = after_ref.at[:, pl.ds(place, width)]
        copies.append(pltpu.make_async_copy(arrived, to, sems.at[n]))
        copies[n].start()
    for n, arrived in enumerate((first_ref, second_ref)):

        def step(i, carry):
            lanes = lane_tile(i)
            place = start + (1 - odd if n == 0 else odd) * width
            to = pl.ds(pl.multiple_of(place + i * LANES, LANES), LANES)
            head = arrived[0:8, lanes]
            radius = arrived[9:10, lanes]
            volume = 4.18879 * (radius * radius * radius)
            value = jnp.where(row8 == QUANT_ROW[0], volume, volume * head)
            quant_ref[:, to] = jnp.where(row8 >= COLUMN_ROW, quant_in[:, to], value)
            return carry

        lax.fori_loop(0, width // LANES, step, 0, unroll=8)
    for copy in copies:
        copy.wait()


def join(after, quant, first, second):
    return pl.pallas_call(
        join_kernel,
        out_shape=(
            jax.ShapeDtypeStruct(after.shape, after.dtype),
            jax.ShapeDtypeStruct(quant.shape, quant.dtype),
        ),
        in_specs=[HBM, VMEM, VMEM, VMEM],
        out_specs=(HBM, VMEM),
        scratch_shapes=[pltpu.SemaphoreType.DMA((2,))],
        input_output_aliases={0: 0, 1: 1},
        compiler_params=params(16),
        cost_estimate=cost(1),
        name="join",
    )(*in_hbm(after), quant, first, second)


def deposit_kernel(base, chunk, edges, quant_ref, depth_ref, *refs):
    field_ref = refs[0]
    left_a, left_b, right_a, right_b, total = refs[-5:]
    channels = len(QUANT_ROW)
    columns = field_ref.shape[0] // channels
    depth = depth_ref.shape[1]
    steps = quant_ref.shape[1] // chunk
    row16 = lax.broadcasted_iota(jnp.int32, (16, LANES), 0).astype(jnp.float32)
    lanes_at = lax.broadcasted_iota(jnp.int32, (LANES, LANES), 1).astype(jnp.float32)
    zero = jnp.zeros((16, LANES), jnp.bfloat16)
    zeros = jnp.zeros((LANES, LANES), jnp.bfloat16)
    ones = jnp.ones((LANES, LANES), jnp.bfloat16)
    total[...] = jnp.zeros_like(total)

    def build(left, right, step):
        for j in range(chunk // LANES):
            here = slice(j * LANES, (j + 1) * LANES)
            lanes = pl.ds(pl.multiple_of(step * chunk + j * LANES, LANES), LANES)
            parts = [wide(quant_ref[r:r + 1, lanes]) for r in QUANT_ROW]
            column = wide(quant_ref[COLUMN_ROW:COLUMN_ROW + 1, lanes])
            for k in range(columns // 16):
                hit = (row16 + (base + 16.0 * k)).astype(jnp.bfloat16) == column
                for c in range(channels):
                    left[c * columns + 16 * k:c * columns + 16 * k + 16, here] = jnp.where(hit, parts[c], zero)
        tiles = [quant_ref[:, pl.ds(pl.multiple_of(step * chunk + j * LANES, LANES), LANES)] for j in range(chunk // LANES)]
        turned = jnp.transpose(jnp.concatenate(tiles, axis=0))
        for j in range(chunk // LANES):
            place = j * 8 + LEVEL_ROW
            level = jnp.broadcast_to(turned[:, place:place + 1], (LANES, LANES)).astype(jnp.bfloat16)
            for k in range(depth // LANES):
                hit = (lanes_at + k * LANES).astype(jnp.bfloat16) == level
                right[j * LANES:(j + 1) * LANES, k * LANES:(k + 1) * LANES] = jnp.where(hit, ones, zeros)

    build(left_a, right_a, 0)

    def two(i, carry):
        now = 2 * i
        build(left_b, right_b, now + 1)
        total[...] += dot(left_a[...], right_a[...])
        build(left_a, right_a, jnp.minimum(now + 2, steps - 1))
        total[...] += dot(left_b[...], right_b[...])
        return carry

    lax.fori_loop(0, steps // 2, two, 0)
    if steps % 2:
        total[...] += dot(left_a[...], right_a[...])

    high, low = halves(total[...])
    field_ref[...] = dot(high, depth_ref[0]) + (dot(high, depth_ref[1]) + dot(low, depth_ref[0]))
    if edges:
        first_ref, second_ref = refs[1:3]
        edge = columns // 2
        odd = is_odd("span")
        for c in range(channels):
            to = slice(c * edge, (c + 1) * edge)
            front = c * columns + (1 - odd) * edge
            back = c * columns + odd * edge
            first_ref[to, :] = field_ref[pl.ds(pl.multiple_of(front, 8), edge), :]
            second_ref[to, :] = field_ref[pl.ds(pl.multiple_of(back, 8), edge), :]


def deposit(base, columns, chunk, edges, quant, depth_op):
    depth = depth_op.shape[1]
    channels = len(QUANT_ROW)
    field = jax.ShapeDtypeStruct((channels * columns, depth), jnp.float32)
    edge = jax.ShapeDtypeStruct((channels * columns // 2, depth), jnp.float32)
    outs = (field, edge, edge) if edges else (field,)
    left = pltpu.VMEM((channels * columns, chunk), jnp.bfloat16)
    right = pltpu.VMEM((chunk, depth), jnp.bfloat16)
    return pl.pallas_call(
        functools.partial(deposit_kernel, base, chunk, edges),
        out_shape=outs,
        in_specs=[VMEM, VMEM],
        out_specs=(VMEM,) * len(outs),
        scratch_shapes=[left, left, right, right, pltpu.VMEM(field.shape, jnp.float32)],
        compiler_params=params(20),
        cost_estimate=cost(columns * 0.09),
        name="deposit",
    )(quant, depth_op)


def mix(operator_ref, start, piece):
    take = slice(start, start + piece.shape[0])
    high, low = halves(piece)
    return dot(operator_ref[0, :, take], high) + (
        dot(operator_ref[1, :, take], high) + dot(operator_ref[0, :, take], low)
    )


def own_kernel(operator_ref, *refs):
    channels = len(QUANT_ROW)
    part_ref = refs[-1]
    columns = part_ref.shape[0] // channels
    for c in range(channels):
        start, value = 0, None
        for ref in refs[:-1]:
            size = ref.shape[0] // channels
            piece = mix(operator_ref, start, ref[c * size:(c + 1) * size, :])
            value = piece if value is None else value + piece
            start += size
        part_ref[c * columns:(c + 1) * columns, :] = value


def own_part(operator, *fields):
    rows = sum(field.shape[0] for field in fields)
    return pl.pallas_call(
        own_kernel,
        out_shape=jax.ShapeDtypeStruct((rows, fields[0].shape[1]), jnp.float32),
        in_specs=[VMEM] * (1 + len(fields)),
        out_specs=VMEM,
        compiler_params=params(12),
        cost_estimate=cost(1),
        name="own_part",
    )(operator, *fields)


def sides(axis, first, second):
    odd = is_odd(axis) == 1
    return jnp.concatenate([jnp.where(odd, first, second), jnp.where(odd, second, first)], axis=0)


def span_kernel(rows_x, rows_y, part_ref, first_in, second_in, operator_ref, field_ref, first_ref, second_ref):
    channels = len(QUANT_ROW)
    columns = rows_x * rows_y
    halo = first_in.shape[0] // channels
    odd = is_odd("stream")
    first_x = (1 - odd) * (rows_x - REACH)
    second_x = odd * (rows_x - REACH)
    for c in range(channels):
        own = slice(c * columns, (c + 1) * columns)
        side = slice(c * halo, (c + 1) * halo)
        field_ref[own, :] = part_ref[own, :] + mix(
            operator_ref, columns, sides("span", first_in[side, :], second_in[side, :])
        )
    for c in range(channels):
        for k in range(REACH):
            for y in range(rows_y):
                to = (c * REACH + k) * rows_y + y
                row = c * columns + y * rows_x + k
                first_ref[to:to + 1, :] = field_ref[pl.ds(row + first_x, 1), :]
                second_ref[to:to + 1, :] = field_ref[pl.ds(row + second_x, 1), :]


def span_pass(rows_x, rows_y, part, first, second, operator):
    channels = len(QUANT_ROW)
    depth = part.shape[1]
    halo = jax.ShapeDtypeStruct((channels * REACH * rows_y, depth), jnp.float32)
    return pl.pallas_call(
        functools.partial(span_kernel, rows_x, rows_y),
        out_shape=(jax.ShapeDtypeStruct((channels * rows_x * rows_y, depth), jnp.float32), halo, halo),
        in_specs=[VMEM] * 4,
        out_specs=(VMEM,) * 3,
        compiler_params=params(12),
        cost_estimate=cost(1),
        name="span_pass",
    )(part, first, second, operator)


def stream_kernel(rows_q, part_ref, first_in, second_in, operator_ref, choose_ref, fluid_ref, solid_ref, out_ref):
    channels = len(QUANT_ROW)
    columns = part_ref.shape[0] // channels
    halo = first_in.shape[0] // channels
    choose = choose_ref[...]
    base = None
    for c in range(channels):
        own = slice(c * columns, (c + 1) * columns)
        side = slice(c * halo, (c + 1) * halo)
        solid = part_ref[own, :] + mix(
            operator_ref, columns, sides("stream", first_in[side, :], second_in[side, :])
        )
        solid_ref[own, :] = solid
        if c == 0:
            base = solid
            value = 1.0 / (1.0 + base)
        else:
            flow = fluid_ref[(c - 1) * columns:c * columns, :]
            value = flow + drag_rate * (solid - base * flow)
        first, rest = halves(value)
        second, third = halves(value - first.astype(jnp.float32))
        sent = dot(choose, first) + (dot(choose, second) + dot(choose, third))
        place = (c - 1) % channels
        out_ref[:, :, place, :] = sent.reshape(sent.shape[0] // rows_q, rows_q, -1)


def stream_pass(peers, rows_q, part, first, second, operator, choose, fluid):
    channels = len(QUANT_ROW)
    depth = part.shape[1]
    return pl.pallas_call(
        functools.partial(stream_kernel, rows_q),
        out_shape=(
            jax.ShapeDtypeStruct(part.shape, jnp.float32),
            jax.ShapeDtypeStruct((peers, rows_q, channels, depth), jnp.float32),
        ),
        in_specs=[VMEM] * 6,
        out_specs=(VMEM, VMEM),
        compiler_params=params(16),
        cost_estimate=cost(3.5),
        name="stream_pass",
    )(part, first, second, operator, choose, fluid)


def swap(first, second, axis, periodic):
    count = lax.axis_size(axis)
    assert count % 2 == 0
    pairs = [(source, source ^ 1) for source in range(count)]
    others = [(source, (source + 1 if source % 2 else source - 1) % count) for source in range(count)]
    if not periodic:
        others = [pair for pair in others if abs(pair[0] - pair[1]) == 1]
    second = lax.ppermute(second, axis, others)
    return lax.ppermute(first, axis, pairs), second


def per_device(grains, send_slots, send_counts, cell_index, fluid, block_slots, block_counts):
    rows_x, rows_y, depth = fluid.shape[1:]
    columns = rows_x * rows_y
    width = send_slots.shape[2]
    peers, rows_q = block_slots.shape[1:]
    total = cell_index.shape[0]
    axes = ("stream", "span")

    first, second, depth_op, stream_op, span_op, choose, marks, cells = leave(
        grains, send_slots[0], send_counts, cell_index.reshape(1, -1), block_slots[0].T, block_counts,
        rows_x, rows_y, depth,
    )
    arrived = swap(first, second, "stream", True)
    after, quant = keep(grains, marks, cells, rows_x, rows_y, depth)
    grains_after, quant = join(after, quant, *arrived)

    chunk = math.gcd(total, 2048)
    faces = 2 * REACH * rows_x
    edge, first, second = deposit(0, faces, chunk, True, quant, depth_op)
    first, second = swap(first, second, "span", False)
    (inner,) = deposit(faces, columns - faces, chunk, False, quant, depth_op)
    part = own_part(span_op, edge, inner)
    field, *halos = span_pass(rows_x, rows_y, part, first, second, span_op)
    halos = swap(*halos, "stream", True)
    part = own_part(stream_op, field)
    solid, outgoing = stream_pass(
        peers, rows_q, part, *halos, stream_op, choose, fluid.reshape(3 * columns, depth)
    )
    arrived = lax.all_to_all(outgoing, axes, split_axis=0, concat_axis=0, tiled=True)
    return grains_after, solid.reshape(4, rows_x, rows_y, depth), arrived[None]


def solution(mesh):
    return jax.shard_map(
        per_device,
        mesh=mesh,
        in_specs=(
            P(None, ("stream", "span")),
            P(("stream", "span"), None, None),
            P(("stream", "span"), None),
            P(("stream", "span")),
            P(None, "stream", "span", None),
            P(("stream", "span"), None, None),
            P(("stream", "span"), None),
        ),
        out_specs=(
            P(None, ("stream", "span")),
            P(None, "stream", "span", None),
            P(("stream", "span"), None, None, None, None),
        ),
        check_vma=False,
    )
```

```python
import functools
import math

import jax
import jax.numpy as jnp
from jax import lax
from jax.experimental import pallas as pl
from jax.experimental.pallas import tpu as pltpu
from jax.sharding import PartitionSpec as P

REACH = 3
LANES = 128
RECORD = 16
BATCH = 32

spread_cells = 1.5
drag_rate = 0.25

VMEM = pl.BlockSpec(memory_space=pltpu.VMEM)
HBM = pl.BlockSpec(memory_space=pltpu.HBM)
NT = (((1,), (1,)), ((), ()))
NN = (((1,), (0,)), ((), ()))

QUANT_ROW = (0, 3, 4, 5)
COLUMN_ROW = 6
LEVEL_ROW = 7


def kernel_taps():
    raw = [
        math.exp(-(k * k) / (2.0 * spread_cells * spread_cells)) for k in range(-REACH, REACH + 1)
    ]
    total = sum(raw)
    return [value / total for value in raw]


def params(mib):
    return pltpu.CompilerParams(vmem_limit_bytes=mib * 2**20)


def cost(micros):
    return pl.CostEstimate(flops=0, bytes_accessed=int(micros * 3.0e6), transcendentals=0)


def split(values, size):
    if size & (size - 1):
        return lax.div(values, size), lax.rem(values, size)
    return lax.shift_right_logical(values, size.bit_length() - 1), lax.bitwise_and(values, size - 1)


def halves(values):
    high = values.astype(jnp.bfloat16)
    return high, (values - high.astype(jnp.float32)).astype(jnp.bfloat16)


def dot(left, right, dims=NN):
    return lax.dot_general(left, right, dims, preferred_element_type=jnp.float32)


def wide(values):
    return jnp.broadcast_to(values, (16, LANES)).astype(jnp.bfloat16)


def lane_tile(i):
    return pl.ds(pl.multiple_of(i * LANES, LANES), LANES)


def in_hbm(*values):
    return tuple(pltpu.with_memory_space_constraint(value, pltpu.HBM) for value in values)


def is_odd(axis):
    return lax.rem(lax.axis_index(axis), 2)


def leave_kernel(
    rows_x, rows_y, grains_hbm, slots_hbm, counts_hbm, cells_hbm, picks_hbm, alive_hbm,
    first_ref, second_ref, depth_ref, stream_ref, span_ref, choose_ref, marks_ref, cells_ref,
    grains_ref, stage, table, picked, slots_v, slots_s, counts_s, picks_v, alive_v, sems,
):
    records, slot_count = grains_ref.shape
    width = first_ref.shape[1]
    rows = table.shape[0]
    parts = -(-slot_count // rows)
    sources = (grains_hbm, slots_hbm, slots_hbm, counts_hbm, picks_hbm, alive_hbm, cells_hbm)
    targets = (grains_ref, slots_v, slots_s, counts_s, picks_v, alive_v, cells_ref)
    copies = [
        pltpu.make_async_copy(source, target, sems.at[i])
        for i, (source, target) in enumerate(zip(sources, targets))
    ]
    for copy in copies:
        copy.start()
    build_operators(rows_x, rows_y, depth_ref, stream_ref, span_ref)
    copies[0].wait()

    for part in range(parts):
        size = min(rows, slot_count - part * rows)
        here = slice(part * rows, part * rows + size)
        stage[part * RECORD:part * RECORD + 8, 0:size] = grains_ref[0:8, here]
        stage[part * RECORD + 8:part * RECORD + records, 0:size] = grains_ref[8:records, here]
    for block in range(rows // LANES):
        here = slice(block * LANES, (block + 1) * LANES)
        table[here, :] = jnp.transpose(stage[:, here])
    for copy in copies[1:]:
        copy.wait()
    build_choice(picks_v, alive_v, choose_ref)
    for which in (0, 1):
        live = lax.broadcasted_iota(jnp.int32, (1, width), 1) < counts_s[0, which]
        marks_ref[which:which + 1, :] = jnp.where(live, slots_v[which:which + 1, :], -1)

    run = picked.shape[0]
    lane = lax.broadcasted_iota(jnp.int32, (8, LANES), 1)
    odd = is_odd("stream")
    for which in (0, 1):
        live_count = counts_s[0, which]

        def put(lanes, rows_to, value):
            @pl.when(odd == which)
            def _():
                first_ref[rows_to, lanes] = value

            @pl.when(odd != which)
            def _():
                second_ref[rows_to, lanes] = value

        def gather(i, carry):
            base = i * run
            for k in range(0, run, BATCH):
                found = [lax.bitwise_and(slots_s[which, base + k + n], rows - 1) for n in range(BATCH)]
                found = [table[pl.ds(row, 1), :] for row in found]
                for n in range(BATCH):
                    picked[k + n:k + n + 1, :] = found[n]
            heads, rests = [], []
            for piece in range(run // LANES):
                lanes = pl.ds(pl.multiple_of(base + piece * LANES, LANES), LANES)
                turned = jnp.transpose(picked[piece * LANES:(piece + 1) * LANES, :])
                slot = jnp.broadcast_to(slots_v[which:which + 1, lanes], (8, LANES))
                part_of = lax.shift_right_logical(slot, rows.bit_length() - 1)
                live = lane + (base + piece * LANES) < live_count
                first = jnp.zeros((8, LANES), jnp.float32)
                second = first
                for part in range(parts):
                    hit = jnp.logical_and(live, part_of == part)
                    first = jnp.where(hit, turned[part * RECORD:part * RECORD + 8], first)
                    second = jnp.where(hit, turned[part * RECORD + 8:part * RECORD + 16], second)
                heads.append(first)
                rests.append(second[0:records - 8])
            lanes = pl.ds(pl.multiple_of(base, LANES), run)
            put(lanes, slice(0, 8), jnp.concatenate(heads, axis=1))
            put(lanes, slice(8, records), jnp.concatenate(rests, axis=1))
            return carry

        used = lax.div(live_count + (run - 1), run)
        lax.fori_loop(0, used, gather, 0)

        def blank(i, carry):
            lanes = pl.ds(pl.multiple_of(i * run, LANES), run)
            put(lanes, slice(0, records), jnp.zeros((records, run), jnp.float32))
            return carry

        lax.fori_loop(used, width // run, blank, 0)


def leave(grains, slots, counts, cells, picks, alive, rows_x, rows_y, depth):
    records, slot_count = grains.shape
    width = slots.shape[1]
    columns = rows_x * rows_y
    rows = max(LANES, 1 << (-(-slot_count // 8) - 1).bit_length())
    run = 2 * LANES if width % (2 * LANES) == 0 else LANES
    out = jax.ShapeDtypeStruct((records, width), jnp.float32)
    bf16 = jnp.bfloat16
    return pl.pallas_call(
        functools.partial(leave_kernel, rows_x, rows_y),
        out_shape=(
            out,
            out,
            jax.ShapeDtypeStruct((2, depth, depth), bf16),
            jax.ShapeDtypeStruct((2, columns, columns + 2 * REACH * rows_y), bf16),
            jax.ShapeDtypeStruct((2, columns, columns + 2 * REACH * rows_x), bf16),
            jax.ShapeDtypeStruct((picks.size, columns), bf16),
            jax.ShapeDtypeStruct(slots.shape, jnp.int32),
            jax.ShapeDtypeStruct(cells.shape, jnp.int32),
        ),
        in_specs=[HBM] * 6,
        out_specs=(VMEM,) * 8,
        scratch_shapes=[
            pltpu.VMEM(grains.shape, jnp.float32),
            pltpu.VMEM((LANES, rows), jnp.float32),
            pltpu.VMEM((rows, LANES), jnp.float32),
            pltpu.VMEM((run, LANES), jnp.float32),
            pltpu.VMEM(slots.shape, jnp.int32),
            pltpu.SMEM(slots.shape, jnp.int32),
            pltpu.SMEM(counts.shape, jnp.int32),
            pltpu.VMEM(picks.shape, jnp.int32),
            pltpu.VMEM(alive.shape, jnp.int32),
            pltpu.SemaphoreType.DMA((7,)),
        ],
        compiler_params=params(16),
        cost_estimate=cost(8),
        name="leave",
    )(*in_hbm(grains, slots, counts, cells, picks, alive))


def weights_at(apart):
    taps = kernel_taps()[REACH:]
    apart = jnp.abs(apart)
    value = jnp.where(apart == 0, taps[0], 0.0)
    for k in range(1, REACH + 1):
        value = jnp.where(apart == k, taps[k], value)
    return value


def put_operator(out_ref, start, value):
    high, low = halves(value)
    stop = start + value.shape[1]
    out_ref[0, :, start:stop] = high
    out_ref[1, :, start:stop] = low


def build_choice(picks_ref, alive_ref, choose_ref):
    rows_q, peers = picks_ref.shape
    slots, columns = choose_ref.shape
    alive = lax.broadcasted_iota(jnp.int32, (rows_q, peers), 0) < alive_ref[...]
    picks = jnp.where(alive, picks_ref[...], -1).astype(jnp.float32).astype(jnp.bfloat16)
    place_e, _ = split(lax.broadcasted_iota(jnp.int32, (slots, peers), 0), rows_q)
    here = place_e == lax.broadcasted_iota(jnp.int32, (slots, peers), 1)
    named = dot(jnp.where(here, 1.0, 0.0).astype(jnp.bfloat16), picks, NT)
    _, place_q = split(lax.broadcasted_iota(jnp.int32, (slots, rows_q), 0), rows_q)
    mine = place_q == lax.broadcasted_iota(jnp.int32, (slots, rows_q), 1)
    named = jnp.sum(jnp.where(mine, named, 0.0), axis=1, keepdims=True)
    hit = named == lax.broadcasted_iota(jnp.int32, (slots, columns), 1).astype(jnp.float32)
    choose_ref[...] = jnp.where(hit, 1.0, 0.0).astype(jnp.bfloat16)


def build_operators(rows_x, rows_y, depth_ref, stream_ref, span_ref):
    columns = rows_x * rows_y
    depth = depth_ref.shape[1]
    target = lax.broadcasted_iota(jnp.int32, (depth, depth), 0)
    source = lax.broadcasted_iota(jnp.int32, (depth, depth), 1)
    put_operator(depth_ref, 0, weights_at(target - source))

    own = (columns, columns)
    target_y, target_x = split(lax.broadcasted_iota(jnp.int32, own, 0), rows_x)
    row, source_x = split(lax.broadcasted_iota(jnp.int32, own, 1), rows_x)
    source_y = jnp.where(row < REACH, row, jnp.where(row < 2 * REACH, row + rows_y - 2 * REACH, row - REACH))
    put_operator(span_ref, 0, jnp.where(target_x == source_x, weights_at(target_y - source_y), 0.0))
    side = (columns, 2 * REACH * rows_x)
    target_y, target_x = split(lax.broadcasted_iota(jnp.int32, side, 0), rows_x)
    row, source_x = split(lax.broadcasted_iota(jnp.int32, side, 1), rows_x)
    source_y = jnp.where(row < REACH, row - REACH, row - REACH + rows_y)
    put_operator(span_ref, columns, jnp.where(target_x == source_x, weights_at(target_y - source_y), 0.0))

    target_x, target_y = split(lax.broadcasted_iota(jnp.int32, own, 0), rows_y)
    source_y, source_x = split(lax.broadcasted_iota(jnp.int32, own, 1), rows_x)
    put_operator(stream_ref, 0, jnp.where(target_y == source_y, weights_at(target_x - source_x), 0.0))
    side = (columns, 2 * REACH * rows_y)
    target_x, target_y = split(lax.broadcasted_iota(jnp.int32, side, 0), rows_y)
    plane, source_y = split(lax.broadcasted_iota(jnp.int32, side, 1), rows_y)
    source_x = jnp.where(plane < REACH, plane - REACH, plane - REACH + rows_x)
    put_operator(stream_ref, columns, jnp.where(target_y == source_y, weights_at(target_x - source_x), 0.0))


def row_of(y, rows_y):
    return jnp.where(y < REACH, y, jnp.where(y < rows_y - REACH, y + REACH, y - (rows_y - 2 * REACH)))


def keep_kernel(
    rows_x, rows_y, depth, grains_ref, marks_ref, cells_ref, after_hbm, quant_ref,
    high_rows, low_rows, gone, kept, sems,
):
    records, slot_count = grains_ref.shape
    total = quant_ref.shape[1]
    width = marks_ref.shape[1]
    tiles = slot_count // LANES
    pieces = sems.shape[0]

    row16 = lax.broadcasted_iota(jnp.int32, (16, LANES), 0).astype(jnp.float32)
    zero = jnp.zeros((16, LANES), jnp.bfloat16)
    one = jnp.ones((16, LANES), jnp.bfloat16)
    for which in (0, 1):

        def put(i, carry):
            lanes = lane_tile(i)
            to = pl.ds(pl.multiple_of(which * width + i * LANES, LANES), LANES)
            mark = marks_ref[which:which + 1, lanes]
            tile_of, lane_of = split(mark, LANES)
            tile_of = jnp.where(mark < 0, -1, tile_of)
            tile_of = wide(tile_of.astype(jnp.float32))
            lane_of = wide(lane_of.astype(jnp.float32))
            for k in range(high_rows.shape[0] // 16):
                hit = (row16 + 16.0 * k).astype(jnp.bfloat16) == tile_of
                high_rows[16 * k:16 * k + 16, to] = jnp.where(hit, one, zero)
            for k in range(LANES // 16):
                hit = (row16 + 16.0 * k).astype(jnp.bfloat16) == lane_of
                low_rows[16 * k:16 * k + 16, to] = jnp.where(hit, one, zero)
            return carry

        lax.fori_loop(0, width // LANES, put, 0, unroll=8)
    gone[...] = dot(high_rows[...], low_rows[...], NT)

    def place(cell):
        x, rest = split(cell, rows_y * depth)
        y, level = split(rest, depth)
        return (row_of(y, rows_y) * rows_x + x).astype(jnp.float32), level.astype(jnp.float32)

    block = math.gcd(math.gcd(slot_count, total - slot_count), 16 * LANES)

    def table(head, volume, start):
        row8 = lax.broadcasted_iota(jnp.int32, (8, block), 0)
        col, lev = place(cells_ref[:, pl.ds(start, block)])
        value = jnp.where(row8 == QUANT_ROW[0], volume, volume * head)
        value = jnp.where(row8 == COLUMN_ROW, col, value)
        return jnp.where(row8 == LEVEL_ROW, lev, value)

    def keep(i, carry):
        start = pl.multiple_of(i * block, block)
        lanes = pl.ds(start, block)
        first = i * (block // LANES)
        stay = [1.0 - gone[pl.ds(first + n, 1), :] for n in range(block // LANES)]
        stay = jnp.concatenate(stay, axis=1)
        head = grains_ref[0:8, lanes] * stay
        rest = grains_ref[8:records, lanes] * stay
        radius = rest[1:2]
        value = table(head, 4.18879 * (radius * radius * radius), start)
        kept[0:8, lanes] = head
        kept[8:records, lanes] = rest
        quant_ref[:, lanes] = value
        return carry

    writes = []
    blocks = slot_count // block
    for n in range(pieces):
        first = blocks * n // pieces
        last = blocks * (n + 1) // pieces
        lax.fori_loop(first, last, keep, 0)
        here = pl.ds(first * block, (last - first) * block)
        writes.append(pltpu.make_async_copy(kept.at[:, here], after_hbm.at[:, here], sems.at[n]))
        writes[n].start()

    def arrivals(i, carry):
        start = pl.multiple_of(i * block, block)
        none = jnp.zeros((8, block), jnp.float32)
        quant_ref[:, pl.ds(start, block)] = table(none, none[0:1], start)
        return carry

    lax.fori_loop(blocks, total // block, arrivals, 0)
    for write in writes:
        write.wait()


def keep(grains, marks, cells, rows_x, rows_y, depth):
    records, slot_count = grains.shape
    total = cells.shape[1]
    rows = -(-(slot_count // LANES) // 16) * 16
    f32, bf16 = jnp.float32, jnp.bfloat16
    return pl.pallas_call(
        functools.partial(keep_kernel, rows_x, rows_y, depth),
        out_shape=(jax.ShapeDtypeStruct((records, total), f32), jax.ShapeDtypeStruct((8, total), f32)),
        in_specs=[VMEM] * 3,
        out_specs=(HBM, VMEM),
        scratch_shapes=[
            pltpu.VMEM((rows, 2 * marks.shape[1]), bf16),
            pltpu.VMEM((LANES, 2 * marks.shape[1]), bf16),
            pltpu.VMEM((rows, LANES), f32),
            pltpu.VMEM(grains.shape, f32),
            pltpu.SemaphoreType.DMA((4,)),
        ],
        compiler_params=params(20),
        cost_estimate=cost(4),
        name="keep",
    )(grains, marks, cells)


def join_kernel(after_in, quant_in, first_ref, second_ref, after_ref, quant_ref, sems):
    records, width = first_ref.shape
    start = after_ref.shape[1] - 2 * width
    block = math.gcd(math.gcd(width, start), 16 * LANES)
    row8 = lax.broadcasted_iota(jnp.int32, (8, block), 0)
    odd = is_odd("stream")
    copies = []
    for n, arrived in enumerate((first_ref, second_ref)):
        place = pl.multiple_of(start + (1 - odd if n == 0 else odd) * width, LANES)
        to = after_ref.at[:, pl.ds(place, width)]
        copies.append(pltpu.make_async_copy(arrived, to, sems.at[n]))
        copies[n].start()
    for n, arrived in enumerate((first_ref, second_ref)):

        def step(i, carry):
            lanes = pl.ds(pl.multiple_of(i * block, block), block)
            place = start + (1 - odd if n == 0 else odd) * width
            to = pl.ds(pl.multiple_of(place + i * block, block), block)
            head = arrived[0:8, lanes]
            radius = arrived[9:10, lanes]
            volume = 4.18879 * (radius * radius * radius)
            value = jnp.where(row8 == QUANT_ROW[0], volume, volume * head)
            quant_ref[:, to] = jnp.where(row8 >= COLUMN_ROW, quant_in[:, to], value)
            return carry

        lax.fori_loop(0, width // block, step, 0)
    for copy in copies:
        copy.wait()


def join(after, quant, first, second):
    return pl.pallas_call(
        join_kernel,
        out_shape=(
            jax.ShapeDtypeStruct(after.shape, after.dtype),
            jax.ShapeDtypeStruct(quant.shape, quant.dtype),
        ),
        in_specs=[HBM, VMEM, VMEM, VMEM],
        out_specs=(HBM, VMEM),
        scratch_shapes=[pltpu.SemaphoreType.DMA((2,))],
        input_output_aliases={0: 0, 1: 1},
        compiler_params=params(16),
        cost_estimate=cost(1),
        name="join",
    )(*in_hbm(after), quant, first, second)


def deposit_kernel(base, chunk, edges, quant_ref, depth_ref, *refs):
    field_ref = refs[0]
    left_a, left_b, right_a, right_b, now_a, now_b, total = refs[-7:]
    channels = len(QUANT_ROW)
    columns = field_ref.shape[0] // channels
    depth = depth_ref.shape[1]
    steps = quant_ref.shape[1] // chunk
    row16 = lax.broadcasted_iota(jnp.int32, (16, LANES), 0).astype(jnp.float32)
    zero = jnp.zeros((16, LANES), jnp.bfloat16)
    one = jnp.ones((16, LANES), jnp.bfloat16)
    total[...] = jnp.zeros_like(total)

    def build(left, right, now, step):
        now[...] = quant_ref[:, pl.ds(pl.multiple_of(step * chunk, chunk), chunk)]
        for j in range(chunk // LANES):
            here = slice(j * LANES, (j + 1) * LANES)
            parts = [wide(now[r:r + 1, here]) for r in QUANT_ROW]
            column = wide(now[COLUMN_ROW:COLUMN_ROW + 1, here])
            level = wide(now[LEVEL_ROW:LEVEL_ROW + 1, here])
            for k in range(columns // 16):
                hit = (row16 + (base + 16.0 * k)).astype(jnp.bfloat16) == column
                for c in range(channels):
                    left[c * columns + 16 * k:c * columns + 16 * k + 16, here] = jnp.where(hit, parts[c], zero)
            for k in range(depth // 16):
                hit = (row16 + 16.0 * k).astype(jnp.bfloat16) == level
                right[16 * k:16 * k + 16, here] = jnp.where(hit, one, zero)

    build(left_a, right_a, now_a, 0)

    def two(i, carry):
        now = 2 * i
        build(left_b, right_b, now_b, now + 1)
        total[...] += dot(left_a[...], right_a[...], NT)
        build(left_a, right_a, now_a, jnp.minimum(now + 2, steps - 1))
        total[...] += dot(left_b[...], right_b[...], NT)
        return carry

    lax.fori_loop(0, steps // 2, two, 0)
    if steps % 2:
        total[...] += dot(left_a[...], right_a[...], NT)

    high, low = halves(total[...])
    field_ref[...] = dot(high, depth_ref[0]) + (dot(high, depth_ref[1]) + dot(low, depth_ref[0]))
    if edges:
        first_ref, second_ref = refs[1:3]
        edge = columns // 2
        odd = is_odd("span")
        for c in range(channels):
            to = slice(c * edge, (c + 1) * edge)
            front = c * columns + (1 - odd) * edge
            back = c * columns + odd * edge
            first_ref[to, :] = field_ref[pl.ds(pl.multiple_of(front, 8), edge), :]
            second_ref[to, :] = field_ref[pl.ds(pl.multiple_of(back, 8), edge), :]


def deposit(base, columns, chunk, edges, quant, depth_op):
    depth = depth_op.shape[1]
    channels = len(QUANT_ROW)
    field = jax.ShapeDtypeStruct((channels * columns, depth), jnp.float32)
    edge = jax.ShapeDtypeStruct((channels * columns // 2, depth), jnp.float32)
    outs = (field, edge, edge) if edges else (field,)
    left = pltpu.VMEM((channels * columns, chunk), jnp.bfloat16)
    right = pltpu.VMEM((depth, chunk), jnp.bfloat16)
    now = pltpu.VMEM((8, chunk), jnp.float32)
    return pl.pallas_call(
        functools.partial(deposit_kernel, base, chunk, edges),
        out_shape=outs,
        in_specs=[VMEM, VMEM],
        out_specs=(VMEM,) * len(outs),
        scratch_shapes=[left, left, right, right, now, now, pltpu.VMEM(field.shape, jnp.float32)],
        compiler_params=params(20),
        cost_estimate=cost(columns * 0.09),
        name="deposit",
    )(quant, depth_op)


def mix(operator_ref, start, piece):
    take = slice(start, start + piece.shape[0])
    high, low = halves(piece)
    return dot(operator_ref[0, :, take], high) + (
        dot(operator_ref[1, :, take], high) + dot(operator_ref[0, :, take], low)
    )


def own_kernel(operator_ref, *refs):
    channels = len(QUANT_ROW)
    part_ref = refs[-1]
    columns = part_ref.shape[0] // channels
    for c in range(channels):
        start, value = 0, None
        for ref in refs[:-1]:
            size = ref.shape[0] // channels
            piece = mix(operator_ref, start, ref[c * size:(c + 1) * size, :])
            value = piece if value is None else value + piece
            start += size
        part_ref[c * columns:(c + 1) * columns, :] = value


def own_part(operator, *fields):
    rows = sum(field.shape[0] for field in fields)
    return pl.pallas_call(
        own_kernel,
        out_shape=jax.ShapeDtypeStruct((rows, fields[0].shape[1]), jnp.float32),
        in_specs=[VMEM] * (1 + len(fields)),
        out_specs=VMEM,
        compiler_params=params(12),
        cost_estimate=cost(1),
        name="own_part",
    )(operator, *fields)


def sides(axis, first, second):
    odd = is_odd(axis) == 1
    return jnp.concatenate([jnp.where(odd, first, second), jnp.where(odd, second, first)], axis=0)


def span_kernel(rows_x, rows_y, part_ref, first_in, second_in, operator_ref, field_ref, first_ref, second_ref):
    channels = len(QUANT_ROW)
    columns = rows_x * rows_y
    halo = first_in.shape[0] // channels
    odd = is_odd("stream")
    first_x = (1 - odd) * (rows_x - REACH)
    second_x = odd * (rows_x - REACH)
    for c in range(channels):
        own = slice(c * columns, (c + 1) * columns)
        side = slice(c * halo, (c + 1) * halo)
        field_ref[own, :] = part_ref[own, :] + mix(
            operator_ref, columns, sides("span", first_in[side, :], second_in[side, :])
        )
    for c in range(channels):
        for k in range(REACH):
            for y in range(rows_y):
                to = (c * REACH + k) * rows_y + y
                row = c * columns + y * rows_x + k
                first_ref[to:to + 1, :] = field_ref[pl.ds(row + first_x, 1), :]
                second_ref[to:to + 1, :] = field_ref[pl.ds(row + second_x, 1), :]


def span_pass(rows_x, rows_y, part, first, second, operator):
    channels = len(QUANT_ROW)
    depth = part.shape[1]
    halo = jax.ShapeDtypeStruct((channels * REACH * rows_y, depth), jnp.float32)
    return pl.pallas_call(
        functools.partial(span_kernel, rows_x, rows_y),
        out_shape=(jax.ShapeDtypeStruct((channels * rows_x * rows_y, depth), jnp.float32), halo, halo),
        in_specs=[VMEM] * 4,
        out_specs=(VMEM,) * 3,
        compiler_params=params(12),
        cost_estimate=cost(1),
        name="span_pass",
    )(part, first, second, operator)


def stream_kernel(
    rows_q, part_ref, first_in, second_in, operator_ref, choose_ref, fluid_ref, solid_hbm, out_ref, solid_ref, sems
):
    channels = len(QUANT_ROW)
    columns = part_ref.shape[0] // channels
    halo = first_in.shape[0] // channels
    choose = choose_ref[...]
    copies = []
    for c in range(channels):
        own = slice(c * columns, (c + 1) * columns)
        side = slice(c * halo, (c + 1) * halo)
        solid_ref[own, :] = part_ref[own, :] + mix(
            operator_ref, columns, sides("stream", first_in[side, :], second_in[side, :])
        )
        copies.append(pltpu.make_async_copy(solid_ref.at[own, :], solid_hbm.at[own, :], sems.at[c]))
        copies[c].start()
    base = solid_ref[0:columns, :]
    for c in range(channels):
        if c == 0:
            value = 1.0 / (1.0 + base)
        else:
            flow = fluid_ref[(c - 1) * columns:c * columns, :]
            value = flow + drag_rate * (solid_ref[c * columns:(c + 1) * columns, :] - base * flow)
        first, rest = halves(value)
        second, third = halves(value - first.astype(jnp.float32))
        sent = dot(choose, first) + (dot(choose, second) + dot(choose, third))
        place = (c - 1) % channels
        out_ref[:, :, place, :] = sent.reshape(sent.shape[0] // rows_q, rows_q, -1)
    for copy in copies:
        copy.wait()


def stream_pass(peers, rows_q, part, first, second, operator, choose, fluid):
    channels = len(QUANT_ROW)
    depth = part.shape[1]
    return pl.pallas_call(
        functools.partial(stream_kernel, rows_q),
        out_shape=(
            jax.ShapeDtypeStruct(part.shape, jnp.float32),
            jax.ShapeDtypeStruct((peers, rows_q, channels, depth), jnp.float32),
        ),
        in_specs=[VMEM] * 6,
        out_specs=(HBM, VMEM),
        scratch_shapes=[pltpu.VMEM(part.shape, jnp.float32), pltpu.SemaphoreType.DMA((channels,))],
        compiler_params=params(16),
        cost_estimate=cost(2),
        name="stream_pass",
    )(part, first, second, operator, choose, fluid)


def swap(first, second, axis, periodic):
    count = lax.axis_size(axis)
    assert count % 2 == 0
    pairs = [(source, source ^ 1) for source in range(count)]
    others = [(source, (source + 1 if source % 2 else source - 1) % count) for source in range(count)]
    if not periodic:
        others = [pair for pair in others if abs(pair[0] - pair[1]) == 1]
    second = lax.ppermute(second, axis, others)
    return lax.ppermute(first, axis, pairs), second


def per_device(grains, send_slots, send_counts, cell_index, fluid, block_slots, block_counts):
    rows_x, rows_y, depth = fluid.shape[1:]
    columns = rows_x * rows_y
    width = send_slots.shape[2]
    peers, rows_q = block_slots.shape[1:]
    total = cell_index.shape[0]
    axes = ("stream", "span")

    first, second, depth_op, stream_op, span_op, choose, marks, cells = leave(
        grains, send_slots[0], send_counts, cell_index.reshape(1, -1), block_slots[0].T, block_counts,
        rows_x, rows_y, depth,
    )
    arrived = swap(first, second, "stream", True)
    after, quant = keep(grains, marks, cells, rows_x, rows_y, depth)
    grains_after, quant = join(after, quant, *arrived)

    chunk = math.gcd(total, 2048)
    faces = 2 * REACH * rows_x
    edge, first, second = deposit(0, faces, chunk, True, quant, depth_op)
    first, second = swap(first, second, "span", False)
    (inner,) = deposit(faces, columns - faces, chunk, False, quant, depth_op)
    part = own_part(span_op, edge, inner)
    field, *halos = span_pass(rows_x, rows_y, part, first, second, span_op)
    halos = swap(*halos, "stream", True)
    part = own_part(stream_op, field)
    solid, outgoing = stream_pass(
        peers, rows_q, part, *halos, stream_op, choose, fluid.reshape(3 * columns, depth)
    )
    arrived = lax.all_to_all(outgoing, axes, split_axis=0, concat_axis=0, tiled=True)
    return grains_after, solid.reshape(4, rows_x, rows_y, depth), arrived[None]


def solution(mesh):
    return jax.shard_map(
        per_device,
        mesh=mesh,
        in_specs=(
            P(None, ("stream", "span")),
            P(("stream", "span"), None, None),
            P(("stream", "span"), None),
            P(("stream", "span")),
            P(None, "stream", "span", None),
            P(("stream", "span"), None, None),
            P(("stream", "span"), None),
        ),
        out_specs=(
            P(None, ("stream", "span")),
            P(None, "stream", "span", None),
            P(("stream", "span"), None, None, None, None),
        ),
        check_vma=False,
    )
```

```python
import functools
import math

import jax
import jax.numpy as jnp
from jax import lax
from jax.experimental import pallas as pl
from jax.experimental.pallas import tpu as pltpu
from jax.sharding import PartitionSpec as P

REACH = 3
LANES = 128
RECORD = 16
BATCH = 32

spread_cells = 1.5
drag_rate = 0.25

VMEM = pl.BlockSpec(memory_space=pltpu.VMEM)
HBM = pl.BlockSpec(memory_space=pltpu.HBM)
NT = (((1,), (1,)), ((), ()))
NN = (((1,), (0,)), ((), ()))

QUANT_ROW = (0, 3, 4, 5)
COLUMN_ROW = 6
LEVEL_ROW = 7


def kernel_taps():
    raw = [
        math.exp(-(k * k) / (2.0 * spread_cells * spread_cells)) for k in range(-REACH, REACH + 1)
    ]
    total = sum(raw)
    return [value / total for value in raw]


def params(mib):
    return pltpu.CompilerParams(vmem_limit_bytes=mib * 2**20)


def cost(micros):
    return pl.CostEstimate(flops=0, bytes_accessed=int(micros * 3.0e6), transcendentals=0)


def split(values, size):
    if size & (size - 1):
        return lax.div(values, size), lax.rem(values, size)
    return lax.shift_right_logical(values, size.bit_length() - 1), lax.bitwise_and(values, size - 1)


def halves(values):
    high = values.astype(jnp.bfloat16)
    return high, (values - high.astype(jnp.float32)).astype(jnp.bfloat16)


def dot(left, right, dims=NN):
    return lax.dot_general(left, right, dims, preferred_element_type=jnp.float32)


def wide(values):
    return jnp.broadcast_to(values, (16, LANES)).astype(jnp.bfloat16)


def lane_tile(i):
    return pl.ds(pl.multiple_of(i * LANES, LANES), LANES)


def in_hbm(*values):
    return tuple(pltpu.with_memory_space_constraint(value, pltpu.HBM) for value in values)


def is_odd(axis):
    return lax.rem(lax.axis_index(axis), 2)


def leave_kernel(
    rows_x, rows_y, grains_hbm, slots_hbm, counts_hbm, cells_hbm, picks_hbm, alive_hbm,
    first_ref, second_ref, depth_ref, stream_ref, span_ref, choose_ref, marks_ref, cells_ref,
    grains_ref, stage, table, picked, slots_v, rows_v, rows_s, counts_s, picks_v, alive_v, sems,
):
    records, slot_count = grains_ref.shape
    width = first_ref.shape[1]
    rows = table.shape[0]
    parts = -(-slot_count // rows)
    sources = (grains_hbm, slots_hbm, counts_hbm, picks_hbm, alive_hbm, cells_hbm)
    targets = (grains_ref, slots_v, counts_s, picks_v, alive_v, cells_ref)
    copies = [
        pltpu.make_async_copy(source, target, sems.at[i])
        for i, (source, target) in enumerate(zip(sources, targets))
    ]
    for copy in copies:
        copy.start()
    build_operators(rows_x, rows_y, depth_ref, stream_ref, span_ref)
    copies[1].wait()
    rows_v[...] = lax.bitwise_and(slots_v[...], table.shape[0] - 1)
    copies.append(pltpu.make_async_copy(rows_v, rows_s, sems.at[len(copies)]))
    copies[-1].start()
    copies[0].wait()

    for part in range(parts):
        size = min(rows, slot_count - part * rows)
        here = slice(part * rows, part * rows + size)
        stage[part * RECORD:part * RECORD + 8, 0:size] = grains_ref[0:8, here]
        stage[part * RECORD + 8:part * RECORD + records, 0:size] = grains_ref[8:records, here]
    for block in range(rows // LANES):
        here = slice(block * LANES, (block + 1) * LANES)
        table[here, :] = jnp.transpose(stage[:, here])
    for copy in copies[2:]:
        copy.wait()
    build_choice(picks_v, alive_v, choose_ref)
    for which in (0, 1):
        live = lax.broadcasted_iota(jnp.int32, (1, width), 1) < counts_s[0, which]
        marks_ref[which:which + 1, :] = jnp.where(live, slots_v[which:which + 1, :], -1)

    run = picked.shape[0]
    lane = lax.broadcasted_iota(jnp.int32, (8, LANES), 1)
    odd = is_odd("stream")
    for which in (0, 1):
        live_count = counts_s[0, which]

        def put(lanes, rows_to, value):
            @pl.when(odd == which)
            def _():
                first_ref[rows_to, lanes] = value

            @pl.when(odd != which)
            def _():
                second_ref[rows_to, lanes] = value

        def gather(i, carry):
            base = i * run
            for k in range(0, run, BATCH):
                found = [rows_s[which, base + k + n] for n in range(BATCH)]
                found = [table[pl.ds(row, 1), :] for row in found]
                for n in range(BATCH):
                    picked[k + n:k + n + 1, :] = found[n]
            heads, rests = [], []
            for piece in range(run // LANES):
                lanes = pl.ds(pl.multiple_of(base + piece * LANES, LANES), LANES)
                turned = jnp.transpose(picked[piece * LANES:(piece + 1) * LANES, :])
                slot = jnp.broadcast_to(slots_v[which:which + 1, lanes], (8, LANES))
                part_of = lax.shift_right_logical(slot, rows.bit_length() - 1)
                live = lane + (base + piece * LANES) < live_count
                first = jnp.zeros((8, LANES), jnp.float32)
                second = first
                for part in range(parts):
                    hit = jnp.logical_and(live, part_of == part)
                    first = jnp.where(hit, turned[part * RECORD:part * RECORD + 8], first)
                    second = jnp.where(hit, turned[part * RECORD + 8:part * RECORD + 16], second)
                heads.append(first)
                rests.append(second[0:records - 8])
            lanes = pl.ds(pl.multiple_of(base, LANES), run)
            put(lanes, slice(0, 8), jnp.concatenate(heads, axis=1))
            put(lanes, slice(8, records), jnp.concatenate(rests, axis=1))
            return carry

        used = lax.div(live_count + (run - 1), run)
        lax.fori_loop(0, used, gather, 0)

        def blank(i, carry):
            lanes = pl.ds(pl.multiple_of(i * run, LANES), run)
            put(lanes, slice(0, records), jnp.zeros((records, run), jnp.float32))
            return carry

        lax.fori_loop(used, width // run, blank, 0)


def leave(grains, slots, counts, cells, picks, alive, rows_x, rows_y, depth):
    records, slot_count = grains.shape
    width = slots.shape[1]
    columns = rows_x * rows_y
    rows = max(LANES, 1 << (-(-slot_count // 8) - 1).bit_length())
    run = 2 * LANES if width % (2 * LANES) == 0 else LANES
    out = jax.ShapeDtypeStruct((records, width), jnp.float32)
    bf16 = jnp.bfloat16
    return pl.pallas_call(
        functools.partial(leave_kernel, rows_x, rows_y),
        out_shape=(
            out,
            out,
            jax.ShapeDtypeStruct((2, depth, depth), bf16),
            jax.ShapeDtypeStruct((2, columns, columns + 2 * REACH * rows_y), bf16),
            jax.ShapeDtypeStruct((2, columns, columns + 2 * REACH * rows_x), bf16),
            jax.ShapeDtypeStruct((picks.size, columns), bf16),
            jax.ShapeDtypeStruct(slots.shape, jnp.int32),
            jax.ShapeDtypeStruct(cells.shape, jnp.int32),
        ),
        in_specs=[HBM] * 6,
        out_specs=(VMEM,) * 8,
        scratch_shapes=[
            pltpu.VMEM(grains.shape, jnp.float32),
            pltpu.VMEM((LANES, rows), jnp.float32),
            pltpu.VMEM((rows, LANES), jnp.float32),
            pltpu.VMEM((run, LANES), jnp.float32),
            pltpu.VMEM(slots.shape, jnp.int32),
            pltpu.VMEM(slots.shape, jnp.int32),
            pltpu.SMEM(slots.shape, jnp.int32),
            pltpu.SMEM(counts.shape, jnp.int32),
            pltpu.VMEM(picks.shape, jnp.int32),
            pltpu.VMEM(alive.shape, jnp.int32),
            pltpu.SemaphoreType.DMA((7,)),
        ],
        compiler_params=params(16),
        cost_estimate=cost(8),
        name="leave",
    )(*in_hbm(grains, slots, counts, cells, picks, alive))


def weights_at(apart):
    taps = kernel_taps()[REACH:]
    apart = jnp.abs(apart)
    value = jnp.where(apart == 0, taps[0], 0.0)
    for k in range(1, REACH + 1):
        value = jnp.where(apart == k, taps[k], value)
    return value


def put_operator(out_ref, start, value):
    high, low = halves(value)
    stop = start + value.shape[1]
    out_ref[0, :, start:stop] = high
    out_ref[1, :, start:stop] = low


def build_choice(picks_ref, alive_ref, choose_ref):
    rows_q, peers = picks_ref.shape
    slots, columns = choose_ref.shape
    alive = lax.broadcasted_iota(jnp.int32, (rows_q, peers), 0) < alive_ref[...]
    picks = jnp.where(alive, picks_ref[...], -1).astype(jnp.float32).astype(jnp.bfloat16)
    place_e, _ = split(lax.broadcasted_iota(jnp.int32, (slots, peers), 0), rows_q)
    here = place_e == lax.broadcasted_iota(jnp.int32, (slots, peers), 1)
    named = dot(jnp.where(here, 1.0, 0.0).astype(jnp.bfloat16), picks, NT)
    _, place_q = split(lax.broadcasted_iota(jnp.int32, (slots, rows_q), 0), rows_q)
    mine = place_q == lax.broadcasted_iota(jnp.int32, (slots, rows_q), 1)
    named = jnp.sum(jnp.where(mine, named, 0.0), axis=1, keepdims=True)
    hit = named == lax.broadcasted_iota(jnp.int32, (slots, columns), 1).astype(jnp.float32)
    choose_ref[...] = jnp.where(hit, 1.0, 0.0).astype(jnp.bfloat16)


def build_operators(rows_x, rows_y, depth_ref, stream_ref, span_ref):
    columns = rows_x * rows_y
    depth = depth_ref.shape[1]
    target = lax.broadcasted_iota(jnp.int32, (depth, depth), 0)
    source = lax.broadcasted_iota(jnp.int32, (depth, depth), 1)
    put_operator(depth_ref, 0, weights_at(target - source))

    own = (columns, columns)
    target_y, target_x = split(lax.broadcasted_iota(jnp.int32, own, 0), rows_x)
    row, source_x = split(lax.broadcasted_iota(jnp.int32, own, 1), rows_x)
    source_y = jnp.where(row < REACH, row, jnp.where(row < 2 * REACH, row + rows_y - 2 * REACH, row - REACH))
    put_operator(span_ref, 0, jnp.where(target_x == source_x, weights_at(target_y - source_y), 0.0))
    side = (columns, 2 * REACH * rows_x)
    target_y, target_x = split(lax.broadcasted_iota(jnp.int32, side, 0), rows_x)
    row, source_x = split(lax.broadcasted_iota(jnp.int32, side, 1), rows_x)
    source_y = jnp.where(row < REACH, row - REACH, row - REACH + rows_y)
    put_operator(span_ref, columns, jnp.where(target_x == source_x, weights_at(target_y - source_y), 0.0))

    target_x, target_y = split(lax.broadcasted_iota(jnp.int32, own, 0), rows_y)
    source_y, source_x = split(lax.broadcasted_iota(jnp.int32, own, 1), rows_x)
    put_operator(stream_ref, 0, jnp.where(target_y == source_y, weights_at(target_x - source_x), 0.0))
    side = (columns, 2 * REACH * rows_y)
    target_x, target_y = split(lax.broadcasted_iota(jnp.int32, side, 0), rows_y)
    plane, source_y = split(lax.broadcasted_iota(jnp.int32, side, 1), rows_y)
    source_x = jnp.where(plane < REACH, plane - REACH, plane - REACH + rows_x)
    put_operator(stream_ref, columns, jnp.where(target_y == source_y, weights_at(target_x - source_x), 0.0))


def row_of(y, rows_y):
    return jnp.where(y < REACH, y, jnp.where(y < rows_y - REACH, y + REACH, y - (rows_y - 2 * REACH)))


def keep_kernel(
    rows_x, rows_y, depth, grains_ref, marks_ref, cells_ref, after_hbm, quant_ref,
    high_rows, low_rows, gone, kept, sems,
):
    records, slot_count = grains_ref.shape
    total = quant_ref.shape[1]
    width = marks_ref.shape[1]
    tiles = slot_count // LANES
    pieces = sems.shape[0]

    row16 = lax.broadcasted_iota(jnp.int32, (16, LANES), 0).astype(jnp.float32)
    zero = jnp.zeros((16, LANES), jnp.bfloat16)
    one = jnp.ones((16, LANES), jnp.bfloat16)
    for which in (0, 1):

        def put(i, carry):
            lanes = lane_tile(i)
            to = pl.ds(pl.multiple_of(which * width + i * LANES, LANES), LANES)
            mark = marks_ref[which:which + 1, lanes]
            tile_of, lane_of = split(mark, LANES)
            tile_of = jnp.where(mark < 0, -1, tile_of)
            tile_of = wide(tile_of.astype(jnp.float32))
            lane_of = wide(lane_of.astype(jnp.float32))
            for k in range(high_rows.shape[0] // 16):
                hit = (row16 + 16.0 * k).astype(jnp.bfloat16) == tile_of
                high_rows[16 * k:16 * k + 16, to] = jnp.where(hit, one, zero)
            for k in range(LANES // 16):
                hit = (row16 + 16.0 * k).astype(jnp.bfloat16) == lane_of
                low_rows[16 * k:16 * k + 16, to] = jnp.where(hit, one, zero)
            return carry

        lax.fori_loop(0, width // LANES, put, 0, unroll=8)
    gone[...] = dot(high_rows[...], low_rows[...], NT)

    def place(cell):
        x, rest = split(cell, rows_y * depth)
        y, level = split(rest, depth)
        return (row_of(y, rows_y) * rows_x + x).astype(jnp.float32), level.astype(jnp.float32)

    block = math.gcd(math.gcd(slot_count, total - slot_count), 16 * LANES)

    def table(head, volume, start):
        row8 = lax.broadcasted_iota(jnp.int32, (8, block), 0)
        col, lev = place(cells_ref[:, pl.ds(start, block)])
        value = jnp.where(row8 == QUANT_ROW[0], volume, volume * head)
        value = jnp.where(row8 == COLUMN_ROW, col, value)
        return jnp.where(row8 == LEVEL_ROW, lev, value)

    def keep(i, carry):
        start = pl.multiple_of(i * block, block)
        lanes = pl.ds(start, block)
        first = i * (block // LANES)
        stay = [1.0 - gone[pl.ds(first + n, 1), :] for n in range(block // LANES)]
        stay = jnp.concatenate(stay, axis=1)
        head = grains_ref[0:8, lanes] * stay
        rest = grains_ref[8:records, lanes] * stay
        radius = rest[1:2]
        value = table(head, 4.18879 * (radius * radius * radius), start)
        kept[0:8, lanes] = head
        kept[8:records, lanes] = rest
        quant_ref[:, lanes] = value
        return carry

    writes = []
    blocks = slot_count // block
    for n in range(pieces):
        first = blocks * n // pieces
        last = blocks * (n + 1) // pieces
        lax.fori_loop(first, last, keep, 0)
        here = pl.ds(first * block, (last - first) * block)
        writes.append(pltpu.make_async_copy(kept.at[:, here], after_hbm.at[:, here], sems.at[n]))
        writes[n].start()

    def arrivals(i, carry):
        start = pl.multiple_of(i * block, block)
        none = jnp.zeros((8, block), jnp.float32)
        quant_ref[:, pl.ds(start, block)] = table(none, none[0:1], start)
        return carry

    lax.fori_loop(blocks, total // block, arrivals, 0)
    for write in writes:
        write.wait()


def keep(grains, marks, cells, rows_x, rows_y, depth):
    records, slot_count = grains.shape
    total = cells.shape[1]
    rows = -(-(slot_count // LANES) // 16) * 16
    f32, bf16 = jnp.float32, jnp.bfloat16
    return pl.pallas_call(
        functools.partial(keep_kernel, rows_x, rows_y, depth),
        out_shape=(jax.ShapeDtypeStruct((records, total), f32), jax.ShapeDtypeStruct((8, total), f32)),
        in_specs=[VMEM] * 3,
        out_specs=(HBM, VMEM),
        scratch_shapes=[
            pltpu.VMEM((rows, 2 * marks.shape[1]), bf16),
            pltpu.VMEM((LANES, 2 * marks.shape[1]), bf16),
            pltpu.VMEM((rows, LANES), f32),
            pltpu.VMEM(grains.shape, f32),
            pltpu.SemaphoreType.DMA((4,)),
        ],
        compiler_params=params(20),
        cost_estimate=cost(4),
        name="keep",
    )(grains, marks, cells)


def join_kernel(after_in, quant_in, first_ref, second_ref, earlier_ref, after_ref, quant_ref, sems):
    records, width = first_ref.shape
    start = after_ref.shape[1] - 2 * width
    block = math.gcd(math.gcd(width, start), 16 * LANES)
    row8 = lax.broadcasted_iota(jnp.int32, (8, block), 0)
    odd = is_odd("stream")
    copies = []
    for n, arrived in enumerate((first_ref, second_ref)):
        place = pl.multiple_of(start + (1 - odd if n == 0 else odd) * width, LANES)
        to = after_ref.at[:, pl.ds(place, width)]
        copies.append(pltpu.make_async_copy(arrived, to, sems.at[n]))
        copies[n].start()
    for n, arrived in enumerate((first_ref, second_ref)):

        def step(i, carry):
            lanes = pl.ds(pl.multiple_of(i * block, block), block)
            place = start + (1 - odd if n == 0 else odd) * width
            to = pl.ds(pl.multiple_of(place + i * block, block), block)
            head = arrived[0:8, lanes]
            radius = arrived[9:10, lanes]
            volume = 4.18879 * (radius * radius * radius)
            value = jnp.where(row8 == QUANT_ROW[0], volume, volume * head)
            quant_ref[:, to] = jnp.where(row8 >= COLUMN_ROW, quant_in[:, to], value)
            return carry

        lax.fori_loop(0, width // block, step, 0)
    for copy in copies:
        copy.wait()


def join(after, quant, first, second, earlier):
    return pl.pallas_call(
        join_kernel,
        out_shape=(
            jax.ShapeDtypeStruct(after.shape, after.dtype),
            jax.ShapeDtypeStruct(quant.shape, quant.dtype),
        ),
        in_specs=[HBM, VMEM, VMEM, VMEM, pl.BlockSpec(memory_space=pl.ANY)],
        out_specs=(HBM, VMEM),
        scratch_shapes=[pltpu.SemaphoreType.DMA((2,))],
        input_output_aliases={0: 0, 1: 1},
        compiler_params=params(16),
        cost_estimate=cost(1),
        name="join",
    )(*in_hbm(after), quant, first, second, earlier)


def deposit_kernel(base, chunk, span, begins, ends, edges, quant_ref, *refs):
    refs = list(refs)
    partial_ref = None if begins else refs.pop(0)
    depth_ref = refs.pop(0) if ends else None
    field_ref = refs[0]
    begin, end = span
    left_a, left_b, right_a, right_b, now_a, now_b, total = refs[-7:]
    channels = len(QUANT_ROW)
    columns = field_ref.shape[0] // channels
    depth = field_ref.shape[1]
    row16 = lax.broadcasted_iota(jnp.int32, (16, LANES), 0).astype(jnp.float32)
    zero = jnp.zeros((16, LANES), jnp.bfloat16)
    one = jnp.ones((16, LANES), jnp.bfloat16)
    total[...] = jnp.zeros_like(total) if begins else partial_ref[...]

    def build(left, right, now, step):
        now[...] = quant_ref[:, pl.ds(pl.multiple_of(step * chunk, chunk), chunk)]
        for j in range(chunk // LANES):
            here = slice(j * LANES, (j + 1) * LANES)
            parts = [wide(now[r:r + 1, here]) for r in QUANT_ROW]
            column = wide(now[COLUMN_ROW:COLUMN_ROW + 1, here])
            level = wide(now[LEVEL_ROW:LEVEL_ROW + 1, here])
            for k in range(columns // 16):
                hit = (row16 + (base + 16.0 * k)).astype(jnp.bfloat16) == column
                for c in range(channels):
                    left[c * columns + 16 * k:c * columns + 16 * k + 16, here] = jnp.where(hit, parts[c], zero)
            for k in range(depth // 16):
                hit = (row16 + 16.0 * k).astype(jnp.bfloat16) == level
                right[16 * k:16 * k + 16, here] = jnp.where(hit, one, zero)

    build(left_a, right_a, now_a, begin)

    def two(i, carry):
        now = begin + 2 * i
        build(left_b, right_b, now_b, now + 1)
        total[...] += dot(left_a[...], right_a[...], NT)
        build(left_a, right_a, now_a, jnp.minimum(now + 2, end - 1))
        total[...] += dot(left_b[...], right_b[...], NT)
        return carry

    lax.fori_loop(0, (end - begin) // 2, two, 0)
    if (end - begin) % 2:
        total[...] += dot(left_a[...], right_a[...], NT)

    if not ends:
        field_ref[...] = total[...]
        return
    high, low = halves(total[...])
    field_ref[...] = dot(high, depth_ref[0]) + (dot(high, depth_ref[1]) + dot(low, depth_ref[0]))
    if edges:
        first_ref, second_ref = refs[1:3]
        edge = columns // 2
        odd = is_odd("span")
        for c in range(channels):
            to = slice(c * edge, (c + 1) * edge)
            front = c * columns + (1 - odd) * edge
            back = c * columns + odd * edge
            first_ref[to, :] = field_ref[pl.ds(pl.multiple_of(front, 8), edge), :]
            second_ref[to, :] = field_ref[pl.ds(pl.multiple_of(back, 8), edge), :]


def deposit(base, columns, depth, chunk, span, edges, quant, partial=None, depth_op=None):
    channels = len(QUANT_ROW)
    begins, ends = partial is None, depth_op is not None
    field = jax.ShapeDtypeStruct((channels * columns, depth), jnp.float32)
    edge = jax.ShapeDtypeStruct((channels * columns // 2, depth), jnp.float32)
    operands = [quant] + ([] if begins else [partial]) + ([depth_op] if ends else [])
    outs = (field, edge, edge) if edges else (field,)
    left = pltpu.VMEM((channels * columns, chunk), jnp.bfloat16)
    right = pltpu.VMEM((depth, chunk), jnp.bfloat16)
    now = pltpu.VMEM((8, chunk), jnp.float32)
    return pl.pallas_call(
        functools.partial(deposit_kernel, base, chunk, span, begins, ends, edges),
        out_shape=outs,
        in_specs=[VMEM] * len(operands),
        out_specs=(VMEM,) * len(outs),
        scratch_shapes=[left, left, right, right, now, now, pltpu.VMEM(field.shape, jnp.float32)],
        compiler_params=params(28),
        cost_estimate=cost(columns * 0.006 * (span[1] - span[0])),
        name="deposit",
    )(*operands)


def mix(operator_ref, start, piece):
    take = slice(start, start + piece.shape[0])
    high, low = halves(piece)
    return dot(operator_ref[0, :, take], high) + (
        dot(operator_ref[1, :, take], high) + dot(operator_ref[0, :, take], low)
    )


def own_kernel(operator_ref, *refs):
    channels = len(QUANT_ROW)
    part_ref = refs[-1]
    columns = part_ref.shape[0] // channels
    for c in range(channels):
        start, value = 0, None
        for ref in refs[:-1]:
            size = ref.shape[0] // channels
            piece = mix(operator_ref, start, ref[c * size:(c + 1) * size, :])
            value = piece if value is None else value + piece
            start += size
        part_ref[c * columns:(c + 1) * columns, :] = value


def own_part(operator, *fields):
    rows = sum(field.shape[0] for field in fields)
    return pl.pallas_call(
        own_kernel,
        out_shape=jax.ShapeDtypeStruct((rows, fields[0].shape[1]), jnp.float32),
        in_specs=[VMEM] * (1 + len(fields)),
        out_specs=VMEM,
        compiler_params=params(12),
        cost_estimate=cost(1),
        name="own_part",
    )(operator, *fields)


def sides(axis, first, second):
    odd = is_odd(axis) == 1
    return jnp.concatenate([jnp.where(odd, first, second), jnp.where(odd, second, first)], axis=0)


def span_kernel(rows_x, rows_y, part_ref, first_in, second_in, operator_ref, field_ref, first_ref, second_ref):
    channels = len(QUANT_ROW)
    columns = rows_x * rows_y
    halo = first_in.shape[0] // channels
    odd = is_odd("stream")
    first_x = (1 - odd) * (rows_x - REACH)
    second_x = odd * (rows_x - REACH)
    for c in range(channels):
        own = slice(c * columns, (c + 1) * columns)
        side = slice(c * halo, (c + 1) * halo)
        field_ref[own, :] = part_ref[own, :] + mix(
            operator_ref, columns, sides("span", first_in[side, :], second_in[side, :])
        )
    for c in range(channels):
        for k in range(REACH):
            for y in range(rows_y):
                to = (c * REACH + k) * rows_y + y
                row = c * columns + y * rows_x + k
                first_ref[to:to + 1, :] = field_ref[pl.ds(row + first_x, 1), :]
                second_ref[to:to + 1, :] = field_ref[pl.ds(row + second_x, 1), :]


def span_pass(rows_x, rows_y, part, first, second, operator):
    channels = len(QUANT_ROW)
    depth = part.shape[1]
    halo = jax.ShapeDtypeStruct((channels * REACH * rows_y, depth), jnp.float32)
    return pl.pallas_call(
        functools.partial(span_kernel, rows_x, rows_y),
        out_shape=(jax.ShapeDtypeStruct((channels * rows_x * rows_y, depth), jnp.float32), halo, halo),
        in_specs=[VMEM] * 4,
        out_specs=(VMEM,) * 3,
        compiler_params=params(12),
        cost_estimate=cost(1),
        name="span_pass",
    )(part, first, second, operator)


def stream_kernel(
    rows_q, part_ref, first_in, second_in, operator_ref, choose_ref, fluid_ref, solid_hbm, out_ref, solid_ref, sems
):
    channels = len(QUANT_ROW)
    columns = part_ref.shape[0] // channels
    halo = first_in.shape[0] // channels
    choose = choose_ref[...]
    copies = []
    for c in range(channels):
        own = slice(c * columns, (c + 1) * columns)
        side = slice(c * halo, (c + 1) * halo)
        solid_ref[own, :] = part_ref[own, :] + mix(
            operator_ref, columns, sides("stream", first_in[side, :], second_in[side, :])
        )
        copies.append(pltpu.make_async_copy(solid_ref.at[own, :], solid_hbm.at[own, :], sems.at[c]))
        copies[c].start()
    base = solid_ref[0:columns, :]
    for c in range(channels):
        if c == 0:
            value = 1.0 / (1.0 + base)
        else:
            flow = fluid_ref[(c - 1) * columns:c * columns, :]
            value = flow + drag_rate * (solid_ref[c * columns:(c + 1) * columns, :] - base * flow)
        first, rest = halves(value)
        second, third = halves(value - first.astype(jnp.float32))
        sent = dot(choose, first) + (dot(choose, second) + dot(choose, third))
        place = (c - 1) % channels
        out_ref[:, :, place, :] = sent.reshape(sent.shape[0] // rows_q, rows_q, -1)
    for copy in copies:
        copy.wait()


def stream_pass(peers, rows_q, part, first, second, operator, choose, fluid):
    channels = len(QUANT_ROW)
    depth = part.shape[1]
    return pl.pallas_call(
        functools.partial(stream_kernel, rows_q),
        out_shape=(
            jax.ShapeDtypeStruct(part.shape, jnp.float32),
            jax.ShapeDtypeStruct((peers, rows_q, channels, depth), jnp.float32),
        ),
        in_specs=[VMEM] * 6,
        out_specs=(HBM, VMEM),
        scratch_shapes=[pltpu.VMEM(part.shape, jnp.float32), pltpu.SemaphoreType.DMA((channels,))],
        compiler_params=params(16),
        cost_estimate=cost(2),
        name="stream_pass",
    )(part, first, second, operator, choose, fluid)


def swap_first(value, axis):
    count = lax.axis_size(axis)
    assert count % 2 == 0
    return lax.ppermute(value, axis, [(source, source ^ 1) for source in range(count)])


def swap_second(value, axis, periodic):
    count = lax.axis_size(axis)
    pairs = [(source, (source + 1 if source % 2 else source - 1) % count) for source in range(count)]
    if not periodic:
        pairs = [pair for pair in pairs if abs(pair[0] - pair[1]) == 1]
    return lax.ppermute(value, axis, pairs)


def swap(first, second, axis, periodic):
    return swap_first(first, axis), swap_second(second, axis, periodic)


def per_device(grains, send_slots, send_counts, cell_index, fluid, block_slots, block_counts):
    rows_x, rows_y, depth = fluid.shape[1:]
    columns = rows_x * rows_y
    width = send_slots.shape[2]
    peers, rows_q = block_slots.shape[1:]
    total = cell_index.shape[0]
    axes = ("stream", "span")

    first, second, depth_op, stream_op, span_op, choose, marks, cells = leave(
        grains, send_slots[0], send_counts, cell_index.reshape(1, -1), block_slots[0].T, block_counts,
        rows_x, rows_y, depth,
    )
    first = swap_first(first, "stream")
    after, quant = keep(grains, marks, cells, rows_x, rows_y, depth)
    second, quant = lax.optimization_barrier((second, quant))
    second = swap_second(second, "stream", True)

    chunk = math.gcd(math.gcd(grains.shape[1], 2 * width), 4096)
    steps = total // chunk
    kept = grains.shape[1] // chunk
    faces = 2 * REACH * rows_x
    (partial,) = deposit(0, faces, depth, chunk, (0, kept), False, quant)
    grains_after, quant = join(after, quant, first, second, partial)
    edge, first, second = deposit(0, faces, depth, chunk, (kept, steps), True, quant, partial, depth_op)
    first, second = swap(first, second, "span", False)
    (inner,) = deposit(faces, columns - faces, depth, chunk, (0, steps), False, quant, None, depth_op)
    part = own_part(span_op, edge, inner)
    field, *halos = span_pass(rows_x, rows_y, part, first, second, span_op)
    halos = swap(*halos, "stream", True)
    part = own_part(stream_op, field)
    solid, outgoing = stream_pass(
        peers, rows_q, part, *halos, stream_op, choose, fluid.reshape(3 * columns, depth)
    )
    arrived = lax.all_to_all(outgoing, axes, split_axis=0, concat_axis=0, tiled=True)
    return grains_after, solid.reshape(4, rows_x, rows_y, depth), arrived[None]


def solution(mesh):
    return jax.shard_map(
        per_device,
        mesh=mesh,
        in_specs=(
            P(None, ("stream", "span")),
            P(("stream", "span"), None, None),
            P(("stream", "span"), None),
            P(("stream", "span")),
            P(None, "stream", "span", None),
            P(("stream", "span"), None, None),
            P(("stream", "span"), None),
        ),
        out_specs=(
            P(None, ("stream", "span")),
            P(None, "stream", "span", None),
            P(("stream", "span"), None, None, None, None),
        ),
        check_vma=False,
    )
```

```python
import functools
import math

import jax
import jax.numpy as jnp
from jax import lax
from jax.experimental import pallas as pl
from jax.experimental.pallas import tpu as pltpu
from jax.sharding import PartitionSpec as P

REACH = 3
LANES = 128
RECORD = 16
BATCH = 32

spread_cells = 1.5
drag_rate = 0.25

VMEM = pl.BlockSpec(memory_space=pltpu.VMEM)
HBM = pl.BlockSpec(memory_space=pltpu.HBM)
NT = (((1,), (1,)), ((), ()))
NN = (((1,), (0,)), ((), ()))

QUANT_ROW = (0, 3, 4, 5)
COLUMN_ROW = 6
LEVEL_ROW = 7


def kernel_taps():
    raw = [
        math.exp(-(k * k) / (2.0 * spread_cells * spread_cells)) for k in range(-REACH, REACH + 1)
    ]
    total = sum(raw)
    return [value / total for value in raw]


def params(mib):
    return pltpu.CompilerParams(vmem_limit_bytes=mib * 2**20)


def cost(micros):
    return pl.CostEstimate(flops=0, bytes_accessed=int(micros * 3.0e6), transcendentals=0)


def split(values, size):
    if size & (size - 1):
        return lax.div(values, size), lax.rem(values, size)
    return lax.shift_right_logical(values, size.bit_length() - 1), lax.bitwise_and(values, size - 1)


def halves(values):
    high = values.astype(jnp.bfloat16)
    return high, (values - high.astype(jnp.float32)).astype(jnp.bfloat16)


def dot(left, right, dims=NN):
    return lax.dot_general(left, right, dims, preferred_element_type=jnp.float32)


def wide(values):
    return jnp.broadcast_to(values, (16, LANES)).astype(jnp.bfloat16)


def lane_tile(i):
    return pl.ds(pl.multiple_of(i * LANES, LANES), LANES)


def in_hbm(*values):
    return tuple(pltpu.with_memory_space_constraint(value, pltpu.HBM) for value in values)


def is_odd(axis):
    return lax.rem(lax.axis_index(axis), 2)


def leave_kernel(
    rows_x, rows_y, grains_hbm, slots_hbm, counts_hbm, cells_hbm, picks_hbm, alive_hbm,
    first_ref, second_ref, depth_ref, stream_ref, span_ref, choose_ref, marks_ref, cells_ref,
    grains_ref, stage, table, picked, slots_v, rows_v, rows_s, counts_s, picks_v, alive_v, sems,
):
    records, slot_count = grains_ref.shape
    width = first_ref.shape[1]
    rows = table.shape[0]
    parts = -(-slot_count // rows)
    sources = (grains_hbm, slots_hbm, counts_hbm, picks_hbm, alive_hbm, cells_hbm)
    targets = (grains_ref, slots_v, counts_s, picks_v, alive_v, cells_ref)
    copies = [
        pltpu.make_async_copy(source, target, sems.at[i])
        for i, (source, target) in enumerate(zip(sources, targets))
    ]
    for copy in copies:
        copy.start()
    build_operators(rows_x, rows_y, depth_ref, stream_ref, span_ref)
    copies[1].wait()
    rows_v[...] = lax.bitwise_and(slots_v[...], table.shape[0] - 1)
    copies.append(pltpu.make_async_copy(rows_v, rows_s, sems.at[len(copies)]))
    copies[-1].start()
    copies[0].wait()

    for part in range(parts):
        size = min(rows, slot_count - part * rows)
        here = slice(part * rows, part * rows + size)
        stage[part * RECORD:part * RECORD + 8, 0:size] = grains_ref[0:8, here]
        stage[part * RECORD + 8:part * RECORD + records, 0:size] = grains_ref[8:records, here]
    for block in range(rows // LANES):
        here = slice(block * LANES, (block + 1) * LANES)
        table[here, :] = jnp.transpose(stage[:, here])
    for copy in copies[2:]:
        copy.wait()
    build_choice(picks_v, alive_v, choose_ref)
    for which in (0, 1):
        live = lax.broadcasted_iota(jnp.int32, (1, width), 1) < counts_s[0, which]
        marks_ref[which:which + 1, :] = jnp.where(live, slots_v[which:which + 1, :], -1)

    run = picked.shape[0]
    lane = lax.broadcasted_iota(jnp.int32, (8, LANES), 1)
    odd = is_odd("stream")
    for which in (0, 1):
        live_count = counts_s[0, which]

        def put(lanes, rows_to, value):
            @pl.when(odd == which)
            def _():
                first_ref[rows_to, lanes] = value

            @pl.when(odd != which)
            def _():
                second_ref[rows_to, lanes] = value

        def gather(i, carry):
            base = i * run
            for k in range(0, run, BATCH):
                found = [rows_s[which, base + k + n] for n in range(BATCH)]
                found = [table[pl.ds(row, 1), :] for row in found]
                for n in range(BATCH):
                    picked[k + n:k + n + 1, :] = found[n]
            heads, rests = [], []
            for piece in range(run // LANES):
                lanes = pl.ds(pl.multiple_of(base + piece * LANES, LANES), LANES)
                turned = jnp.transpose(picked[piece * LANES:(piece + 1) * LANES, :])
                slot = jnp.broadcast_to(slots_v[which:which + 1, lanes], (8, LANES))
                part_of = lax.shift_right_logical(slot, rows.bit_length() - 1)
                live = lane + (base + piece * LANES) < live_count
                first = jnp.zeros((8, LANES), jnp.float32)
                second = first
                for part in range(parts):
                    hit = jnp.logical_and(live, part_of == part)
                    first = jnp.where(hit, turned[part * RECORD:part * RECORD + 8], first)
                    second = jnp.where(hit, turned[part * RECORD + 8:part * RECORD + 16], second)
                heads.append(first)
                rests.append(second[0:records - 8])
            lanes = pl.ds(pl.multiple_of(base, LANES), run)
            put(lanes, slice(0, 8), jnp.concatenate(heads, axis=1))
            put(lanes, slice(8, records), jnp.concatenate(rests, axis=1))
            return carry

        used = lax.div(live_count + (run - 1), run)
        lax.fori_loop(0, used, gather, 0)

        def blank(i, carry):
            lanes = pl.ds(pl.multiple_of(i * run, LANES), run)
            put(lanes, slice(0, records), jnp.zeros((records, run), jnp.float32))
            return carry

        lax.fori_loop(used, width // run, blank, 0)


def leave(grains, slots, counts, cells, picks, alive, rows_x, rows_y, depth):
    records, slot_count = grains.shape
    width = slots.shape[1]
    columns = rows_x * rows_y
    rows = max(LANES, 1 << (-(-slot_count // 8) - 1).bit_length())
    run = 2 * LANES if width % (2 * LANES) == 0 else LANES
    out = jax.ShapeDtypeStruct((records, width), jnp.float32)
    bf16 = jnp.bfloat16
    return pl.pallas_call(
        functools.partial(leave_kernel, rows_x, rows_y),
        out_shape=(
            out,
            out,
            jax.ShapeDtypeStruct((2, depth, depth), bf16),
            jax.ShapeDtypeStruct((2, columns, columns + 2 * REACH * rows_y), bf16),
            jax.ShapeDtypeStruct((2, columns, columns + 2 * REACH * rows_x), bf16),
            jax.ShapeDtypeStruct((picks.size, columns), bf16),
            jax.ShapeDtypeStruct(slots.shape, jnp.int32),
            jax.ShapeDtypeStruct(cells.shape, jnp.int32),
        ),
        in_specs=[HBM] * 6,
        out_specs=(VMEM,) * 8,
        scratch_shapes=[
            pltpu.VMEM(grains.shape, jnp.float32),
            pltpu.VMEM((LANES, rows), jnp.float32),
            pltpu.VMEM((rows, LANES), jnp.float32),
            pltpu.VMEM((run, LANES), jnp.float32),
            pltpu.VMEM(slots.shape, jnp.int32),
            pltpu.VMEM(slots.shape, jnp.int32),
            pltpu.SMEM(slots.shape, jnp.int32),
            pltpu.SMEM(counts.shape, jnp.int32),
            pltpu.VMEM(picks.shape, jnp.int32),
            pltpu.VMEM(alive.shape, jnp.int32),
            pltpu.SemaphoreType.DMA((7,)),
        ],
        compiler_params=params(16),
        cost_estimate=cost(8),
        name="leave",
    )(*in_hbm(grains, slots, counts, cells, picks, alive))


def weights_at(apart):
    taps = kernel_taps()[REACH:]
    apart = jnp.abs(apart)
    value = jnp.where(apart == 0, taps[0], 0.0)
    for k in range(1, REACH + 1):
        value = jnp.where(apart == k, taps[k], value)
    return value


def put_operator(out_ref, start, value):
    high, low = halves(value)
    stop = start + value.shape[1]
    out_ref[0, :, start:stop] = high
    out_ref[1, :, start:stop] = low


def build_choice(picks_ref, alive_ref, choose_ref):
    rows_q, peers = picks_ref.shape
    slots, columns = choose_ref.shape
    alive = lax.broadcasted_iota(jnp.int32, (rows_q, peers), 0) < alive_ref[...]
    picks = jnp.where(alive, picks_ref[...], -1).astype(jnp.float32).astype(jnp.bfloat16)
    place_e, _ = split(lax.broadcasted_iota(jnp.int32, (slots, peers), 0), rows_q)
    here = place_e == lax.broadcasted_iota(jnp.int32, (slots, peers), 1)
    named = dot(jnp.where(here, 1.0, 0.0).astype(jnp.bfloat16), picks, NT)
    _, place_q = split(lax.broadcasted_iota(jnp.int32, (slots, rows_q), 0), rows_q)
    mine = place_q == lax.broadcasted_iota(jnp.int32, (slots, rows_q), 1)
    named = jnp.sum(jnp.where(mine, named, 0.0), axis=1, keepdims=True)
    hit = named == lax.broadcasted_iota(jnp.int32, (slots, columns), 1).astype(jnp.float32)
    choose_ref[...] = jnp.where(hit, 1.0, 0.0).astype(jnp.bfloat16)


def build_operators(rows_x, rows_y, depth_ref, stream_ref, span_ref):
    columns = rows_x * rows_y
    depth = depth_ref.shape[1]
    target = lax.broadcasted_iota(jnp.int32, (depth, depth), 0)
    source = lax.broadcasted_iota(jnp.int32, (depth, depth), 1)
    put_operator(depth_ref, 0, weights_at(target - source))

    own = (columns, columns)
    target_y, target_x = split(lax.broadcasted_iota(jnp.int32, own, 0), rows_x)
    row, source_x = split(lax.broadcasted_iota(jnp.int32, own, 1), rows_x)
    source_y = jnp.where(row < REACH, row, jnp.where(row < 2 * REACH, row + rows_y - 2 * REACH, row - REACH))
    put_operator(span_ref, 0, jnp.where(target_x == source_x, weights_at(target_y - source_y), 0.0))
    side = (columns, 2 * REACH * rows_x)
    target_y, target_x = split(lax.broadcasted_iota(jnp.int32, side, 0), rows_x)
    row, source_x = split(lax.broadcasted_iota(jnp.int32, side, 1), rows_x)
    source_y = jnp.where(row < REACH, row - REACH, row - REACH + rows_y)
    put_operator(span_ref, columns, jnp.where(target_x == source_x, weights_at(target_y - source_y), 0.0))

    target_x, target_y = split(lax.broadcasted_iota(jnp.int32, own, 0), rows_y)
    source_y, source_x = split(lax.broadcasted_iota(jnp.int32, own, 1), rows_x)
    put_operator(stream_ref, 0, jnp.where(target_y == source_y, weights_at(target_x - source_x), 0.0))
    side = (columns, 2 * REACH * rows_y)
    target_x, target_y = split(lax.broadcasted_iota(jnp.int32, side, 0), rows_y)
    plane, source_y = split(lax.broadcasted_iota(jnp.int32, side, 1), rows_y)
    source_x = jnp.where(plane < REACH, plane - REACH, plane - REACH + rows_x)
    put_operator(stream_ref, columns, jnp.where(target_y == source_y, weights_at(target_x - source_x), 0.0))


def row_of(y, rows_y):
    return jnp.where(y < REACH, y, jnp.where(y < rows_y - REACH, y + REACH, y - (rows_y - 2 * REACH)))


def keep_kernel(
    rows_x, rows_y, depth, grains_ref, marks_ref, cells_ref, after_hbm, quant_ref,
    high_rows, low_rows, gone, kept, sems,
):
    records, slot_count = grains_ref.shape
    total = quant_ref.shape[1]
    width = marks_ref.shape[1]
    tiles = slot_count // LANES
    pieces = sems.shape[0]

    row16 = lax.broadcasted_iota(jnp.int32, (16, LANES), 0).astype(jnp.float32)
    zero = jnp.zeros((16, LANES), jnp.bfloat16)
    one = jnp.ones((16, LANES), jnp.bfloat16)
    for which in (0, 1):

        def put(i, carry):
            lanes = lane_tile(i)
            to = pl.ds(pl.multiple_of(which * width + i * LANES, LANES), LANES)
            mark = marks_ref[which:which + 1, lanes]
            tile_of, lane_of = split(mark, LANES)
            tile_of = jnp.where(mark < 0, -1, tile_of)
            tile_of = wide(tile_of.astype(jnp.float32))
            lane_of = wide(lane_of.astype(jnp.float32))
            for k in range(high_rows.shape[0] // 16):
                hit = (row16 + 16.0 * k).astype(jnp.bfloat16) == tile_of
                high_rows[16 * k:16 * k + 16, to] = jnp.where(hit, one, zero)
            for k in range(LANES // 16):
                hit = (row16 + 16.0 * k).astype(jnp.bfloat16) == lane_of
                low_rows[16 * k:16 * k + 16, to] = jnp.where(hit, one, zero)
            return carry

        lax.fori_loop(0, width // LANES, put, 0, unroll=8)
    gone[...] = dot(high_rows[...], low_rows[...], NT)

    def place(cell):
        x, rest = split(cell, rows_y * depth)
        y, level = split(rest, depth)
        return (row_of(y, rows_y) * rows_x + x).astype(jnp.float32), level.astype(jnp.float32)

    block = math.gcd(math.gcd(slot_count, total - slot_count), 16 * LANES)

    def table(head, volume, start):
        row8 = lax.broadcasted_iota(jnp.int32, (8, block), 0)
        col, lev = place(cells_ref[:, pl.ds(start, block)])
        value = jnp.where(row8 == QUANT_ROW[0], volume, volume * head)
        value = jnp.where(row8 == COLUMN_ROW, col, value)
        return jnp.where(row8 == LEVEL_ROW, lev, value)

    def keep(i, carry):
        start = pl.multiple_of(i * block, block)
        lanes = pl.ds(start, block)
        first = i * (block // LANES)
        stay = [1.0 - gone[pl.ds(first + n, 1), :] for n in range(block // LANES)]
        stay = jnp.concatenate(stay, axis=1)
        head = grains_ref[0:8, lanes] * stay
        rest = grains_ref[8:records, lanes] * stay
        radius = rest[1:2]
        value = table(head, 4.18879 * (radius * radius * radius), start)
        kept[0:8, lanes] = head
        kept[8:records, lanes] = rest
        quant_ref[:, lanes] = value
        return carry

    writes = []
    blocks = slot_count // block
    for n in range(pieces):
        first = blocks * n // pieces
        last = blocks * (n + 1) // pieces
        lax.fori_loop(first, last, keep, 0)
        here = pl.ds(first * block, (last - first) * block)
        writes.append(pltpu.make_async_copy(kept.at[:, here], after_hbm.at[:, here], sems.at[n]))
        writes[n].start()

    def arrivals(i, carry):
        start = pl.multiple_of(i * block, block)
        none = jnp.zeros((8, block), jnp.float32)
        quant_ref[:, pl.ds(start, block)] = table(none, none[0:1], start)
        return carry

    lax.fori_loop(blocks, total // block, arrivals, 0)
    for write in writes:
        write.wait()


def keep(grains, marks, cells, rows_x, rows_y, depth):
    records, slot_count = grains.shape
    total = cells.shape[1]
    rows = -(-(slot_count // LANES) // 16) * 16
    f32, bf16 = jnp.float32, jnp.bfloat16
    return pl.pallas_call(
        functools.partial(keep_kernel, rows_x, rows_y, depth),
        out_shape=(jax.ShapeDtypeStruct((records, total), f32), jax.ShapeDtypeStruct((8, total), f32)),
        in_specs=[VMEM] * 3,
        out_specs=(HBM, VMEM),
        scratch_shapes=[
            pltpu.VMEM((rows, 2 * marks.shape[1]), bf16),
            pltpu.VMEM((LANES, 2 * marks.shape[1]), bf16),
            pltpu.VMEM((rows, LANES), f32),
            pltpu.VMEM(grains.shape, f32),
            pltpu.SemaphoreType.DMA((4,)),
        ],
        compiler_params=params(20),
        cost_estimate=cost(4),
        name="keep",
    )(grains, marks, cells)


def join_kernel(after_in, quant_in, first_ref, second_ref, earlier_ref, after_ref, quant_ref, sems):
    records, width = first_ref.shape
    start = after_ref.shape[1] - 2 * width
    block = math.gcd(math.gcd(width, start), 16 * LANES)
    row8 = lax.broadcasted_iota(jnp.int32, (8, block), 0)
    odd = is_odd("stream")
    copies = []
    for n, arrived in enumerate((first_ref, second_ref)):
        place = pl.multiple_of(start + (1 - odd if n == 0 else odd) * width, LANES)
        to = after_ref.at[:, pl.ds(place, width)]
        copies.append(pltpu.make_async_copy(arrived, to, sems.at[n]))
        copies[n].start()
    for n, arrived in enumerate((first_ref, second_ref)):

        def step(i, carry):
            lanes = pl.ds(pl.multiple_of(i * block, block), block)
            place = start + (1 - odd if n == 0 else odd) * width
            to = pl.ds(pl.multiple_of(place + i * block, block), block)
            head = arrived[0:8, lanes]
            radius = arrived[9:10, lanes]
            volume = 4.18879 * (radius * radius * radius)
            value = jnp.where(row8 == QUANT_ROW[0], volume, volume * head)
            quant_ref[:, to] = jnp.where(row8 >= COLUMN_ROW, quant_in[:, to], value)
            return carry

        lax.fori_loop(0, width // block, step, 0)
    for copy in copies:
        copy.wait()


def join(after, quant, first, second, earlier):
    return pl.pallas_call(
        join_kernel,
        out_shape=(
            jax.ShapeDtypeStruct(after.shape, after.dtype),
            jax.ShapeDtypeStruct(quant.shape, quant.dtype),
        ),
        in_specs=[HBM, VMEM, VMEM, VMEM, pl.BlockSpec(memory_space=pl.ANY)],
        out_specs=(HBM, VMEM),
        scratch_shapes=[pltpu.SemaphoreType.DMA((2,))],
        input_output_aliases={0: 0, 1: 1},
        compiler_params=params(16),
        cost_estimate=cost(1),
        name="join",
    )(*in_hbm(after), quant, first, second, earlier)


def deposit_kernel(base, chunk, span, begins, ends, edges, quant_ref, *refs):
    refs = list(refs)
    partial_ref = None if begins else refs.pop(0)
    depth_ref = refs.pop(0) if ends else None
    field_ref = refs[0]
    begin, end = span
    left_a, left_b, right_a, right_b, now_a, now_b, total = refs[-7:]
    channels = len(QUANT_ROW)
    columns = field_ref.shape[0] // channels
    depth = field_ref.shape[1]
    row16 = lax.broadcasted_iota(jnp.int32, (16, LANES), 0).astype(jnp.float32)
    zero = jnp.zeros((16, LANES), jnp.bfloat16)
    one = jnp.ones((16, LANES), jnp.bfloat16)
    total[...] = jnp.zeros_like(total) if begins else partial_ref[...]

    def build(left, right, now, step):
        now[...] = quant_ref[:, pl.ds(pl.multiple_of(step * chunk, chunk), chunk)]
        for j in range(chunk // LANES):
            here = slice(j * LANES, (j + 1) * LANES)
            parts = [wide(now[r:r + 1, here]) for r in QUANT_ROW]
            column = wide(now[COLUMN_ROW:COLUMN_ROW + 1, here])
            level = wide(now[LEVEL_ROW:LEVEL_ROW + 1, here])
            for k in range(columns // 16):
                hit = (row16 + (base + 16.0 * k)).astype(jnp.bfloat16) == column
                for c in range(channels):
                    left[c * columns + 16 * k:c * columns + 16 * k + 16, here] = jnp.where(hit, parts[c], zero)
            for k in range(depth // 16):
                hit = (row16 + 16.0 * k).astype(jnp.bfloat16) == level
                right[16 * k:16 * k + 16, here] = jnp.where(hit, one, zero)

    build(left_a, right_a, now_a, begin)

    def two(i, carry):
        now = begin + 2 * i
        build(left_b, right_b, now_b, now + 1)
        total[...] += dot(left_a[...], right_a[...], NT)
        build(left_a, right_a, now_a, jnp.minimum(now + 2, end - 1))
        total[...] += dot(left_b[...], right_b[...], NT)
        return carry

    lax.fori_loop(0, (end - begin) // 2, two, 0)
    if (end - begin) % 2:
        total[...] += dot(left_a[...], right_a[...], NT)

    if not ends:
        field_ref[...] = total[...]
        return
    high, low = halves(total[...])
    field_ref[...] = dot(high, depth_ref[0]) + (dot(high, depth_ref[1]) + dot(low, depth_ref[0]))
    if edges:
        first_ref, second_ref = refs[1:3]
        edge = columns // 2
        odd = is_odd("span")
        for c in range(channels):
            to = slice(c * edge, (c + 1) * edge)
            front = c * columns + (1 - odd) * edge
            back = c * columns + odd * edge
            first_ref[to, :] = field_ref[pl.ds(pl.multiple_of(front, 8), edge), :]
            second_ref[to, :] = field_ref[pl.ds(pl.multiple_of(back, 8), edge), :]


def deposit(base, columns, depth, chunk, span, edges, quant, partial=None, depth_op=None):
    channels = len(QUANT_ROW)
    begins, ends = partial is None, depth_op is not None
    field = jax.ShapeDtypeStruct((channels * columns, depth), jnp.float32)
    edge = jax.ShapeDtypeStruct((channels * columns // 2, depth), jnp.float32)
    operands = [quant] + ([] if begins else [partial]) + ([depth_op] if ends else [])
    outs = (field, edge, edge) if edges else (field,)
    left = pltpu.VMEM((channels * columns, chunk), jnp.bfloat16)
    right = pltpu.VMEM((depth, chunk), jnp.bfloat16)
    now = pltpu.VMEM((8, chunk), jnp.float32)
    return pl.pallas_call(
        functools.partial(deposit_kernel, base, chunk, span, begins, ends, edges),
        out_shape=outs,
        in_specs=[VMEM] * len(operands),
        out_specs=(VMEM,) * len(outs),
        scratch_shapes=[left, left, right, right, now, now, pltpu.VMEM(field.shape, jnp.float32)],
        compiler_params=params(28),
        cost_estimate=cost(columns * 0.006 * (span[1] - span[0])),
        name="deposit",
    )(*operands)


def mix(operator_ref, start, piece):
    take = slice(start, start + piece.shape[0])
    high, low = halves(piece)
    return dot(operator_ref[0, :, take], high) + (
        dot(operator_ref[1, :, take], high) + dot(operator_ref[0, :, take], low)
    )


def own_kernel(operator_ref, *refs):
    channels = len(QUANT_ROW)
    part_ref = refs[-1]
    columns = part_ref.shape[0] // channels
    for c in range(channels):
        start, value = 0, None
        for ref in refs[:-1]:
            size = ref.shape[0] // channels
            piece = mix(operator_ref, start, ref[c * size:(c + 1) * size, :])
            value = piece if value is None else value + piece
            start += size
        part_ref[c * columns:(c + 1) * columns, :] = value


def own_part(operator, *fields):
    rows = sum(field.shape[0] for field in fields)
    return pl.pallas_call(
        own_kernel,
        out_shape=jax.ShapeDtypeStruct((rows, fields[0].shape[1]), jnp.float32),
        in_specs=[VMEM] * (1 + len(fields)),
        out_specs=VMEM,
        compiler_params=params(12),
        cost_estimate=cost(1),
        name="own_part",
    )(operator, *fields)


def sides(axis, first, second):
    odd = is_odd(axis) == 1
    return jnp.concatenate([jnp.where(odd, first, second), jnp.where(odd, second, first)], axis=0)


def span_kernel(rows_x, rows_y, part_ref, second_in, first_in, operator_ref, field_ref, first_ref, second_ref):
    channels = len(QUANT_ROW)
    columns = rows_x * rows_y
    halo = first_in.shape[0] // channels
    odd = is_odd("stream")
    first_x = (1 - odd) * (rows_x - REACH)
    second_x = odd * (rows_x - REACH)
    for c in range(channels):
        own = slice(c * columns, (c + 1) * columns)
        side = slice(c * halo, (c + 1) * halo)
        field_ref[own, :] = part_ref[own, :] + mix(
            operator_ref, columns, sides("span", first_in[side, :], second_in[side, :])
        )
    for c in range(channels):
        for k in range(REACH):
            for y in range(rows_y):
                to = (c * REACH + k) * rows_y + y
                row = c * columns + y * rows_x + k
                first_ref[to:to + 1, :] = field_ref[pl.ds(row + first_x, 1), :]
                second_ref[to:to + 1, :] = field_ref[pl.ds(row + second_x, 1), :]


def span_pass(rows_x, rows_y, part, first, second, operator):
    channels = len(QUANT_ROW)
    depth = part.shape[1]
    halo = jax.ShapeDtypeStruct((channels * REACH * rows_y, depth), jnp.float32)
    return pl.pallas_call(
        functools.partial(span_kernel, rows_x, rows_y),
        out_shape=(jax.ShapeDtypeStruct((channels * rows_x * rows_y, depth), jnp.float32), halo, halo),
        in_specs=[VMEM] * 4,
        out_specs=(VMEM,) * 3,
        compiler_params=params(12),
        cost_estimate=cost(1),
        name="span_pass",
    )(part, second, first, operator)


def stream_kernel(
    rows_q, part_ref, second_in, first_in, operator_ref, choose_ref, fluid_ref, solid_hbm, out_ref, solid_ref, sems
):
    channels = len(QUANT_ROW)
    columns = part_ref.shape[0] // channels
    halo = first_in.shape[0] // channels
    choose = choose_ref[...]
    copies = []
    for c in range(channels):
        own = slice(c * columns, (c + 1) * columns)
        side = slice(c * halo, (c + 1) * halo)
        solid_ref[own, :] = part_ref[own, :] + mix(
            operator_ref, columns, sides("stream", first_in[side, :], second_in[side, :])
        )
        copies.append(pltpu.make_async_copy(solid_ref.at[own, :], solid_hbm.at[own, :], sems.at[c]))
        copies[c].start()
    base = solid_ref[0:columns, :]
    for c in range(channels):
        if c == 0:
            value = 1.0 / (1.0 + base)
        else:
            flow = fluid_ref[(c - 1) * columns:c * columns, :]
            value = flow + drag_rate * (solid_ref[c * columns:(c + 1) * columns, :] - base * flow)
        first, rest = halves(value)
        second, third = halves(value - first.astype(jnp.float32))
        sent = dot(choose, first) + (dot(choose, second) + dot(choose, third))
        place = (c - 1) % channels
        out_ref[:, :, place, :] = sent.reshape(sent.shape[0] // rows_q, rows_q, -1)
    for copy in copies:
        copy.wait()


def stream_pass(peers, rows_q, part, first, second, operator, choose, fluid):
    channels = len(QUANT_ROW)
    depth = part.shape[1]
    return pl.pallas_call(
        functools.partial(stream_kernel, rows_q),
        out_shape=(
            jax.ShapeDtypeStruct(part.shape, jnp.float32),
            jax.ShapeDtypeStruct((peers, rows_q, channels, depth), jnp.float32),
        ),
        in_specs=[VMEM] * 6,
        out_specs=(HBM, VMEM),
        scratch_shapes=[pltpu.VMEM(part.shape, jnp.float32), pltpu.SemaphoreType.DMA((channels,))],
        compiler_params=params(16),
        cost_estimate=cost(2),
        name="stream_pass",
    )(part, second, first, operator, choose, fluid)


def swap_first(value, axis):
    count = lax.axis_size(axis)
    assert count % 2 == 0
    return lax.ppermute(value, axis, [(source, source ^ 1) for source in range(count)])


def swap_second(value, axis, periodic):
    count = lax.axis_size(axis)
    pairs = [(source, (source + 1 if source % 2 else source - 1) % count) for source in range(count)]
    if not periodic:
        pairs = [pair for pair in pairs if abs(pair[0] - pair[1]) == 1]
    return lax.ppermute(value, axis, pairs)


def swap(first, second, axis, periodic):
    return swap_first(first, axis), swap_second(second, axis, periodic)


def per_device(grains, send_slots, send_counts, cell_index, fluid, block_slots, block_counts):
    rows_x, rows_y, depth = fluid.shape[1:]
    columns = rows_x * rows_y
    width = send_slots.shape[2]
    peers, rows_q = block_slots.shape[1:]
    total = cell_index.shape[0]
    axes = ("stream", "span")

    first, second, depth_op, stream_op, span_op, choose, marks, cells = leave(
        grains, send_slots[0], send_counts, cell_index.reshape(1, -1), block_slots[0].T, block_counts,
        rows_x, rows_y, depth,
    )
    first = swap_first(first, "stream")
    after, quant = keep(grains, marks, cells, rows_x, rows_y, depth)
    second, quant = lax.optimization_barrier((second, quant))
    second = swap_second(second, "stream", True)

    chunk = math.gcd(math.gcd(grains.shape[1], 2 * width), 4096)
    steps = total // chunk
    kept = grains.shape[1] // chunk
    faces = 2 * REACH * rows_x
    (partial,) = deposit(0, faces, depth, chunk, (0, kept), False, quant)
    grains_after, quant = join(after, quant, first, second, partial)
    edge, first, second = deposit(0, faces, depth, chunk, (kept, steps), True, quant, partial, depth_op)
    first, second = swap(first, second, "span", False)
    (inner,) = deposit(faces, columns - faces, depth, chunk, (0, steps), False, quant, None, depth_op)
    part = own_part(span_op, edge, inner)
    field, *halos = span_pass(rows_x, rows_y, part, first, second, span_op)
    halos = swap(*halos, "stream", True)
    part = own_part(stream_op, field)
    solid, outgoing = stream_pass(
        peers, rows_q, part, *halos, stream_op, choose, fluid.reshape(3 * columns, depth)
    )
    arrived = lax.all_to_all(outgoing, axes, split_axis=0, concat_axis=0, tiled=True)
    return grains_after, solid.reshape(4, rows_x, rows_y, depth), arrived[None]


def solution(mesh):
    return jax.shard_map(
        per_device,
        mesh=mesh,
        in_specs=(
            P(None, ("stream", "span")),
            P(("stream", "span"), None, None),
            P(("stream", "span"), None),
            P(("stream", "span")),
            P(None, "stream", "span", None),
            P(("stream", "span"), None, None),
            P(("stream", "span"), None),
        ),
        out_specs=(
            P(None, ("stream", "span")),
            P(None, "stream", "span", None),
            P(("stream", "span"), None, None, None, None),
        ),
        check_vma=False,
    )
```
